128 devices in a mesh: img: 32 (over x, z, core), row: 4 (over y).
Axes of the slice: x: 4, y: 4, z: 4, core: 2. Of those that a mesh axis runs over, the one named last changes fastest.
Arguments:
- patches: bfloat16 [256, 256, 768], P('img', 'row'), may hold values from -6 to 6
- cls_tokens: bfloat16 [256, 768], P('img'), may hold values from -6 to 6
- mask_index: int32 [256, 154], P('img'), may hold values from 0 to 255, as said below
- mask_token: bfloat16 [768], P(('img', 'row')), may hold values from -5 to 5
- attention_gain: bfloat16 [768], P(('img', 'row')), may hold values from 0.5 to 1.5
- attention_shift: bfloat16 [768], P(('img', 'row')), may hold values from -3 to 3
- input_weight: bfloat16 [768, 2304], P(('img', 'row')), may hold values from -0.21875 to 0.21875
- query_bias: bfloat16 [768], P(('img', 'row')), may hold values from -3 to 3
- value_bias: bfloat16 [768], P(('img', 'row')), may hold values from -3 to 3
- output_weight: bfloat16 [768, 768], P(('img', 'row')), may hold values from -0.875 to 0.875
- output_bias: bfloat16 [768], P(('img', 'row')), may hold values from -3 to 3
- attention_scale: bfloat16 [768], P(('img', 'row')), may hold values from 0.5 to 1.5
- hidden_gain: bfloat16 [768], P(('img', 'row')), may hold values from 0.5 to 1.5
- hidden_shift: bfloat16 [768], P(('img', 'row')), may hold values from -3 to 3
- expand_weight: bfloat16 [768, 3072], P(('img', 'row')), may hold values from -0.21875 to 0.21875
- expand_bias: bfloat16 [3072], P(('img', 'row')), may hold values from -3 to 3
- reduce_weight: bfloat16 [3072, 768], P(('img', 'row')), may hold values from -0.109375 to 0.109375
- reduce_bias: bfloat16 [768], P(('img', 'row')), may hold values from -3 to 3
- hidden_scale: bfloat16 [768], P(('img', 'row')), may hold values from 0.5 to 1.5
- cotangent_patches: bfloat16 [256, 256, 768], P('img', 'row'), may hold values from -6 to 6
- cotangent_cls: bfloat16 [256, 768], P('img'), may hold values from -6 to 6
Outputs:
- output_patches: bfloat16 [256, 256, 768], P('img', 'row')
- output_cls: bfloat16 [256, 768], P('img')
- grad_patches: bfloat16 [256, 256, 768], P('img', 'row')
- grad_cls: bfloat16 [256, 768], P('img')
- grad_mask_token: float32 [768], P(('img', 'row'))
- grad_attention_gain: float32 [768], P(('img', 'row'))
- grad_attention_shift: float32 [768], P(('img', 'row'))
- grad_input_weight: float32 [768, 2304], P(('img', 'row'))
- grad_query_bias: float32 [768], P(('img', 'row'))
- grad_value_bias: float32 [768], P(('img', 'row'))
- grad_output_weight: float32 [768, 768], P(('img', 'row'))
- grad_output_bias: float32 [768], P(('img', 'row'))
- grad_attention_scale: float32 [768], P(('img', 'row'))
- grad_hidden_gain: float32 [768], P(('img', 'row'))
- grad_hidden_shift: float32 [768], P(('img', 'row'))
- grad_expand_weight: float32 [768, 3072], P(('img', 'row'))
- grad_expand_bias: float32 [3072], P(('img', 'row'))
- grad_reduce_weight: float32 [3072, 768], P(('img', 'row'))
- grad_reduce_bias: float32 [768], P(('img', 'row'))
- grad_hidden_scale: float32 [768], P(('img', 'row'))
The draws below stay inside these ranges and needn't reach their ends.
Inputs may be any that keep to these rules, and one draw needn't show every extreme that they name: `mask_index`: the 154 numbers of an image are distinct patch numbers.
All inputs are finite; a program needn't handle non-finite values.
Results may differ from the reference program's by a relative error of at most 0.019.
Values may be sent and summed in bfloat16 or wider, within the bound.
A program may use at most 192 MiB of HBM per device.

```python
import math
import jax
import jax.numpy as jnp
from jax import lax

D = 768
H = 12
E = 64
FF = 3072
GRID = 16
MASKED = 154
IMAGES = 256


def draw_mask_index(key, part):
    key = jax.random.fold_in(key, 11)
    image_keys = jax.random.split(key, IMAGES)

    def one_image(image_key):
        return jax.random.permutation(image_key, GRID * GRID)[:MASKED]
    return jax.vmap(one_image)(image_keys).astype(jnp.int32)


def shard_levels(own_key, shape, cuts, least, largest):
    def one(position, blocks):
        draws = jax.random.uniform(jax.random.fold_in(jax.random.fold_in(own_key, 6), position), (blocks,), jnp.float32, least / len(cuts), largest / len(cuts))
        return jnp.repeat(jnp.exp(draws), shape[position] // blocks).reshape((-1,) + (1,) * (len(shape) - position - 1))

    factor_of = one(*cuts[0])
    for cut in cuts[1:]:
        factor_of = factor_of * one(*cut)
    return factor_of


def bell_draw(rng, shape, deviation, most, cuts=(), kind=jnp.bfloat16):
    drawn = deviation * jax.random.normal(rng, shape, jnp.float32)
    if cuts:
        drawn = drawn * shard_levels(rng, shape, cuts, -0.22, 0.18)
    return jnp.clip(drawn, -most, most).astype(kind)


def setup_inputs(seed: int = 0) -> dict:
    key_list = jax.random.split(jax.random.key(seed), 22)
    patches = bell_draw(key_list[0], (IMAGES, GRID * GRID, D), 1.0, 6.0, ((0, 32), (1, 4)))
    cls_tokens = bell_draw(key_list[1], (IMAGES, D), 1.0, 6.0, ((0, 32),))
    mask_index = draw_mask_index(jax.random.fold_in(key_list[21], 71), 0)
    mask_token = bell_draw(key_list[3], (D,), 1.0, 5.0, ((0, 128),))
    attention_gain = jnp.clip(0.5 + 1.0 * jax.random.uniform(key_list[4], (D,), jnp.float32) ** shard_levels(key_list[4], (D,), ((0, 128),), -0.2, 0.2), 0.5, 1.5).astype(jnp.bfloat16)
    attention_shift = bell_draw(key_list[5], (D,), 0.5, 3.0, ((0, 128),))
    input_weight = bell_draw(key_list[6], (D, 3 * D), D ** -0.5, 0.21875, ((0, 128),))
    query_bias = bell_draw(key_list[7], (D,), 0.5, 3.0, ((0, 128),))
    value_bias = bell_draw(key_list[8], (D,), 0.5, 3.0, ((0, 128),))
    output_weight = bell_draw(key_list[9], (D, D), (D // 16) ** -0.5, 0.875, ((0, 128),))
    output_bias = bell_draw(key_list[10], (D,), 0.5, 3.0, ((0, 128),))
    attention_scale = jnp.clip(0.5 + 1.0 * jax.random.uniform(key_list[11], (D,), jnp.float32) ** shard_levels(key_list[11], (D,), ((0, 128),), -0.2, 0.2), 0.5, 1.5).astype(jnp.bfloat16)
    hidden_gain = jnp.clip(0.5 + 1.0 * jax.random.uniform(key_list[12], (D,), jnp.float32) ** shard_levels(key_list[12], (D,), ((0, 128),), -0.2, 0.2), 0.5, 1.5).astype(jnp.bfloat16)
    hidden_shift = bell_draw(key_list[13], (D,), 0.5, 3.0, ((0, 128),))
    expand_weight = bell_draw(key_list[14], (D, FF), D ** -0.5, 0.21875, ((0, 128),))
    expand_bias = bell_draw(key_list[15], (FF,), 0.5, 3.0, ((0, 128),))
    reduce_weight = bell_draw(key_list[16], (FF, D), FF ** -0.5, 0.109375, ((0, 128),))
    reduce_bias = bell_draw(key_list[17], (D,), 0.5, 3.0, ((0, 128),))
    hidden_scale = jnp.clip(0.5 + 1.0 * jax.random.uniform(key_list[18], (D,), jnp.float32) ** shard_levels(key_list[18], (D,), ((0, 128),), -0.2, 0.2), 0.5, 1.5).astype(jnp.bfloat16)
    cotangent_patches = bell_draw(key_list[19], (IMAGES, GRID * GRID, D), 1.0, 6.0, ((0, 32), (1, 4)))
    cotangent_cls = bell_draw(key_list[20], (IMAGES, D), 1.0, 6.0, ((0, 32),))
    return {"patches": patches, "cls_tokens": cls_tokens, "mask_index": mask_index, "mask_token": mask_token, "attention_gain": attention_gain, "attention_shift": attention_shift, "input_weight": input_weight, "query_bias": query_bias, "value_bias": value_bias, "output_weight": output_weight, "output_bias": output_bias, "attention_scale": attention_scale, "hidden_gain": hidden_gain, "hidden_shift": hidden_shift, "expand_weight": expand_weight, "expand_bias": expand_bias, "reduce_weight": reduce_weight, "reduce_bias": reduce_bias, "hidden_scale": hidden_scale, "cotangent_patches": cotangent_patches, "cotangent_cls": cotangent_cls}


EPSILON = 1e-06
SCORE_SCALE = 0.125
HIGHEST = lax.Precision.HIGHEST

@jax.custom_vjp
def low(v):
    return lax.optimization_barrier(v.astype(jnp.bfloat16)).astype(jnp.float32)

@jax.custom_vjp
def low_back(v):
    return v

def low_keep(v):
    return (low(v), None)

def low_pass(kept, grad):
    return (grad,)

def back_keep(v):
    return (v, None)

def back_low(kept, grad):
    return (low(grad),)
low.defvjp(low_keep, low_pass)
low_back.defvjp(back_keep, back_low)

def normalize(values, gain, shift):
    average = lax.optimization_barrier(jnp.mean(values, -1, keepdims=True))
    centred = values - average
    variance = lax.optimization_barrier(jnp.mean(centred * centred, -1, keepdims=True))
    return centred * lax.rsqrt(variance + EPSILON) * gain + shift

def project(left, right):
    return jnp.einsum('gld,de->gle', left, right, precision=HIGHEST)

def group_forward(params, cls_rows, patch_rows, masked):
    token_mask, gain_attn, shift_attn, weight_in, bias_query, bias_value, weight_out, bias_out, scale_attn, gain_hidden, shift_hidden, weight_up, bias_up, weight_down, bias_down, scale_hidden = params
    width = cls_rows.shape[-1]
    images = cls_rows.shape[0]
    filled = jnp.where(masked[..., None], token_mask[None, None, :], patch_rows)
    hidden_in = jnp.concatenate([cls_rows[:, None, :], filled], 1)
    seq_rows = hidden_in.shape[1]
    attn_input = low(normalize(hidden_in, gain_attn, shift_attn))
    bias_all = jnp.concatenate([bias_query, jnp.zeros_like(bias_query), bias_value])
    packed = low(low_back(project(attn_input, weight_in) + bias_all))
    queries = packed[..., :width].reshape(images, seq_rows, H, E)
    key_rows = packed[..., width:2 * width].reshape(images, seq_rows, H, E)
    value_rows = packed[..., 2 * width:].reshape(images, seq_rows, H, E)
    scores = low_back(jnp.einsum('gqhe,gkhe->ghqk', queries, key_rows, precision=HIGHEST) * SCORE_SCALE)
    attention = low(jax.nn.softmax(scores, axis=-1))
    mixed = jnp.einsum('ghqk,gkhe->gqhe', attention, value_rows, precision=HIGHEST).reshape(images, seq_rows, width)
    mixed = low(low_back(mixed))
    branch_attn = low_back(project(mixed, weight_out) + bias_out)
    middle = hidden_in + scale_attn * branch_attn
    hidden_input = low(normalize(middle, gain_hidden, shift_hidden))
    pre_act = low_back(project(hidden_input, weight_up) + bias_up)
    activated = low(jax.nn.gelu(pre_act, approximate=False))
    branch_hidden = low_back(project(activated, weight_down) + bias_down)
    return middle + scale_hidden * branch_hidden

def reference(patches, cls_tokens, mask_index, mask_token, attention_gain, attention_shift, input_weight, query_bias, value_bias, output_weight, output_bias, attention_scale, hidden_gain, hidden_shift, expand_weight, expand_bias, reduce_weight, reduce_bias, hidden_scale, cotangent_patches, cotangent_cls):
    params = tuple((member.astype(jnp.float32) for member in (mask_token, attention_gain, attention_shift, input_weight, query_bias, value_bias, output_weight, output_bias, attention_scale, hidden_gain, hidden_shift, expand_weight, expand_bias, reduce_weight, reduce_bias, hidden_scale)))
    patch_count = GRID * GRID
    positions = jnp.arange(patch_count, dtype=jnp.int32)
    masked = jnp.any(positions[None, :, None] == mask_index[:, None, :], axis=-1)
    group_size = math.gcd(IMAGES, 8)
    masked_groups = masked.reshape(-1, group_size, patch_count)

    def whole(weights_all, cls_rows, patch_rows):

        def one_group(block_items):
            return group_forward(weights_all, block_items[0], block_items[1], block_items[2])
        blocks = (cls_rows.reshape(-1, group_size, D), patch_rows.reshape(-1, group_size, patch_count, D), masked_groups)
        return lax.map(jax.checkpoint(one_group), blocks).reshape(IMAGES, patch_count + 1, D)
    result, pullback = jax.vjp(whole, params, cls_tokens.astype(jnp.float32), patches.astype(jnp.float32))
    cotangent = jnp.concatenate([cotangent_cls[:, None, :], cotangent_patches], 1).astype(jnp.float32)
    grad_params, grad_cls, grad_patch_rows = pullback(cotangent)
    grad_token, grad_gain_attn, grad_shift_attn, grad_weight_in, grad_bias_query, grad_bias_value, grad_weight_out, grad_bias_out, grad_scale_attn, grad_gain_hidden, grad_shift_hidden, grad_weight_up, grad_bias_up, grad_weight_down, grad_bias_down, grad_scale_hidden = grad_params
    return (result[:, 1:].astype(jnp.bfloat16), result[:, 0].astype(jnp.bfloat16), grad_patch_rows.astype(jnp.bfloat16), grad_cls.astype(jnp.bfloat16), grad_token, grad_gain_attn, grad_shift_attn, grad_weight_in, grad_bias_query, grad_bias_value, grad_weight_out, grad_bias_out, grad_scale_attn, grad_gain_hidden, grad_shift_hidden, grad_weight_up, grad_bias_up, grad_weight_down, grad_bias_down, grad_scale_hidden)
```

```python
import functools

import jax
import jax.numpy as jnp
from jax import lax
from jax.experimental import pallas as pl
from jax.experimental.pallas import tpu as pltpu
from jax.sharding import PartitionSpec as P

D = 768
H = 12
E = 64
FF = 3072
EPSILON = 1e-06
SCORE_SCALE = 0.125
MESH = pl.DeviceIdType.MESH
BF = jnp.bfloat16
F32 = jnp.float32

GROUPS = (
    ("in_a", 6, 640, "xz"),
    ("in_b", 6, 640, "zx"),
    ("out", 6, 384, "xz"),
    ("up", 6, 1536, "zx"),
    ("down", 24, 384, "xz"),
)
PACKS = ((0, 1), (2, 3), (4,))


class Place:
    def __init__(self):
        img = lax.axis_index("img")
        self.y = lax.axis_index("row")
        self.x = img // 8
        self.z = (img // 2) % 4
        self.c = img % 2

    def at(self, dx=0, dz=0, dy=0, flip=0):
        x = (self.x + dx) % 4
        z = (self.z + dz) % 4
        y = (self.y + dy) % 4
        c = 1 - self.c if flip else self.c
        return ((x * 4 + z) * 2 + c, y)

    def near(self):
        return [(dy, flip) for flip in (0, 1) for dy in range(4) if (dy, flip) != (0, 0)]

    def partners(self):
        found = [self.at(dy=dy, flip=flip) for dy, flip in self.near()]
        found += [self.at(dx=k) for k in (1, 2, 3)]
        found += [self.at(dz=k) for k in (1, 2, 3)]
        return found


def greet(place):
    barrier = pltpu.get_barrier_semaphore()
    partners = place.partners()
    for device in partners:
        pl.semaphore_signal(barrier, inc=1, device_id=device, device_id_type=MESH)
    pl.semaphore_wait(barrier, len(partners))


def send(src, dst, send_sem, recv_sem, device):
    copy = pltpu.make_async_remote_copy(
        src_ref=src, dst_ref=dst, send_sem=send_sem, recv_sem=recv_sem, device_id=device, device_id_type=MESH
    )
    copy.start()
    return copy


def local(src, dst, sem):
    copy = pltpu.make_async_copy(src, dst, sem)
    copy.start()
    return copy


def gather_kernel(*refs):
    n = len(GROUPS)
    np_ = len(PACKS)
    packs, refs = refs[:np_], refs[np_:]
    (patches, cots), refs = refs[:2], refs[2:]
    whole, refs = refs[:n], refs[n:]
    (x_all, c_all), refs = refs[:2], refs[2:]
    got, refs = refs[:np_], refs[np_:]
    wide, refs = refs[:np_], refs[np_:]
    stage, refs = refs[:n], refs[n:]
    p1_s, p1_r, p2_s, p2_r, p3_s, p3_r, p4_s, p4_r, a_s, a_r, l_pack, l_stage, l_a = refs
    me = Place()
    slot = me.c * 4 + me.y
    greet(me)
    waits = []
    first = []
    for i in range(np_):
        own = local(packs[i].at[me.c], got[i].at[slot], l_pack.at[i])
        row = [own]
        for j, (dy, flip) in enumerate(me.near()):
            half = 1 - me.c if flip else me.c
            row.append(send(packs[i].at[half], got[i].at[slot], p1_s.at[i, j], p1_r.at[i, j], me.at(dy=dy, flip=flip)))
        first.append(row)
    shuffle = []
    for t, (src, dst) in enumerate(((patches, x_all), (cots, c_all))):
        lane = dst.at[:, pl.ds(pl.multiple_of(64 * me.y, 64), 64)]
        shuffle.append(local(src.at[pl.ds(2 * me.y, 2)], lane, l_a.at[t]))
        for k in (1, 2, 3):
            peer = (me.y + k) % 4
            shuffle.append(send(src.at[pl.ds(2 * peer, 2)], lane, a_s.at[t, k - 1], a_r.at[t, k - 1], me.at(dy=k)))
    second = {}
    for i in range(np_):
        rho = GROUPS[PACKS[i][0]][1]
        for copy in first[i]:
            copy.wait() if copy is first[i][0] else copy.wait_recv()
        for d in range(8):
            wide[i][d * rho : (d + 1) * rho, :] = got[i][d].astype(F32)
        col = 0
        for g in PACKS[i]:
            width, order = GROUPS[g][2], GROUPS[g][3]
            stage[g][...] = wide[i][:, col : col + width].astype(BF)
            col += width
            place = whole[g].at[me.c, me.x, me.z]
            row = [local(stage[g], place, l_stage.at[g])]
            for k in (1, 2, 3):
                device = me.at(dx=k) if order == "xz" else me.at(dz=k)
                row.append(send(stage[g], place, p2_s.at[g, k - 1], p2_r.at[g, k - 1], device))
            second[g] = row
    third = {}
    for g in range(n):
        for copy in second[g]:
            copy.wait()
        order = GROUPS[g][3]
        part = whole[g].at[me.c, :, me.z] if order == "xz" else whole[g].at[me.c, me.x]
        row = []
        for k in (1, 2, 3):
            device = me.at(dz=k) if order == "xz" else me.at(dx=k)
            row.append(send(part, part, p3_s.at[g, k - 1], p3_r.at[g, k - 1], device))
        third[g] = row
    fourth = {}
    for g in range(n):
        for copy in third[g]:
            copy.wait()
        fourth[g] = send(whole[g].at[me.c], whole[g].at[me.c], p4_s.at[g], p4_r.at[g], me.at(flip=1))
    for i in range(np_):
        for copy in first[i][1:]:
            copy.wait_send()
    for copy in shuffle:
        copy.wait()
    for g in range(n):
        fourth[g].wait()


def gather(packs, patches, cots):
    vmem = pl.BlockSpec(memory_space=pltpu.VMEM)
    anywhere = pl.BlockSpec(memory_space=pl.ANY)
    n = len(GROUPS)
    outs = [jax.ShapeDtypeStruct((2, 4, 4, 8 * rho, width), BF) for _, rho, width, _ in GROUPS]
    outs += [jax.ShapeDtypeStruct((2, 256, D), BF)] * 2
    pack_width = [sum(GROUPS[g][2] for g in pack) for pack in PACKS]
    pack_rho = [GROUPS[pack[0]][1] for pack in PACKS]
    dma = pltpu.SemaphoreType.DMA
    scratch = [pltpu.VMEM((8, r, w), BF) for r, w in zip(pack_rho, pack_width)]
    scratch += [pltpu.VMEM((8 * r, w), F32) for r, w in zip(pack_rho, pack_width)]
    scratch += [pltpu.VMEM((8 * rho, width), BF) for _, rho, width, _ in GROUPS]
    scratch += [dma((len(PACKS), 7))] * 2 + [dma((n, 3))] * 4 + [dma((n,))] * 2 + [dma((2, 3))] * 2
    scratch += [dma((len(PACKS),)), dma((n,)), dma((2,))]
    return pl.pallas_call(
        gather_kernel,
        out_shape=outs,
        in_specs=[vmem] * len(PACKS) + [anywhere] * 2,
        out_specs=[anywhere] * len(outs),
        scratch_shapes=scratch,
        compiler_params=pltpu.CompilerParams(collective_id=0, has_side_effects=True, vmem_limit_bytes=56 * 2**20),
        name="gather",
    )(*packs, patches, cots)


def scatter_kernel(*refs):
    n = len(GROUPS)
    grads, refs = refs[:n], refs[n:]
    (res, gp, cls), refs = refs[:3], refs[3:]
    outs, refs = refs[:n], refs[n:]
    (o_res, o_gp, o_cls), refs = refs[:3], refs[3:]
    held, refs = refs[:n], refs[n:]
    sib, refs = refs[:n], refs[n:]
    in1, refs = refs[:n], refs[n:]
    part, refs = refs[:n], refs[n:]
    in2, refs = refs[:n], refs[n:]
    wide, refs = refs[:n], refs[n:]
    cut, refs = refs[:n], refs[n:]
    in3, refs = refs[:n], refs[n:]
    q0_s, q0_r, q1_s, q1_r, q2_s, q2_r, q3_s, q3_r, a_s, a_r, l_g, l_cut, l_a = refs
    me = Place()
    slot = me.c * 4 + me.y
    greet(me)
    zero = {}
    for g in range(n):
        zero[g] = (
            send(grads[g].at[1 - me.c], sib[g], q0_s.at[g], q0_r.at[g], me.at(flip=1)),
            local(grads[g].at[me.c], held[g], l_g.at[g]),
        )
    shuffle = []
    for t, (src, dst) in enumerate(((res, o_res), (gp, o_gp))):
        lane = dst.at[pl.ds(2 * me.y, 2)]
        shuffle.append(local(src.at[:, pl.ds(pl.multiple_of(64 * me.y, 64), 64)], lane, l_a.at[t]))
        for k in (1, 2, 3):
            peer = (me.y + k) % 4
            part_src = src.at[:, pl.ds(pl.multiple_of(64 * peer, 64), 64)]
            shuffle.append(send(part_src, lane, a_s.at[t, k - 1], a_r.at[t, k - 1], me.at(dy=k)))
    shuffle.append(local(cls, o_cls.at[me.y], l_a.at[2]))
    for k in (1, 2, 3):
        shuffle.append(send(cls, o_cls.at[me.y], a_s.at[2, k - 1], a_r.at[2, k - 1], me.at(dy=k)))

    first = {}
    for g in range(n):
        for copy in zero[g]:
            copy.wait()

        def add(i, carry, g=g):
            a, b = i // 4, i % 4
            held[g][a, b] = (held[g][a, b].astype(F32) + sib[g][a, b].astype(F32)).astype(BF)
            return carry

        lax.fori_loop(0, 16, add, 0)
        row = []
        for k in (1, 2, 3):
            if GROUPS[g][3] == "xz":
                src, device = held[g].at[:, (me.z + k) % 4], me.at(dz=k)
            else:
                src, device = held[g].at[(me.x + k) % 4], me.at(dx=k)
            row.append(send(src, in1[g].at[k - 1], q1_s.at[g, k - 1], q1_r.at[g, k - 1], device))
        first[g] = row
    second = {}
    for g in range(n):
        for copy in first[g]:
            copy.wait()
        xz = GROUPS[g][3] == "xz"

        def add1(i, carry, g=g, xz=xz):
            own = held[g][i, me.z] if xz else held[g][me.x, i]
            total = own.astype(F32) + in1[g][0, i].astype(F32) + in1[g][1, i].astype(F32) + in1[g][2, i].astype(F32)
            part[g][i] = total.astype(BF)
            return carry

        lax.fori_loop(0, 4, add1, 0)
        row = []
        for k in (1, 2, 3):
            if xz:
                src, device = part[g].at[(me.x + k) % 4], me.at(dx=k)
            else:
                src, device = part[g].at[(me.z + k) % 4], me.at(dz=k)
            row.append(send(src, in2[g].at[k - 1], q2_s.at[g, k - 1], q2_r.at[g, k - 1], device))
        second[g] = row
    third = {}
    for g in range(n):
        for copy in second[g]:
            copy.wait()
        rho = GROUPS[g][1]
        own = part[g][me.x if GROUPS[g][3] == "xz" else me.z]
        wide[g][...] = own.astype(F32) + in2[g][0].astype(F32) + in2[g][1].astype(F32) + in2[g][2].astype(F32)
        for d in range(8):
            cut[g][d] = wide[g][d * rho : (d + 1) * rho, :].astype(BF)
        row = [local(cut[g].at[slot], in3[g].at[slot], l_cut.at[g])]
        for j, (dy, flip) in enumerate(me.near()):
            core = 1 - me.c if flip else me.c
            peer = core * 4 + (me.y + dy) % 4
            row.append(send(cut[g].at[peer], in3[g].at[slot], q3_s.at[g, j], q3_r.at[g, j], me.at(dy=dy, flip=flip)))
        third[g] = row
    for g in range(n):
        for copy in third[g]:
            copy.wait()
        for half in range(2):
            total = in3[g][half * 4].astype(F32)
            for y in range(1, 4):
                total = total + in3[g][half * 4 + y].astype(F32)
            outs[g][half] = total
    for copy in shuffle:
        copy.wait()


def scatter(grads, res, gp, cls):
    vmem = pl.BlockSpec(memory_space=pltpu.VMEM)
    anywhere = pl.BlockSpec(memory_space=pl.ANY)
    n = len(GROUPS)
    outs = [jax.ShapeDtypeStruct((2, rho, width), F32) for _, rho, width, _ in GROUPS]
    outs += [jax.ShapeDtypeStruct((8, 64, D), BF)] * 2 + [jax.ShapeDtypeStruct((4, 16, D), BF)]
    dma = pltpu.SemaphoreType.DMA
    scratch = []
    scratch += [pltpu.VMEM((4, 4, 8 * rho, width), BF) for _, rho, width, _ in GROUPS]
    scratch += [pltpu.VMEM((4, 4, 8 * rho, width), BF) for _, rho, width, _ in GROUPS]
    scratch += [pltpu.VMEM((3, 4, 8 * rho, width), BF) for _, rho, width, _ in GROUPS]
    scratch += [pltpu.VMEM((4, 8 * rho, width), BF) for _, rho, width, _ in GROUPS]
    scratch += [pltpu.VMEM((3, 8 * rho, width), BF) for _, rho, width, _ in GROUPS]
    scratch += [pltpu.VMEM((8 * rho, width), F32) for _, rho, width, _ in GROUPS]
    scratch += [pltpu.VMEM((8, rho, width), BF) for _, rho, width, _ in GROUPS]
    scratch += [pltpu.VMEM((8, rho, width), BF) for _, rho, width, _ in GROUPS]
    scratch += [dma((n,))] * 2 + [dma((n, 3))] * 4 + [dma((n, 7))] * 2 + [dma((3, 3))] * 2
    scratch += [dma((n,)), dma((n,)), dma((3,))]
    return pl.pallas_call(
        scatter_kernel,
        out_shape=outs,
        in_specs=[anywhere] * (n + 3),
        out_specs=[vmem] * n + [anywhere] * 3,
        scratch_shapes=scratch,
        compiler_params=pltpu.CompilerParams(collective_id=1, has_side_effects=True, vmem_limit_bytes=56 * 2**20),
        name="scatter",
    )(*grads, res, gp, cls)


def standardize(values):
    average = jnp.mean(values, -1, keepdims=True)
    centred = values - average
    variance = jnp.mean(centred * centred, -1, keepdims=True)
    inverse = lax.rsqrt(variance + EPSILON)
    return (centred * inverse, inverse)


def standardize_back(grad_normed, normed, inverse):
    first_mean = jnp.mean(grad_normed, -1, keepdims=True)
    second_mean = jnp.mean(grad_normed * normed, -1, keepdims=True)
    return inverse * (grad_normed - first_mean - normed * second_mean)


def gelu_exact(values):
    return jax.nn.gelu(values, approximate=False)


def dot(left, right):
    return jnp.einsum("bld,de->ble", left, right, preferred_element_type=F32)


def dot_back(left, right):
    return jnp.einsum("ble,de->bld", left, right, preferred_element_type=F32)


def outer(left, right):
    return jnp.einsum("bld,ble->de", left, right, preferred_element_type=F32)


def col(values):
    return jnp.sum(values, axis=(0, 1))


def layer(whole, x_all, c_all, cls_rows, cot_cls, masked):
    in_a, in_b, out, up, down = whole
    vec = in_b[0, ..., 512:].reshape(D, 128)
    names = vec[:, :11].T.astype(F32)
    (token, gain_a, shift_a, b_q, b_v, b_out, scale_a, gain_h, shift_h, b_down, scale_h) = [names[i] for i in range(11)]
    b_up = vec[:, 11:15].reshape(FF).astype(F32)
    halves = [jnp.concatenate([in_a[h].reshape(D, 640), in_b[h, ..., :512].reshape(D, 512)], -1) for h in range(2)]
    w_in = jnp.concatenate([halves[h][:, 384 * t : 384 * (t + 1)] for t in range(3) for h in range(2)], -1)
    w_out = jnp.concatenate([out[0].reshape(D, 384), out[1].reshape(D, 384)], -1)
    w_up = jnp.concatenate([up[0].reshape(D, 1536), up[1].reshape(D, 1536)], -1)
    w_down = jnp.concatenate([down[0].reshape(FF, 384), down[1].reshape(FF, 384)], -1)
    batch = x_all.shape[0]
    seq = 257

    filled = jnp.where(masked[..., None], token[None, None, :], x_all.astype(F32))
    hidden_in = jnp.concatenate([cls_rows.astype(F32)[:, None, :], filled], 1)
    normed_a, inv_a = standardize(hidden_in)
    attn_input = (normed_a * gain_a + shift_a).astype(BF)
    bias_all = jnp.concatenate([b_q, jnp.zeros_like(b_q), b_v])
    packed = (dot(attn_input, w_in) + bias_all).astype(BF)
    q, k, v = [packed[..., D * t : D * (t + 1)].reshape(batch, seq, H, E) for t in range(3)]
    scores = jnp.einsum("bqhe,bkhe->bhqk", q, k, preferred_element_type=F32) * SCORE_SCALE
    attention = jax.nn.softmax(scores, axis=-1)
    attention_low = attention.astype(BF)
    mixed = jnp.einsum("bhqk,bkhe->bqhe", attention_low, v, preferred_element_type=F32)
    mixed_low = mixed.reshape(batch, seq, D).astype(BF)
    branch_a = dot(mixed_low, w_out) + b_out
    middle = hidden_in + scale_a * branch_a
    normed_h, inv_h = standardize(middle)
    hidden_input = (normed_h * gain_h + shift_h).astype(BF)
    pre = dot(hidden_input, w_up) + b_up
    activated, pullback = jax.vjp(gelu_exact, pre)
    activated_low = activated.astype(BF)
    branch_h = dot(activated_low, w_down) + b_down
    result = (middle + scale_h * branch_h).astype(BF)
    grad_out = jnp.concatenate([cot_cls[:, None, :], c_all], 1).astype(F32)
    g_scale_h = col(grad_out * branch_h)
    g_branch = (scale_h * grad_out).astype(BF)
    g_down = outer(activated_low, g_branch)
    g_b_down = col(g_branch.astype(F32))
    g_act = dot_back(g_branch, w_down)
    (g_pre,) = pullback(g_act)
    g_pre = g_pre.astype(BF)
    g_up = outer(hidden_input, g_pre)
    g_b_up = col(g_pre.astype(F32))
    g_norm_h = dot_back(g_pre, w_up)
    g_gain_h = col(g_norm_h * normed_h)
    g_shift_h = col(g_norm_h)
    g_middle = grad_out + standardize_back(g_norm_h * gain_h, normed_h, inv_h)
    g_scale_a = col(g_middle * branch_a)
    g_attn = (scale_a * g_middle).astype(BF)
    g_out = outer(mixed_low, g_attn)
    g_b_out = col(g_attn.astype(F32))
    g_mixed = dot_back(g_attn, w_out).astype(BF).reshape(batch, seq, H, E)
    g_w = jnp.einsum("bqhe,bkhe->bhqk", g_mixed, v, preferred_element_type=F32)
    g_s = (attention * (g_w - jnp.sum(attention * g_w, -1, keepdims=True))).astype(BF)
    g_q = jnp.einsum("bhqk,bkhe->bqhe", g_s, k, preferred_element_type=F32) * SCORE_SCALE
    g_k = jnp.einsum("bhqk,bqhe->bkhe", g_s, q, preferred_element_type=F32) * SCORE_SCALE
    g_v = jnp.einsum("bhqk,bqhe->bkhe", attention_low, g_mixed, preferred_element_type=F32)
    g_packed = jnp.concatenate([t.reshape(batch, seq, D) for t in (g_q, g_k, g_v)], -1).astype(BF)
    g_in = outer(attn_input, g_packed)
    packed_total = col(g_packed.astype(F32))
    g_norm_a = dot_back(g_packed, w_in)
    g_gain_a = col(g_norm_a * normed_a)
    g_shift_a = col(g_norm_a)
    g_hidden = g_middle + standardize_back(g_norm_a * gain_a, normed_a, inv_a)
    g_patch = g_hidden[:, 1:]
    g_token = col(jnp.where(masked[..., None], g_patch, 0.0))
    g_patch = jnp.where(masked[..., None], 0.0, g_patch).astype(BF)

    vectors = jnp.stack(
        [g_token, g_gain_a, g_shift_a, packed_total[:D], packed_total[2 * D :], g_b_out, g_scale_a, g_gain_h, g_shift_h, g_b_down, g_scale_h], 1
    )
    vectors = jnp.concatenate([vectors, g_b_up.reshape(D, 4), jnp.zeros((D, 113), F32)], 1).astype(BF)
    g_in = g_in.astype(BF)
    g_half = [jnp.concatenate([g_in[:, D * t + 384 * h : D * t + 384 * (h + 1)] for t in range(3)], -1) for h in range(2)]
    grads = (
        jnp.stack([g_half[h][:, :640] for h in range(2)]).reshape(2, 4, 4, 48, 640),
        jnp.stack([jnp.concatenate([g_half[h][:, 640:], vectors if h == 0 else jnp.zeros_like(vectors)], -1) for h in range(2)]).reshape(2, 4, 4, 48, 640),
        jnp.stack([g_out.astype(BF)[:, 384 * h : 384 * (h + 1)] for h in range(2)]).reshape(2, 4, 4, 48, 384),
        jnp.stack([g_up.astype(BF)[:, 1536 * h : 1536 * (h + 1)] for h in range(2)]).reshape(2, 4, 4, 48, 1536),
        jnp.stack([g_down.astype(BF)[:, 384 * h : 384 * (h + 1)] for h in range(2)]).reshape(2, 4, 4, 192, 384),
    )
    cls_out = jnp.concatenate([result[:, 0], g_hidden[:, 0].astype(BF), jnp.zeros((12, D), BF)], 0)
    return grads, result[:, 1:], g_patch, cls_out


def on_device(
    patches,
    cls_tokens,
    mask_index,
    mask_token,
    attention_gain,
    attention_shift,
    input_weight,
    query_bias,
    value_bias,
    output_weight,
    output_bias,
    attention_scale,
    hidden_gain,
    hidden_shift,
    expand_weight,
    expand_bias,
    reduce_weight,
    reduce_bias,
    hidden_scale,
    cotangent_patches,
    cotangent_cls,
):
    y = lax.axis_index("row")
    vectors = jnp.stack(
        [mask_token, attention_gain, attention_shift, query_bias, value_bias, output_bias, attention_scale, hidden_gain, hidden_shift, reduce_bias, hidden_scale],
        1,
    )
    vectors = jnp.concatenate([vectors, expand_bias.reshape(6, 4), jnp.zeros((6, 113), BF)], 1)
    halves = [
        jnp.concatenate([input_weight[:, D * t + 384 * h : D * t + 384 * (h + 1)] for t in range(3)] + [vectors], -1)
        for h in range(2)
    ]
    pack_in = jnp.stack(halves)
    pack_mid = jnp.stack(
        [
            jnp.concatenate([output_weight[:, 384 * h : 384 * (h + 1)], expand_weight[:, 1536 * h : 1536 * (h + 1)]], -1)
            for h in range(2)
        ]
    )
    pack_down = jnp.stack([reduce_weight[:, 384 * h : 384 * (h + 1)] for h in range(2)])
    *whole, x_all, c_all = gather((pack_in, pack_mid, pack_down), patches, cotangent_patches)

    two = functools.partial(lax.dynamic_slice_in_dim, start_index=2 * y, slice_size=2, axis=0)
    masked = jnp.any(jnp.arange(256, dtype=jnp.int32)[None, :, None] == two(mask_index)[:, None, :], axis=-1)
    grads, res, gp, cls = layer(whole, x_all, c_all, two(cls_tokens), two(cotangent_cls), masked)
    o_ina, o_inb, o_out, o_up, o_down, o_res, o_gp, o_cls = scatter(grads, res, gp, cls)
    g_half = [jnp.concatenate([o_ina[h], o_inb[h][:, :512]], -1) for h in range(2)]
    g_in = jnp.concatenate([g_half[h][:, 384 * t : 384 * (t + 1)] for t in range(3) for h in range(2)], -1)
    vec = o_inb[0][:, 512:]
    (g_token, g_gain_a, g_shift_a, g_bq, g_bv, g_b_out, g_scale_a, g_gain_h, g_shift_h, g_b_down, g_scale_h) = [
        vec[:, i] for i in range(11)
    ]
    g_b_up = vec[:, 11:15].reshape(24)
    return (
        o_res,
        o_cls[:, :2].reshape(8, D),
        o_gp,
        o_cls[:, 2:4].reshape(8, D),
        g_token,
        g_gain_a,
        g_shift_a,
        g_in,
        g_bq,
        g_bv,
        jnp.concatenate([o_out[0], o_out[1]], -1),
        g_b_out,
        g_scale_a,
        g_gain_h,
        g_shift_h,
        jnp.concatenate([o_up[0], o_up[1]], -1),
        g_b_up,
        jnp.concatenate([o_down[0], o_down[1]], -1),
        g_b_down,
        g_scale_h,
    )


def solution(mesh):
    vector = P(("img", "row"))
    matrix = P(("img", "row"), None)
    image = P("img", "row", None)
    head = P("img", None)
    in_specs = (image, head, head, vector, vector, vector, matrix, vector, vector, matrix, vector, vector, vector, vector)
    in_specs += (matrix, vector, matrix, vector, vector, image, head)
    out_specs = (image, head, image, head, vector, vector, vector, matrix, vector, vector, matrix, vector, vector)
    out_specs += (vector, vector, matrix, vector, matrix, vector, vector)
    return jax.shard_map(on_device, mesh=mesh, in_specs=in_specs, out_specs=out_specs, check_vma=False)
```

```python
import functools

import jax
import jax.numpy as jnp
from jax import lax
from jax.experimental import pallas as pl
from jax.experimental.pallas import tpu as pltpu
from jax.sharding import PartitionSpec as P

D = 768
H = 12
E = 64
FF = 3072
EPSILON = 1e-06
SCORE_SCALE = 0.125
MESH = pl.DeviceIdType.MESH
BF = jnp.bfloat16
F32 = jnp.float32
ROWS = 528
KEYS = 272
TILE = 16
CHUNK = 512
NCH = FF // CHUNK
MT = 176

TOKEN, GAIN_A, SHIFT_A, B_Q, B_V, B_OUT, SCALE_A, GAIN_H, SHIFT_H, B_DOWN, SCALE_H = range(11)

GROUPS = (
    (6, 512, "xz"),
    (6, 384, "zx"),
    (6, 384, "xz"),
    (6, 384, "zx"),
    (6, 1536, "zx"),
    (24, 384, "xz"),
)
OUT, UP, DOWN = 3, 4, 5
PACKS = ((0, 1, 2), (3, 4), (5,))
BACK = ((6, 384, "xz"),) + GROUPS[1:] + ((6, 128, "zx"),)
VEC = 6


def fdot(a, b):
    return jnp.dot(a, b, preferred_element_type=F32)


def dot_nt(a, b):
    return lax.dot_general(a, b, (((1,), (1,)), ((), ())), preferred_element_type=F32)


def dot_tn(a, b):
    return lax.dot_general(a, b, (((0,), (0,)), ((), ())), preferred_element_type=F32)


def fold(v):
    return v[:8] + v[8:]


def iota(shape, dim):
    return lax.broadcasted_iota(jnp.int32, shape, dim)


def rows_at(i, size=TILE):
    return pl.ds(pl.multiple_of(i * size, size), size)


class Place:
    def __init__(self):
        img = lax.axis_index("img")
        self.y = lax.axis_index("row")
        self.x = img // 8
        self.z = (img // 2) % 4
        self.c = img % 2
        self.slot = self.c * 4 + self.y
        self.lane = 192 * (self.z % 2) + 24 * self.slot

    def at(self, dx=0, dz=0, dy=0, flip=0):
        x = (self.x + dx) % 4
        z = (self.z + dz) % 4
        y = (self.y + dy) % 4
        c = 1 - self.c if flip else self.c
        return ((x * 4 + z) * 2 + c, y)

    def near(self):
        return [(dy, flip) for flip in (0, 1) for dy in range(4) if (dy, flip) != (0, 0)]

    def greet(self):
        barrier = pltpu.get_barrier_semaphore()
        partners = [self.at(dy=dy, flip=flip) for dy, flip in self.near()]
        partners += [self.at(dx=k) for k in (1, 2, 3)]
        partners += [self.at(dz=k) for k in (1, 2, 3)]
        for device in partners:
            pl.semaphore_signal(barrier, inc=1, device_id=device, device_id_type=MESH)
        pl.semaphore_wait(barrier, len(partners))


def send(src, dst, send_sem, recv_sem, device):
    copy = pltpu.make_async_remote_copy(
        src_ref=src, dst_ref=dst, send_sem=send_sem, recv_sem=recv_sem, device_id=device, device_id_type=MESH
    )
    copy.start()
    return copy


def local(src, dst, sem):
    copy = pltpu.make_async_copy(src, dst, sem)
    copy.start()
    return copy


def block(order, ref, first, second):
    return ref.at[first, second] if order == "xz" else ref.at[second, first]


def lane_of_rows(order, ref, second, lo=0, size=4):
    return ref.at[pl.ds(lo, size), second] if order == "xz" else ref.at[second, pl.ds(lo, size)]


class Gather:
    def __init__(self, me, packs, got, wide, stage, whole, sems):
        self.me, self.packs, self.got, self.wide, self.stage, self.whole = me, packs, got, wide, stage, whole
        (self.p1_s, self.p1_r, self.p2_s, self.p2_r, self.p3_s, self.p3_r, self.p5_s, self.p5_r, self.p4_s, self.p4_r, self.l_pack, self.l_stage) = sems
        self.one, self.two, self.three, self.five, self.four = {}, {}, {}, {}, {}

    def first(self, i):
        me = self.me
        row = [local(self.packs[i].at[me.c], self.got[i].at[me.slot], self.l_pack.at[i])]
        for j, (dy, flip) in enumerate(me.near()):
            half = 1 - me.c if flip else me.c
            row.append(
                send(self.packs[i].at[half], self.got[i].at[me.slot], self.p1_s.at[i, j], self.p1_r.at[i, j], me.at(dy=dy, flip=flip))
            )
        self.one[i] = row

    def assemble(self, i):
        rho = GROUPS[PACKS[i][0]][0]
        self.one[i][0].wait()
        for copy in self.one[i][1:]:
            copy.wait()
        for d in range(8):
            self.wide[i][d * rho : (d + 1) * rho, :] = self.got[i][d].astype(F32)
        col = 0
        for g in PACKS[i]:
            width = GROUPS[g][1]
            self.stage[g][...] = self.wide[i][:, col : col + width].astype(BF)
            col += width

    def mine(self, g):
        return self.whole[g].at[self.me.c]

    def second(self, g):
        me, order = self.me, GROUPS[g][2]
        place = self.mine(g).at[me.x, me.z]
        row = [local(self.stage[g], place, self.l_stage.at[g])]
        for k in (1, 2, 3):
            device = me.at(dx=k) if order == "xz" else me.at(dz=k)
            row.append(send(self.stage[g], place, self.p2_s.at[g, k - 1], self.p2_r.at[g, k - 1], device))
        self.two[g] = row

    def on_axis(self, g):
        me, order = self.me, GROUPS[g][2]
        if order == "xz":
            return me.z, lambda k: me.at(dz=k)
        return me.x, lambda k: me.at(dx=k)

    def third(self, g):
        for copy in self.two[g]:
            copy.wait()
        at, device = self.on_axis(g)
        part = lane_of_rows(GROUPS[g][2], self.mine(g), at)
        self.three[g] = [
            send(part, part, self.p3_s.at[g, j], self.p3_r.at[g, j], device(k)) for j, k in enumerate((1, 3))
        ]

    def relay(self, g):
        at, device = self.on_axis(g)
        self.five[g] = []
        for j, k in enumerate((1, 3)):
            self.three[g][j].wait_recv()
            part = lane_of_rows(GROUPS[g][2], self.mine(g), (at + 4 - k) % 4, 2 * j, 2)
            self.five[g].append(send(part, part, self.p5_s.at[g, j], self.p5_r.at[g, j], device(k)))

    def fourth(self, g):
        for copy in self.three[g]:
            copy.wait_send()
        for copy in self.five[g]:
            copy.wait()
        self.four[g] = send(self.mine(g), self.mine(g), self.p4_s.at[g], self.p4_r.at[g], self.me.at(flip=1))

    def done(self, g):
        self.four[g].wait()


def gather_sems():
    dma = pltpu.SemaphoreType.DMA
    n = len(GROUPS)
    return (
        [dma((len(PACKS), 7))] * 2 + [dma((n, 3))] * 2 + [dma((n, 2))] * 4 + [dma((n,))] * 2 + [dma((len(PACKS),)), dma((n,))]
    )


def forward_kernel(
    patches, cots, cls, cot_cls, mask_index, w_in, w_o, w_u, w_d, b_up_in, v0, v1, v2, v3, v4, v5, v6, v7, v8, v9, v10,
    in_o0, in_o1, in_o2, h_out, h_up, h_down, c_all, probs_o, qkv_o, hidden, attn_in, mixed, names, b_up, gcls, masks, pcs,
    in_v0, in_v1, in_v2, x_all, probs, qkv, table, pk0, pk1, pk2, gt0, gt1, gt2, wd0, wd1, wd2, st0, st1, st2, st3, st4, st5,
    *sems,
):
    a_s, a_r, l_a, l_out = sems[-4:]
    me = Place()
    vectors = (v0, v1, v2, v3, v4, v5, v6, v7, v8, v9, v10)
    table[...] = jnp.zeros_like(table)
    for i, v in enumerate(vectors):
        table[i : i + 1, :6] = v[...].astype(F32)
    turned = jnp.transpose(table[...])
    spread = iota((8, 384), 1) - me.lane
    value = jnp.zeros((8, 384), F32)
    b_row = b_up_in[...].astype(F32)
    for t in range(24):
        value = jnp.where(spread == t, b_row[:, t : t + 1], value)
    for h in range(2):
        col = 0
        for t in range(3):
            for part in range(3):
                at = D * part + 384 * h + 128 * t
                pk0[h, :, col : col + 128] = w_in[:, at : at + 128]
                col += 128
            if t == 0:
                if h == 0:
                    pk0[h, :, col : col + 128] = turned[:6].astype(BF)
                else:
                    pick = iota((8, 128), 0)
                    rows = jnp.zeros((8, 128), F32)
                    for i in range(3):
                        rows = jnp.where(pick == i, value[:, 128 * i : 128 * (i + 1)], rows)
                    pk0[h, :, col : col + 128] = rows[:6].astype(BF)
                col += 128
        pk1[h, :, :384] = w_o[:, 384 * h : 384 * (h + 1)]
        pk1[h, :, 384:] = w_u[:, 1536 * h : 1536 * (h + 1)]
        pk2[h] = w_d[:, 384 * h : 384 * (h + 1)]
    me.greet()
    whole = (in_v0, in_v1, in_v2, h_out, h_up, h_down)
    gat = Gather(me, (pk0, pk1, pk2), (gt0, gt1, gt2), (wd0, wd1, wd2), (st0, st1, st2, st3, st4, st5), whole, sems[:-4])
    gat.first(0)
    shuffle = []
    for t, (src, dst) in enumerate(((patches, x_all), (cots, c_all))):
        lane = dst.at[:, pl.ds(pl.multiple_of(64 * me.y, 64), 64)]
        row = [local(src.at[pl.ds(2 * me.y, 2)], lane, l_a.at[t])]
        for k in (1, 2, 3):
            peer = (me.y + k) % 4
            row.append(send(src.at[pl.ds(2 * peer, 2)], lane, a_s.at[t, k - 1], a_r.at[t, k - 1], me.at(dy=k)))
        shuffle.append(row)
        if t == 0:
            gat.first(1)
            gat.first(2)
    gat.assemble(0)
    for g in range(3):
        gat.second(g)
    pick = iota((8, D), 0)
    cls_f, cot_f = cls[...].astype(F32), cot_cls[...].astype(F32)
    place16 = iota((TILE, D), 0)
    cls16, cot16 = jnp.zeros((TILE, D), F32), jnp.zeros((TILE, D), F32)
    for i in range(2):
        this = pick == 2 * me.y + i
        cls16 = jnp.where(place16 == i, jnp.sum(jnp.where(this, cls_f, 0.0), 0, keepdims=True), cls16)
        cot16 = jnp.where(place16 == i, jnp.sum(jnp.where(this, cot_f, 0.0), 0, keepdims=True), cot16)
    gcls[...] = cot16.astype(BF)
    for copy in shuffle[0]:
        copy.wait()
    gat.third(0)
    gat.third(1)
    gat.third(2)
    gat.assemble(1)
    gat.second(OUT)
    gat.relay(0)
    gat.relay(1)
    gat.relay(2)
    gat.assemble(2)
    gat.fourth(0)
    gat.second(DOWN)
    gat.second(UP)
    gat.fourth(1)
    gat.fourth(2)
    gat.done(0)
    names[...] = jnp.transpose(in_v0[0, :, :, :, 384:].reshape(D, 128).astype(F32))[:16]
    for pair in range(8):
        a, b = pair // 2, 2 * (pair % 2)
        rows = in_v0[1, a, pl.ds(b, 2), :, 384:].reshape(96, 128).astype(F32)
        which = iota((96, 128), 0) % 6
        for i in range(3):
            at = 384 * pair + 128 * i
            b_up[:, at : at + 128] = jnp.sum(jnp.where(which == i, rows, 0.0), 0, keepdims=True)

    def row(i):
        return names[i : i + 1, :]

    def norm_rows(r, x):
        avg = jnp.mean(x, -1, keepdims=True)
        cen = x - avg
        nm = cen * lax.rsqrt(jnp.mean(cen * cen, -1, keepdims=True) + EPSILON)
        hidden[r, :] = x
        attn_in[r, :] = (nm * row(GAIN_A) + row(SHIFT_A)).astype(BF)

    def norm_tile(i, carry):
        image, j = i // 16, i % 16
        index = mask_index[pl.ds(2 * me.y + image, 1), :]
        hit = iota((TILE, 154), 0) + TILE * j == index
        masked = jnp.max(jnp.where(hit, 1.0, 0.0), -1, keepdims=True)
        r = rows_at(i)
        masks[r, :] = jnp.broadcast_to(masked, (TILE, 128))
        norm_rows(r, jnp.where(masked > 0.5, row(TOKEN), x_all[image, rows_at(j), :].astype(F32)))
        return carry

    lax.fori_loop(0, 32, norm_tile, 0)
    masks[512:, :] = jnp.zeros((TILE, 128), F32)
    norm_rows(pl.ds(512, TILE), cls16)

    outs = []
    whole_in = (in_v0, in_v1, in_v2)
    mixed[512:, :] = jnp.zeros((TILE, D), BF)
    out_in = (in_o0, in_o1, in_o2)

    def project(t):
        for h in range(2):
            p = 2 * t + h
            w = whole_in[t][h, :, :, :, :384].reshape(D, 384)
            at = 384 * h + 128 * t
            bias_q, bias_v = names[B_Q : B_Q + 1, at : at + 128], names[B_V : B_V + 1, at : at + 128]
            for m in range(3):
                r = pl.ds(MT * m, MT)
                out = fdot(attn_in[r, :], w)
                q = (out[:, :128] + bias_q).astype(BF).astype(F32) * SCORE_SCALE
                qkv[p, r, :128] = q.astype(BF)
                qkv[p, r, 128:256] = out[:, 128:256].astype(BF)
                qkv[p, r, 256:] = (out[:, 256:] + bias_v).astype(BF)

    def attend(p, at, i):
        r = rows_at(i, 256)
        own = iota((TILE, 256), 0) == i
        own1 = iota((TILE, 1), 0) == i
        turned_out, cls_out = [], []
        for hh in range(2):
            lo = 64 * hh
            q, k, v = [qkv[p, r, 128 * s + lo : 128 * s + lo + 64] for s in range(3)]
            qc, kc, vc = [qkv[p, 512:528, 128 * s + lo : 128 * s + lo + 64] for s in range(3)]
            s1 = dot_nt(k, q)
            s2 = jnp.where(own, dot_nt(kc, q), -1e30)
            top = jnp.maximum(jnp.max(s1, 0, keepdims=True), jnp.max(s2, 0, keepdims=True))
            e1, e2 = jnp.exp(s1 - top), jnp.exp(s2 - top)
            scale = 1.0 / (jnp.sum(e1, 0, keepdims=True) + jnp.sum(e2, 0, keepdims=True))
            p1, p2 = (e1 * scale).astype(BF), (e2 * scale).astype(BF)
            u = (p * 2 + i) * 2 + hh
            probs[u, :256, :] = p1
            probs[u, 256:, :] = p2
            turned_out.append(dot_tn(v, p1) + dot_tn(vc, p2))
            sc = dot_nt(qc, k)
            scc = jnp.sum(qc.astype(F32) * kc.astype(F32), -1, keepdims=True)
            topc = jnp.maximum(jnp.max(sc, -1, keepdims=True), scc)
            ec, ecc = jnp.exp(sc - topc), jnp.exp(scc - topc)
            total = jnp.sum(ec, -1, keepdims=True) + ecc
            pc = jnp.where(own, ec / total, 0.0)
            pcc = jnp.where(own1, ecc / total, 0.0)
            pcs[u, :, :256] = pc
            pcs[u, :, 256:] = jnp.broadcast_to(pcc, (TILE, 128))
            cls_out.append(fdot(pc.astype(BF), v) + pcc.astype(BF).astype(F32) * vc.astype(F32))
        mixed[r, at : at + 128] = jnp.transpose(jnp.concatenate(turned_out, 0)).astype(BF)
        kept = mixed[512:, at : at + 128].astype(F32)
        mixed[512:, at : at + 128] = (kept + jnp.concatenate(cls_out, -1)).astype(BF)

    steps = {
        (0, 0): lambda: (gat.third(OUT), gat.done(1)),
        (0, 1): lambda: (gat.third(DOWN), gat.third(UP), gat.relay(OUT)),
        (1, 0): lambda: (gat.fourth(OUT), gat.done(2)),
        (1, 1): lambda: None,
        (2, 0): lambda: (gat.relay(DOWN), gat.relay(UP)),
        (2, 1): lambda: None,
    }
    for t in range(3):
        project(t)
        for h in range(2):
            p = 2 * t + h
            at = 384 * h + 128 * t

            def one(i, carry, p=p, at=at):
                attend(p, at, i)
                return carry

            lax.fori_loop(0, 2, one, 0)
            outs.append(local(probs.at[pl.ds(4 * p, 4)], probs_o.at[pl.ds(4 * p, 4)], l_out.at[p]))
            outs.append(local(qkv.at[p], qkv_o.at[p], l_out.at[6 + p]))
            steps[t, h]()
    gat.fourth(DOWN)
    gat.fourth(UP)
    for t in range(3):
        outs.append(local(whole_in[t], out_in[t], l_out.at[12 + t]))
    for copy in shuffle[1]:
        copy.wait()
    for g in (OUT, DOWN, UP):
        gat.done(g)
    for copy in outs:
        copy.wait()


def forward(patches, cots, cls, cot_cls, mask_index, w_in, w_o, w_u, w_d, b_up, vectors):
    vm = pl.BlockSpec(memory_space=pltpu.VMEM)
    hb = pl.BlockSpec(memory_space=pl.ANY)
    S, V, dma = jax.ShapeDtypeStruct, pltpu.VMEM, pltpu.SemaphoreType.DMA
    outs = [S((2, 4, 4, 8 * rho, width), BF) for rho, width, _ in GROUPS]
    outs += [S((2, 256, D), BF), S((24, KEYS, 256), BF), S((6, ROWS, 384), BF)]
    small = [S((ROWS, D), F32), S((ROWS, D), BF), S((ROWS, D), BF), S((16, D), F32), S((1, FF), F32), S((TILE, D), BF)]
    small += [S((ROWS, 128), F32), S((24, TILE, 384), F32)]
    pack_width = [sum(GROUPS[g][1] for g in pack) for pack in PACKS]
    pack_rho = [GROUPS[pack[0]][0] for pack in PACKS]
    scratch = [V((2, 4, 4, 8 * rho, width), BF) for rho, width, _ in GROUPS[:3]]
    scratch += [V((2, 256, D), BF), V((24, KEYS, 256), BF), V((6, ROWS, 384), BF), V((128, 128), F32)]
    scratch += [V((2, r, w), BF) for r, w in zip(pack_rho, pack_width)]
    scratch += [V((8, r, w), BF) for r, w in zip(pack_rho, pack_width)]
    scratch += [V((8 * r, w), F32) for r, w in zip(pack_rho, pack_width)]
    scratch += [V((8 * rho, width), BF) for rho, width, _ in GROUPS]
    scratch += gather_sems() + [dma((2, 3))] * 2 + [dma((2,)), dma((15,))]
    return pl.pallas_call(
        forward_kernel,
        out_shape=outs + small,
        in_specs=[hb] * 2 + [vm] * 19,
        out_specs=[hb] * len(outs) + [vm] * len(small),
        scratch_shapes=scratch,
        compiler_params=pltpu.CompilerParams(collective_id=0, has_side_effects=True, vmem_limit_bytes=58 * 2**20),
        name="forward",
    )(patches, cots, cls, cot_cls, mask_index, w_in, w_o, w_u, w_d, b_up, *vectors)


def middle_kernel(mixed, hidden, c_all, gcls, names, b_up, w_out_h, w_up_h, w_dn_h,
                  res, g_mid, g_mix, vec_g, bup_g, g_out_h, g_up_h, g_dn_h,
                  w_out, w_up, w_dn, gout, branch, normed, inv, hi, gb, acc, gnorm, act, gpre, gatt,
                  g_out, g_up, g_dn, sums, s_in, s_out):
    loads = []
    def load(i, src, dst):
        c = pltpu.make_async_copy(src, dst, s_in.at[i]); c.start(); return c
    l_out = [load(h, w_out_h.at[h], w_out.at[:, pl.ds(384 * h, 384)]) for h in range(2)]
    l_ch = []
    for n in range(NCH):
        h, m = n // 3, n % 3
        l_ch.append([
            load(2 + 3 * n, w_up_h.at[h, :, pl.ds(CHUNK * m, CHUNK)], w_up.at[n]),
            load(3 + 3 * n, w_dn_h.at[0, pl.ds(CHUNK * n, CHUNK)], w_dn.at[n, :, pl.ds(0, 384)]),
            load(4 + 3 * n, w_dn_h.at[1, pl.ds(CHUNK * n, CHUNK)], w_dn.at[n, :, pl.ds(384, 384)]),
        ])
    sums[...] = jnp.zeros_like(sums)
    gout[:512, :] = c_all[...]
    gout[512:, :] = gcls[...]
    row = lambda i: names[i : i + 1, :]
    for c in l_out: c.wait()
    for m in range(3):
        r = pl.ds(MT * m, MT)
        branch[r, :] = fdot(mixed[r, :], w_out[...]) + row(B_OUT)
    def pre_norm(i, carry):
        r = pl.ds(pl.multiple_of(TILE * i, TILE), TILE)
        m = hidden[r, :] + row(SCALE_A) * branch[r, :]
        avg = jnp.mean(m, -1, keepdims=True)
        cen = m - avg
        iv = lax.rsqrt(jnp.mean(cen * cen, -1, keepdims=True) + EPSILON)
        nm = cen * iv
        normed[r, :] = nm
        inv[r, :] = jnp.broadcast_to(iv, (TILE, 128))
        hi[r, :] = (nm * row(GAIN_H) + row(SHIFT_H)).astype(BF)
        g = (row(SCALE_H) * gout[r, :].astype(F32)).astype(BF)
        gb[r, :] = g
        sums[B_DOWN] += fold(g.astype(F32))
        acc[r, :] = jnp.zeros((TILE, D), F32)
        gnorm[r, :] = jnp.zeros((TILE, D), F32)
        return carry
    lax.fori_loop(0, ROWS // TILE, pre_norm, 0)
    for n in range(NCH):
        for c in l_ch[n]: c.wait()
        b = b_up[:, CHUNK * n : CHUNK * (n + 1)]
        for m in range(3):
            r = pl.ds(MT * m, MT)
            pre = fdot(hi[r, :], w_up[n]) + b
            ga = dot_nt(gb[r, :], w_dn[n])
            cdf = 0.5 * (1.0 + lax.erf(pre * 0.7071067811865476))
            a = (pre * cdf).astype(BF)
            d = cdf + pre * (jnp.exp(-0.5 * pre * pre) * 0.3989422804014327)
            g = (d * ga).astype(BF)
            act[r, :] = a
            gpre[r, :] = g
            acc[r, :] += fdot(a, w_dn[n])
            gnorm[r, :] += dot_nt(g, w_up[n])
        gall = gpre[...]
        bup_g[:, CHUNK * n : CHUNK * (n + 1)] = jnp.sum(gall.astype(F32), 0, keepdims=True)
        g_up[n] = dot_tn(hi[...], gall).astype(BF)
        g_dn[n] = dot_tn(act[...], gb[...]).astype(BF)
        h, m = n // 3, n % 3
        stores = [
            pltpu.make_async_copy(g_up.at[n], g_up_h.at[h, :, pl.ds(CHUNK * m, CHUNK)], s_out.at[2 + 3 * n]),
            pltpu.make_async_copy(g_dn.at[n, :, pl.ds(0, 384)], g_dn_h.at[0, pl.ds(CHUNK * n, CHUNK)], s_out.at[3 + 3 * n]),
            pltpu.make_async_copy(g_dn.at[n, :, pl.ds(384, 384)], g_dn_h.at[1, pl.ds(CHUNK * n, CHUNK)], s_out.at[4 + 3 * n]),
        ]
        for c in stores: c.start()
        loads += stores
    def post_norm(i, carry):
        r = pl.ds(pl.multiple_of(TILE * i, TILE), TILE)
        bh = acc[r, :] + row(B_DOWN)
        go = gout[r, :].astype(F32)
        br = branch[r, :]
        res[r, :] = (hidden[r, :] + row(SCALE_A) * br + row(SCALE_H) * bh).astype(BF)
        sums[SCALE_H] += fold(go * bh)
        gn = gnorm[r, :]
        nm = normed[r, :]
        sums[GAIN_H] += fold(gn * nm)
        sums[SHIFT_H] += fold(gn)
        q = gn * row(GAIN_H)
        iv = inv[r, :1]
        gm = go + iv * (q - jnp.mean(q, -1, keepdims=True) - nm * jnp.mean(q * nm, -1, keepdims=True))
        g_mid[r, :] = gm
        sums[SCALE_A] += fold(gm * br)
        ga = (row(SCALE_A) * gm).astype(BF)
        gatt[r, :] = ga
        sums[B_OUT] += fold(ga.astype(F32))
        return carry
    lax.fori_loop(0, ROWS // TILE, post_norm, 0)
    g_out[...] = dot_tn(mixed[...], gatt[...]).astype(BF)
    for h in range(2):
        c = pltpu.make_async_copy(g_out.at[:, pl.ds(384 * h, 384)], g_out_h.at[h], s_out.at[h]); c.start(); loads.append(c)
    for m in range(3):
        r = pl.ds(MT * m, MT)
        g_mix[r, :] = dot_nt(gatt[r, :], w_out[...]).astype(BF)
    for i in range(16):
        vec_g[i : i + 1, :] = jnp.sum(sums[i], 0, keepdims=True)
    for c in loads: c.wait()

def middle(mixed, hidden, c_all, gcls, names, b_up, w_out, w_up, w_dn):
    vm = pl.BlockSpec(memory_space=pltpu.VMEM)
    hb = pl.BlockSpec(memory_space=pl.ANY)
    S = jax.ShapeDtypeStruct
    V = pltpu.VMEM
    return pl.pallas_call(
        middle_kernel,
        out_shape=[S((ROWS, D), BF), S((ROWS, D), F32), S((ROWS, D), BF), S((16, D), F32), S((1, FF), F32),
                   S((2, D, 384), BF), S((2, D, 1536), BF), S((2, FF, 384), BF)],
        in_specs=[vm] * 6 + [hb] * 3,
        out_specs=[vm] * 5 + [hb] * 3,
        scratch_shapes=[V((D, D), BF), V((NCH, D, CHUNK), BF), V((NCH, CHUNK, D), BF), V((ROWS, D), BF), V((ROWS, D), F32), V((ROWS, D), F32),
                        V((ROWS, 128), F32), V((ROWS, D), BF), V((ROWS, D), BF), V((ROWS, D), F32), V((ROWS, D), F32),
                        V((ROWS, CHUNK), BF), V((ROWS, CHUNK), BF), V((ROWS, D), BF),
                        V((D, D), BF), V((NCH, D, CHUNK), BF), V((NCH, CHUNK, D), BF), V((16, 8, D), F32),
                        pltpu.SemaphoreType.DMA((2 + 3 * NCH,)), pltpu.SemaphoreType.DMA((2 + 3 * NCH,))],
        compiler_params=pltpu.CompilerParams(vmem_limit_bytes=60 * 2**20),
        name="middle",
    )(mixed, hidden, c_all, gcls, names, b_up, w_out, w_up, w_dn)


class Scatter:
    def __init__(self, me, own, src, held, sib, ra, rb, part, in2, wide, cut, in3, sems):
        self.me, self.own, self.src, self.held, self.sib, self.ra, self.rb = me, own, src, held, sib, ra, rb
        self.part, self.in2, self.wide, self.cut, self.in3 = part, in2, wide, cut, in3
        (self.q0_s, self.q0_r, self.qa_s, self.qa_r, self.qb_s, self.qb_r, self.q2_s, self.q2_r, self.q3_s, self.q3_r, self.l_g, self.l_cut) = sems
        self.zero, self.a, self.b, self.two, self.three = {}, {}, {}, {}, {}

    def on_axis(self, g):
        me = self.me
        if BACK[g][2] == "xz":
            return me.z, lambda k: me.at(dz=k)
        return me.x, lambda k: me.at(dx=k)

    def piece(self, g, first, second):
        return (first, second) if BACK[g][2] == "xz" else (second, first)

    def start(self, g):
        me = self.me
        row = [send(self.src[g].at[1 - me.c], self.sib[g], self.q0_s.at[g], self.q0_r.at[g], me.at(flip=1))]
        if self.own[g] is None:
            row.append(local(self.src[g].at[me.c], self.held[g], self.l_g.at[g]))
        self.zero[g] = row

    def pair(self, g):
        for copy in self.zero[g]:
            copy.wait()
        me = self.me

        def add(i, carry):
            a, b = i // 4, i % 4
            mine = self.held[g][a, b] if self.own[g] is None else self.own[g][me.c, a, b]
            self.held[g][a, b] = (mine.astype(F32) + self.sib[g][a, b].astype(F32)).astype(BF)
            return carry

        lax.fori_loop(0, 16, add, 0)
        at, device = self.on_axis(g)
        far = (at + 2) % 4
        self.a[g] = [
            send(
                lane_of_rows(BACK[g][2], self.held[g], far, 2 * j, 2), self.ra[g].at[j], self.qa_s.at[g, j], self.qa_r.at[g, j], device(k)
            )
            for j, k in enumerate((1, 3))
        ]

    def pass_on(self, g):
        at, device = self.on_axis(g)
        row = []
        for j, k in enumerate((1, 3)):
            self.a[g][j].wait_recv()
            near = (at + k) % 4

            def add(i, carry, j=j, near=near):
                p = self.piece(g, 2 * j + i, near)
                self.held[g][p] = (self.held[g][p].astype(F32) + self.ra[g][j, i].astype(F32)).astype(BF)
                return carry

            lax.fori_loop(0, 2, add, 0)
            row.append(
                send(lane_of_rows(BACK[g][2], self.held[g], near), self.rb[g].at[j], self.qb_s.at[g, j], self.qb_r.at[g, j], device(k))
            )
        self.b[g] = row

    def across(self, g):
        for copy in self.b[g]:
            copy.wait()
        for copy in self.a[g]:
            copy.wait_send()
        me = self.me
        at, _ = self.on_axis(g)

        def add(i, carry):
            total = self.held[g][self.piece(g, i, at)].astype(F32) + self.rb[g][0, i].astype(F32) + self.rb[g][1, i].astype(F32)
            self.part[g][i] = total.astype(BF)
            return carry

        lax.fori_loop(0, 4, add, 0)
        row = []
        for k in (1, 2, 3):
            if BACK[g][2] == "xz":
                src, device = self.part[g].at[(me.x + k) % 4], me.at(dx=k)
            else:
                src, device = self.part[g].at[(me.z + k) % 4], me.at(dz=k)
            row.append(send(src, self.in2[g].at[k - 1], self.q2_s.at[g, k - 1], self.q2_r.at[g, k - 1], device))
        self.two[g] = row

    def deal(self, g):
        me = self.me
        for copy in self.two[g]:
            copy.wait()
        rho = BACK[g][0]
        mine = self.part[g][me.x if BACK[g][2] == "xz" else me.z]
        self.wide[g][...] = mine.astype(F32) + self.in2[g][0].astype(F32) + self.in2[g][1].astype(F32) + self.in2[g][2].astype(F32)
        for d in range(8):
            self.cut[g][d] = self.wide[g][d * rho : (d + 1) * rho, :].astype(BF)
        row = [local(self.cut[g].at[me.slot], self.in3[g].at[me.slot], self.l_cut.at[g])]
        for j, (dy, flip) in enumerate(me.near()):
            core = 1 - me.c if flip else me.c
            peer = core * 4 + (me.y + dy) % 4
            row.append(
                send(self.cut[g].at[peer], self.in3[g].at[me.slot], self.q3_s.at[g, j], self.q3_r.at[g, j], me.at(dy=dy, flip=flip))
            )
        self.three[g] = row

    def finish(self, g):
        for copy in self.three[g]:
            copy.wait()
        totals = []
        for half in range(2):
            total = self.in3[g][half * 4].astype(F32)
            for y in range(1, 4):
                total = total + self.in3[g][half * 4 + y].astype(F32)
            totals.append(total)
        return totals


def scatter_sems():
    dma = pltpu.SemaphoreType.DMA
    n = len(BACK)
    return [dma((n,))] * 2 + [dma((n, 2))] * 4 + [dma((n, 3))] * 2 + [dma((n, 7))] * 2 + [dma((n,))] * 2


def backward_kernel(*refs):
    (g_mix, names, vec_g, bup_g, masks, pcs), refs = refs[:6], refs[6:]
    (in_h0, in_h1, in_h2, go_h, gu_h, gd_h, probs_h, qkv_h, attn_h, hidden_h, mid_h, res), refs = refs[:12], refs[12:]
    (o_in, o_out, o_up, o_down, o_cls, o_gcls), refs = refs[:6], refs[6:]
    o_vec, refs = refs[:11], refs[11:]
    (o_bup, o_res, o_gp), refs = refs[:3], refs[3:]
    (in_v0, in_v1, in_v2, gi0, gi1, gi2, gvec, probs, qkv, attn, hidden, mid, gpk, gnorm, gp, sums, vtab, cls_l, gcls_l), refs = refs[:19], refs[19:]
    n = len(BACK)
    bufs = []
    for _ in range(9):
        bufs.append(refs[:n])
        refs = refs[n:]
    held, sib, ra, rb, part, in2, wide, cut, in3 = bufs
    sems = refs
    l_in, a_s, a_r, l_a = sems[-4:]
    me = Place()
    whole_in = (in_v0, in_v1, in_v2)
    loads = {}
    for i, (name, src, dst) in enumerate(
        (
            ("qkv", qkv_h, qkv),
            ("probs", probs_h, probs),
            ("attn", attn_h, attn),
            ("in0", in_h0, in_v0),
            ("in1", in_h1, in_v1),
            ("in2", in_h2, in_v2),
            ("hidden", hidden_h, hidden),
            ("mid", mid_h, mid),
        )
    ):
        loads[name] = local(src, dst, l_in.at[i])
    me.greet()
    src = (gi0, gi1, gi2, go_h, gu_h, gd_h, gvec)
    own = (gi0, gi1, gi2, None, None, None, gvec)
    sc = Scatter(me, own, src, held, sib, ra, rb, part, in2, wide, cut, in3, sems[:-4])
    sc.start(DOWN)
    sc.start(UP)
    sc.start(OUT)
    shuffle = []

    def home(t, source, dst, heads):
        for image in range(2):
            lane = dst.at[2 * me.y + image]
            row = [local(source.at[pl.ds(pl.multiple_of(256 * image + 64 * me.y, 64), 64)], lane, l_a.at[t, image])]
            for k in (1, 2, 3):
                peer = (me.y + k) % 4
                row.append(
                    send(
                        source.at[pl.ds(pl.multiple_of(256 * image + 64 * peer, 64), 64)],
                        lane,
                        a_s.at[t, image, k - 1],
                        a_r.at[t, image, k - 1],
                        me.at(dy=k),
                    )
                )
            shuffle.extend(row)
        last = source.at[pl.ds(512, TILE)]
        shuffle.append(local(last, heads.at[me.y], l_a.at[t, 2]))
        for k in (1, 2, 3):
            shuffle.append(send(last, heads.at[me.y], a_s.at[t, 2, k - 1], a_r.at[t, 2, k - 1], me.at(dy=k)))

    home(0, res, o_res, cls_l)
    sums[...] = jnp.zeros_like(sums)
    vtab[...] = jnp.zeros_like(vtab)
    vtab[:16, :] = vec_g[...]
    loads["qkv"].wait()
    loads["probs"].wait()

    def attend_back(p, at, i):
        r = rows_at(i, 256)
        own1 = iota((TILE, 1), 0) == i
        dq_t, dk, dv, dqc, dkc, dvc = [], [], [], [], [], []
        for hh in range(2):
            lo = 64 * hh
            u = (p * 2 + i) * 2 + hh
            q, k, v = [qkv[p, r, 128 * s + lo : 128 * s + lo + 64] for s in range(3)]
            qc, kc, vc = [qkv[p, 512:528, 128 * s + lo : 128 * s + lo + 64] for s in range(3)]
            do = g_mix[r, at + lo : at + lo + 64]
            doc = g_mix[512:, at + lo : at + lo + 64]
            p1, p2 = probs[u, :256, :], probs[u, 256:, :]
            f1, f2 = p1.astype(F32), p2.astype(F32)
            d1, d2 = dot_nt(v, do), dot_nt(vc, do)
            delta = jnp.sum(f1 * d1, 0, keepdims=True) + jnp.sum(f2 * d2, 0, keepdims=True)
            s1, s2 = (f1 * (d1 - delta)).astype(BF), (f2 * (d2 - delta)).astype(BF)
            dq_t.append(dot_tn(k, s1) + dot_tn(kc, s2))
            pc, pcc = pcs[u, :, :256], pcs[u, :, 256:257]
            qcf, kcf, vcf, docf = qc.astype(F32), kc.astype(F32), vc.astype(F32), doc.astype(F32)
            dc = dot_nt(doc, v)
            dcc = jnp.sum(docf * vcf, -1, keepdims=True)
            deltac = jnp.sum(pc * dc, -1, keepdims=True) + pcc * dcc
            sc_ = (pc * (dc - deltac)).astype(BF)
            scc = pcc * (dcc - deltac)
            pcb = pc.astype(BF)
            dqc.append((fdot(sc_, k) + scc * kcf) * SCORE_SCALE)
            dk.append(fdot(s1, q) + dot_tn(sc_, qc))
            dkc.append(fdot(s2, q) + scc * qcf)
            dv.append(fdot(p1, do) + dot_tn(pcb, doc))
            dvc.append(fdot(p2, do) + pcc * docf)
        gpk[p, r, :128] = (jnp.transpose(jnp.concatenate(dq_t, 0)) * SCORE_SCALE).astype(BF)
        gpk[p, r, 128:256] = jnp.concatenate(dk, -1).astype(BF)
        gpk[p, r, 256:] = jnp.concatenate(dv, -1).astype(BF)
        for s, value in enumerate((dqc, dkc, dvc)):
            lanes = slice(128 * s, 128 * (s + 1))
            keep = gpk[p, 512:, lanes].astype(F32)
            gpk[p, 512:, lanes] = jnp.where(own1, jnp.concatenate(value, -1), keep).astype(BF)

    gin = (gi0, gi1, gi2)
    steps = {
        (0, 0): lambda: (sc.pair(UP), sc.pair(DOWN)),
        (0, 1): lambda: (sc.start(0), sc.pair(OUT), sc.pass_on(UP), sc.pass_on(DOWN)),
        (1, 0): lambda: (sc.pair(0), sc.pass_on(OUT)),
        (1, 1): lambda: (sc.start(1), sc.pass_on(0), sc.across(OUT)),
        (2, 0): lambda: (sc.pair(1), sc.across(UP), sc.across(DOWN), sc.across(0)),
        (2, 1): lambda: (sc.start(2), sc.pass_on(1), sc.deal(OUT), sc.deal(0), sc.deal(UP), sc.deal(DOWN)),
    }
    for t in range(3):
        for h in range(2):
            p = 2 * t + h
            at = 384 * h + 128 * t
            gpk[p, 512:, :] = jnp.zeros((TILE, 384), BF)

            def one(i, carry, p=p, at=at):
                attend_back(p, at, i)
                return carry

            lax.fori_loop(0, 2, one, 0)
            if p == 0:
                loads["attn"].wait()
                loads["in0"].wait()
            elif h == 0:
                loads["in%d" % t].wait()
            piece = gpk[p]
            grad = dot_tn(attn[...], piece)
            gin[t][h] = grad.astype(BF).reshape(4, 4, 48, 384)
            total = jnp.sum(piece.astype(F32), 0, keepdims=True)
            vtab[B_Q : B_Q + 1, at : at + 128] = total[:, :128]
            vtab[B_V : B_V + 1, at : at + 128] = total[:, 256:]
            w = whole_in[t][h, :, :, :, :384].reshape(D, 384)
            for m in range(3):
                r = pl.ds(MT * m, MT)
                back = dot_nt(gpk[p, r, :], w)
                gnorm[r, :] = back if p == 0 else gnorm[r, :] + back
            steps[t, h]()
    loads["hidden"].wait()
    loads["mid"].wait()

    def norm_tile(i, carry):
        r = rows_at(i)
        x = hidden[r, :]
        avg = jnp.mean(x, -1, keepdims=True)
        cen = x - avg
        iv = lax.rsqrt(jnp.mean(cen * cen, -1, keepdims=True) + EPSILON)
        nm = cen * iv
        gn = gnorm[r, :]
        sums[1] += fold(gn * nm)
        sums[2] += fold(gn)
        q = gn * names[GAIN_A : GAIN_A + 1, :]
        gh = mid[r, :] + iv * (q - jnp.mean(q, -1, keepdims=True) - nm * jnp.mean(q * nm, -1, keepdims=True))
        masked = masks[r, :1] > 0.5
        sums[0] += fold(jnp.where(masked, gh, 0.0))
        gp[r, :] = jnp.where(masked, 0.0, gh).astype(BF)
        return carry

    lax.fori_loop(0, ROWS // TILE, norm_tile, 0)
    for i, name in enumerate((TOKEN, GAIN_A, SHIFT_A)):
        vtab[name : name + 1, :] = jnp.sum(sums[i], 0, keepdims=True)
    gvec[0] = jnp.transpose(vtab[...]).astype(BF).reshape(4, 4, 48, 128)
    which = iota((48, 128), 0) % 6
    for pair in range(8):
        rows = jnp.zeros((48, 128), F32)
        for i in range(3):
            at = 384 * pair + 128 * i
            rows = jnp.where(which == i, bup_g[:, at : at + 128], rows)
        for j in range(2):
            gvec[1, pair // 2, 2 * (pair % 2) + j] = rows.astype(BF)
    sc.start(VEC)
    home(1, gp, o_gp, gcls_l)
    sc.pair(2)
    sc.pair(VEC)
    sc.across(1)
    sc.pass_on(2)
    sc.pass_on(VEC)
    sc.deal(1)
    sc.across(2)
    sc.across(VEC)
    sc.deal(2)
    sc.deal(VEC)
    for g, out in ((OUT, o_out), (UP, o_up), (DOWN, o_down)):
        width = BACK[g][1]
        for half, total in enumerate(sc.finish(g)):
            out[:, width * half : width * (half + 1)] = total
    for t in range(3):
        for half, total in enumerate(sc.finish(t)):
            for s in range(3):
                at = D * s + 384 * half + 128 * t
                o_in[:, at : at + 128] = total[:, 128 * s : 128 * (s + 1)]
    low, high = sc.finish(VEC)
    vtab[:128, :128] = jnp.zeros((128, 128), F32)
    vtab[:6, :128] = low
    turned = jnp.transpose(vtab[:128, :128])
    for i in range(11):
        o_vec[i][...] = turned[i : i + 1, :6]
    flat = jnp.concatenate([high[i : i + 1] for i in range(3)], -1)
    pick = jnp.where(iota((384, 128), 0) == iota((384, 128), 1) + me.lane, 1.0, 0.0)
    line = lax.dot_general(
        jnp.broadcast_to(flat, (8, 384)), pick, (((1,), (0,)), ((), ())), precision=lax.Precision.HIGHEST, preferred_element_type=F32
    )
    o_bup[...] = line[:1, :24]
    for copy in shuffle:
        copy.wait()
    order = iota((8, D), 0)
    for landed, out in ((cls_l, o_cls), (gcls_l, o_gcls)):
        rows = jnp.zeros((8, D), F32)
        for y in range(4):
            two = landed[y].astype(F32)
            for i in range(2):
                rows = jnp.where(order == 2 * y + i, two[i : i + 1], rows)
        out[...] = rows.astype(BF)


def backward(small, large):
    vm = pl.BlockSpec(memory_space=pltpu.VMEM)
    hb = pl.BlockSpec(memory_space=pl.ANY)
    S, V, dma = jax.ShapeDtypeStruct, pltpu.VMEM, pltpu.SemaphoreType.DMA
    outs = [S((6, 3 * D), F32), S((6, D), F32), S((6, FF), F32), S((24, D), F32), S((8, D), BF), S((8, D), BF)]
    outs += [S((1, 6), F32)] * 11 + [S((1, 24), F32)]
    far = [S((8, 64, D), BF)] * 2
    scratch = [V((2, 4, 4, 8 * rho, width), BF) for rho, width, _ in GROUPS[:3]]
    scratch += [V((2, 4, 4, 48, 384), BF)] * 3 + [V((2, 4, 4, 48, 128), BF)]
    scratch += [V((24, KEYS, 256), BF), V((6, ROWS, 384), BF), V((ROWS, D), BF), V((ROWS, D), F32), V((ROWS, D), F32)]
    scratch += [V((6, ROWS, 384), BF), V((ROWS, D), F32), V((ROWS, D), BF), V((3, 8, D), F32), V((128, D), F32)]
    scratch += [V((4, TILE, D), BF)] * 2
    for lead in ((4, 4), (4, 4), (2, 2), (2, 4), (4,), (3,)):
        scratch += [V(lead + (8 * rho, width), BF) for rho, width, _ in BACK]
    scratch += [V((8 * rho, width), F32) for rho, width, _ in BACK]
    scratch += [V((8, rho, width), BF) for rho, width, _ in BACK] * 2
    scratch += scatter_sems() + [dma((8,)), dma((2, 3, 3)), dma((2, 3, 3)), dma((2, 3))]
    return pl.pallas_call(
        backward_kernel,
        out_shape=outs + far,
        in_specs=[vm] * len(small) + [hb] * len(large),
        out_specs=[vm] * len(outs) + [hb] * 2,
        scratch_shapes=scratch,
        compiler_params=pltpu.CompilerParams(collective_id=1, has_side_effects=True, vmem_limit_bytes=62 * 2**20),
        name="backward",
    )(*small, *large)


def on_device(
    patches,
    cls_tokens,
    mask_index,
    mask_token,
    attention_gain,
    attention_shift,
    input_weight,
    query_bias,
    value_bias,
    output_weight,
    output_bias,
    attention_scale,
    hidden_gain,
    hidden_shift,
    expand_weight,
    expand_bias,
    reduce_weight,
    reduce_bias,
    hidden_scale,
    cotangent_patches,
    cotangent_cls,
):
    vectors = [mask_token, attention_gain, attention_shift, query_bias, value_bias, output_bias, attention_scale]
    vectors += [hidden_gain, hidden_shift, reduce_bias, hidden_scale]
    vectors = [v.reshape(1, 6) for v in vectors]
    (in0, in1, in2, w_out, w_up, w_down, c_all, probs, qkv, hidden, attn_in, mixed, names, b_up, gcls, masks, pcs) = forward(
        patches,
        cotangent_patches,
        cls_tokens,
        cotangent_cls,
        mask_index,
        input_weight,
        output_weight,
        expand_weight,
        reduce_weight,
        expand_bias.reshape(1, 24),
        vectors,
    )
    res, g_mid, g_mix, vec_g, bup_g, g_out, g_up, g_down = middle(
        mixed,
        hidden,
        c_all.reshape(512, D),
        gcls,
        names,
        b_up,
        w_out.reshape(2, D, 384),
        w_up.reshape(2, D, 1536),
        w_down.reshape(2, FF, 384),
    )
    *outs, o_res, o_gp = backward(
        (g_mix, names, vec_g, bup_g, masks, pcs),
        (
            in0,
            in1,
            in2,
            g_out.reshape(2, 4, 4, 48, 384),
            g_up.reshape(2, 4, 4, 48, 1536),
            g_down.reshape(2, 4, 4, 192, 384),
            probs,
            qkv,
            attn_in,
            hidden,
            g_mid,
            res,
        ),
    )
    g_in, g_o, g_u, g_d, o_cls, o_gcls = outs[:6]
    v = [t.reshape(6) for t in outs[6:17]]
    return (
        o_res,
        o_cls,
        o_gp,
        o_gcls,
        v[TOKEN],
        v[GAIN_A],
        v[SHIFT_A],
        g_in,
        v[B_Q],
        v[B_V],
        g_o,
        v[B_OUT],
        v[SCALE_A],
        v[GAIN_H],
        v[SHIFT_H],
        g_u,
        outs[17].reshape(24),
        g_d,
        v[B_DOWN],
        v[SCALE_H],
    )


def solution(mesh):
    vector = P(("img", "row"))
    matrix = P(("img", "row"), None)
    image = P("img", "row", None)
    head = P("img", None)
    in_specs = (image, head, head, vector, vector, vector, matrix, vector, vector, matrix, vector, vector, vector, vector)
    in_specs += (matrix, vector, matrix, vector, vector, image, head)
    out_specs = (image, head, image, head, vector, vector, vector, matrix, vector, vector, matrix, vector, vector)
    out_specs += (vector, vector, matrix, vector, matrix, vector, vector)
    return jax.shard_map(on_device, mesh=mesh, in_specs=in_specs, out_specs=out_specs, check_vma=False)
```

```python
import jax
import jax.numpy as jnp
from jax import lax
from jax.experimental import pallas as pl
from jax.experimental.pallas import tpu as pltpu
from jax.sharding import PartitionSpec as P

D = 768
FF = 3072
EPSILON = 1e-06
SCORE_SCALE = 0.125
MESH = pl.DeviceIdType.MESH
BF = jnp.bfloat16
F32 = jnp.float32
ROWS = 528
KEYS = 272
PAD = 16
TILE = 176
MT = 264
CHUNK = 768
POOL = 800

TOKEN, GAIN_A, SHIFT_A, B_Q, B_V, B_OUT, SCALE_A, GAIN_H, SHIFT_H, B_DOWN, SCALE_H = range(11)

IN, OUT, UP, DOWN, VEC = (0, 1, 2), 3, (4, 7), (5, 6), 8
GROUPS = (
    (6, 512, "xz", "wide"),
    (6, 384, "zx", "two"),
    (6, 384, "xz", "two"),
    (6, 384, "zx", "ring"),
    (6, 768, "xz", "ring"),
    (24, 256, "zx", "ring"),
    (24, 128, "xz", "ring"),
    (6, 768, "xz", "ring"),
)
PACKS = ((0,), (1, 2), (3, 4), (5, 6), (7,))
BACK = (
    (6, 384, "xz", "wide"),
    (6, 384, "zx", "wide"),
    (6, 384, "xz", "wide"),
    (6, 384, "zx", "wide"),
    (6, 768, "xz", "ring"),
    (24, 256, "zx", "ring"),
    (24, 128, "xz", "ring"),
    (6, 768, "zx", "ring"),
    (6, 128, "xz", "wide"),
)


def fdot(a, b):
    return jnp.dot(a, b, preferred_element_type=F32)


def dot_nt(a, b):
    return lax.dot_general(a, b, (((1,), (1,)), ((), ())), preferred_element_type=F32)


def dot_tn(a, b):
    return lax.dot_general(a, b, (((0,), (0,)), ((), ())), preferred_element_type=F32)


def outer(a, b):
    column = jnp.transpose(a[512:528].astype(F32))
    row = b[512:528].astype(F32)
    return dot_tn(a[:512], b[:512]) + column[:, 0:1] * row[0:1] + column[:, 1:2] * row[1:2]


def fold(v):
    return jnp.sum(v.reshape(-1, 8, v.shape[-1]), 0)


def iota(shape, dim):
    return lax.broadcasted_iota(jnp.int32, shape, dim)


def rows_at(i, size):
    return pl.ds(pl.multiple_of(i * size, size), size)


def centre(x):
    cen = x - jnp.mean(x, -1, keepdims=True)
    inv = lax.rsqrt(jnp.mean(cen * cen, -1, keepdims=True) + EPSILON)
    return cen * inv, inv


def norm_back(q, nm, inv):
    return inv * (q - jnp.mean(q, -1, keepdims=True) - nm * jnp.mean(q * nm, -1, keepdims=True))


class Place:
    def __init__(self, pool):
        img = lax.axis_index("img")
        self.y = lax.axis_index("row")
        self.x = img // 8
        self.z = (img // 2) % 4
        self.c = img % 2
        self.slot = self.c * 4 + self.y
        self.lane = 192 * (self.z % 2) + 24 * self.slot
        self.pool, self.used = pool, 0

    def sem(self):
        self.used += 1
        assert self.used <= POOL
        return self.pool.at[self.used - 1]

    def at(self, dx=0, dz=0, dy=0, flip=0):
        x = (self.x + dx) % 4
        z = (self.z + dz) % 4
        y = (self.y + dy) % 4
        c = 1 - self.c if flip else self.c
        return ((x * 4 + z) * 2 + c, y)

    def near(self):
        return [(dy, flip) for flip in (0, 1) for dy in range(4) if (dy, flip) != (0, 0)]

    def plane(self):
        return [(dx, dz) for dx in range(4) for dz in range(4) if (dx, dz) != (0, 0)]

    def signal(self):
        barrier = pltpu.get_barrier_semaphore()
        for dy, flip in self.near():
            pl.semaphore_signal(barrier, inc=1, device_id=self.at(dy=dy, flip=flip), device_id_type=MESH)
        for dx, dz in self.plane():
            pl.semaphore_signal(barrier, inc=1, device_id=self.at(dx=dx, dz=dz), device_id_type=MESH)

    def await_all(self):
        pl.semaphore_wait(pltpu.get_barrier_semaphore(), 22)

    def send(self, src, dst, device):
        copy = pltpu.make_async_remote_copy(
            src_ref=src, dst_ref=dst, send_sem=self.sem(), recv_sem=self.sem(), device_id=device, device_id_type=MESH
        )
        copy.start()
        return copy

    def local(self, src, dst):
        copy = pltpu.make_async_copy(src, dst, self.sem())
        copy.start()
        return copy


def lane_of_rows(order, ref, second, lo=0, size=4):
    return ref.at[pl.ds(lo, size), second] if order == "xz" else ref.at[second, pl.ds(lo, size)]


def wait_all(copies):
    for copy in copies:
        copy.wait()


class Gather:
    def __init__(self, me, packs, got, wide, stage, whole):
        self.me, self.packs, self.got, self.wide, self.stage, self.whole = me, packs, got, wide, stage, whole
        self.one, self.two, self.three, self.five, self.four = {}, {}, {}, {}, {}

    def first(self, i):
        me = self.me
        place = self.got[i].at[me.slot]
        row = [me.local(self.packs[i].at[me.c], place)]
        for dy, flip in me.near():
            half = 1 - me.c if flip else me.c
            row.append(me.send(self.packs[i].at[half], place, me.at(dy=dy, flip=flip)))
        self.one[i] = row

    def assemble(self, i):
        rho = GROUPS[PACKS[i][0]][0]
        wait_all(self.one[i])
        for d in range(8):
            self.wide[i][d * rho : (d + 1) * rho, :] = self.got[i][d].astype(F32)
        col = 0
        for g in PACKS[i]:
            width = GROUPS[g][1]
            self.stage[g][...] = self.wide[i][:, col : col + width].astype(BF)
            col += width

    def mine(self, g):
        return self.whole[g].at[self.me.c]

    def second(self, g):
        me, order, mode = self.me, GROUPS[g][2], GROUPS[g][3]
        place = self.mine(g).at[me.x, me.z]
        row = [me.local(self.stage[g], place)]
        if mode == "wide":
            row += [me.send(self.stage[g], place, me.at(dx=dx, dz=dz)) for dx, dz in me.plane()]
        else:
            for k in (1, 3, 2):
                row.append(me.send(self.stage[g], place, me.at(dx=k) if order == "xz" else me.at(dz=k)))
        self.two[g] = row

    def on_axis(self, g):
        me = self.me
        if GROUPS[g][2] == "xz":
            return me.z, lambda k: me.at(dz=k)
        return me.x, lambda k: me.at(dx=k)

    def third(self, g):
        wait_all(self.two[g])
        self.three[g], self.five[g] = [], []
        if GROUPS[g][3] == "wide":
            return
        at, device = self.on_axis(g)
        part = lane_of_rows(GROUPS[g][2], self.mine(g), at)
        ways = (1, 3, 2) if GROUPS[g][3] == "two" else (1, 3)
        self.three[g] = [self.me.send(part, part, device(k)) for k in ways]

    def relay(self, g):
        at, device = self.on_axis(g)
        for j, k in enumerate((1, 3)):
            self.three[g][j].wait_recv()
            part = lane_of_rows(GROUPS[g][2], self.mine(g), (at + 4 - k) % 4, 2 * j, 2)
            self.five[g].append(self.me.send(part, part, device(k)))

    def fourth(self, g):
        for copy in self.three[g]:
            copy.wait_send()
            if GROUPS[g][3] == "two":
                copy.wait_recv()
        wait_all(self.five[g])
        self.four[g] = self.me.send(self.mine(g), self.mine(g), self.me.at(flip=1))

    def done(self, g):
        self.four[g].wait()


class Scatter:
    def __init__(self, me, held, sib, far, land, wide, cut, final):
        self.me, self.held, self.sib, self.far, self.land = me, held, sib, far, land
        self.wide, self.cut, self.final = wide, cut, final
        self.zero, self.open, self.a, self.b, self.two, self.three = {}, {}, {}, {}, {}, {}

    def on_axis(self, g):
        me = self.me
        if BACK[g][2] == "xz":
            return me.z, lambda k: me.at(dz=k)
        return me.x, lambda k: me.at(dx=k)

    def piece(self, g, first, second):
        return (first, second) if BACK[g][2] == "xz" else (second, first)

    def start(self, g, src, dst=None):
        copy = self.me.send(src, self.sib[g] if dst is None else dst, self.me.at(flip=1))
        self.zero.setdefault(g, []).append(copy)
        self.open.setdefault(g, []).append(copy)
        return copy

    def drain(self, g):
        for copy in self.open.pop(g, []):
            copy.wait_send()

    def pair(self, g, waits=True):
        me = self.me
        if waits:
            for copy in self.zero[g]:
                copy.wait_recv()
            held, sib = self.held[g], self.sib[g]

            def add(i, carry):
                a, b = i // 4, i % 4
                held[a, b] = (held[a, b].astype(F32) + sib[a, b].astype(F32)).astype(BF)
                return carry

            lax.fori_loop(0, 16, add, 0)
        if BACK[g][3] == "wide":
            row = []
            for dx, dz in me.plane():
                x, z = (me.x + dx) % 4, (me.z + dz) % 4
                row.append(me.send(self.held[g].at[x, z], self.land[g].at[me.x * 4 + me.z], me.at(dx=dx, dz=dz)))
            self.two[g] = row
            return
        at, device = self.on_axis(g)
        far = (at + 2) % 4
        self.a[g] = [
            me.send(lane_of_rows(BACK[g][2], self.held[g], far, 2 * j, 2), self.far[g].at[j], device(k)) for j, k in enumerate((1, 3))
        ]

    def pass_on(self, g):
        at, device = self.on_axis(g)
        for copy in self.a[g]:
            copy.wait_recv()
        row = []
        for j, k in enumerate((1, 3)):
            near = (at + k) % 4

            def add(i, carry, j=j, near=near):
                p = self.piece(g, 2 * j + i, near)
                self.held[g][p] = (self.held[g][p].astype(F32) + self.far[g][j, i].astype(F32)).astype(BF)
                return carry

            lax.fori_loop(0, 2, add, 0)
            row.append(self.me.send(lane_of_rows(BACK[g][2], self.held[g], near), self.sib[g].at[j], device(k)))
        self.b[g] = row

    def across(self, g):
        wait_all(self.b[g])
        for copy in self.a[g]:
            copy.wait_send()
        me = self.me
        at, _ = self.on_axis(g)
        held, sib = self.held[g], self.sib[g]

        def add(i, carry):
            p = self.piece(g, i, at)
            held[p] = (held[p].astype(F32) + sib[0, i].astype(F32) + sib[1, i].astype(F32)).astype(BF)
            return carry

        lax.fori_loop(0, 4, add, 0)
        row = []
        for k in (1, 3, 2):
            if BACK[g][2] == "xz":
                src, device = held.at[(me.x + k) % 4, me.z], me.at(dx=k)
            else:
                src, device = held.at[me.x, (me.z + k) % 4], me.at(dz=k)
            row.append(me.send(src, self.land[g].at[k - 1], device))
        self.two[g] = row

    def deal(self, g):
        me = self.me
        wait_all(self.two[g])
        rho, width = BACK[g][:2]
        size = 8 * rho
        own = self.held[g][me.x, me.z].astype(F32)
        land = self.land[g]
        if BACK[g][3] == "wide":
            land[me.x * 4 + me.z] = self.held[g][me.x, me.z]
            total = land[0].astype(F32)
            for i in range(1, 16):
                total = total + land[i].astype(F32)
        else:
            total = own + land[0].astype(F32) + land[1].astype(F32) + land[2].astype(F32)
        self.wide[:size, :width] = total
        for d in range(8):
            self.cut[g][d] = self.wide[d * rho : (d + 1) * rho, :width].astype(BF)
        row = [me.local(self.cut[g].at[me.slot], self.final[g].at[me.slot])]
        for dy, flip in me.near():
            core = 1 - me.c if flip else me.c
            peer = core * 4 + (me.y + dy) % 4
            row.append(me.send(self.cut[g].at[peer], self.final[g].at[me.slot], me.at(dy=dy, flip=flip)))
        self.three[g] = row

    def finish(self, g):
        wait_all(self.three[g])
        self.drain(g)
        totals = []
        for half in range(2):
            total = self.final[g][half * 4].astype(F32)
            for y in range(1, 4):
                total = total + self.final[g][half * 4 + y].astype(F32)
            totals.append(total)
        return totals


def take(refs, n):
    return refs[:n], refs[n:]


def layer_kernel(*refs):
    ng, nb, npk = len(GROUPS), len(BACK), len(PACKS)
    (patches, cots, cls, cot_cls, mask_index, w_in, w_o, w_u, w_d, b_up_in), refs = take(refs, 10)
    vectors, refs = take(refs, 11)
    (o_in, o_out, o_up, o_down, o_cls, o_gcls, o_vec, o_res, o_gp), refs = take(refs, 9)
    weights_far, refs = take(refs, ng - 3)
    in_v, refs = take(refs, 3)
    (wo, wu, wd), refs = take(refs, 3)
    (x_all, c_all, hidden, attn, qkv, probs, pcs, mixed, branch, hi, gb, acc, gnorm, act, gpre, masks), refs = take(refs, 16)
    (names, vtab, bupv, bupg, bland, bsum, bfinal, sums, cls_l, gcls_l), refs = take(refs, 10)
    packs, refs = take(refs, npk)
    got, refs = take(refs, npk)
    pack_wide, refs = take(refs, npk)
    stage, refs = take(refs, ng)
    gi, refs = take(refs, 3)
    (g_out, gvec, snd_up, snd_da, snd_db), refs = take(refs, 5)
    held_far, refs = take(refs, 4)
    sib, refs = take(refs, nb - 1)
    far, refs = take(refs, 4)
    land, refs = take(refs, nb)
    cut, refs = take(refs, nb)
    final, refs = take(refs, nb)
    wide, pool = refs
    me = Place(pool)
    me.signal()

    vtab[...] = jnp.zeros_like(vtab)
    for i, v in enumerate(vectors):
        vtab[i : i + 1, :6] = v[...].astype(F32)
    turned = jnp.transpose(vtab[:, :128])
    spread = iota((8, 384), 1) - me.lane
    line = jnp.zeros((8, 384), F32)
    b_row = b_up_in[...].astype(F32)
    for t in range(24):
        line = jnp.where(spread == t, b_row[:, t : t + 1], line)
    rows = jnp.zeros((8, 128), F32)
    for i in range(3):
        rows = jnp.where(iota((8, 128), 0) == i, line[:, 128 * i : 128 * (i + 1)], rows)
    for h in range(2):
        for t in range(3):
            dst, col = (packs[0], 0) if t == 0 else (packs[1], 384 * (t - 1))
            for part in range(3):
                at = D * part + 384 * h + 128 * t
                dst[h, :, col + 128 * part : col + 128 * (part + 1)] = w_in[:, at : at + 128]
        packs[0][h, :, 384:] = (turned[:6] if h == 0 else rows[:6]).astype(BF)
        packs[2][h, :, :384] = w_o[:, 384 * h : 384 * (h + 1)]
        packs[2][h, :, 384:] = w_u[:, 1536 * h : 1536 * h + 768]
        packs[3][h] = w_d[:, 384 * h : 384 * (h + 1)]
        packs[4][h] = w_u[:, 1536 * h + 768 : 1536 * (h + 1)]
    me.await_all()
    whole = tuple(in_v) + tuple(weights_far)
    ga = Gather(me, packs, got, pack_wide, stage, whole)
    ga.first(0)

    def bring(src, dst):
        row = []
        for image in range(2):
            lane = dst.at[pl.ds(pl.multiple_of(256 * image + 64 * me.y, 64), 64)]
            row.append(me.local(src.at[2 * me.y + image], lane))
            for k in (1, 3, 2):
                row.append(me.send(src.at[2 * ((me.y + k) % 4) + image], lane, me.at(dy=k)))
        return row

    bring_x = bring(patches, x_all)
    ga.first(1)
    ga.first(2)
    ga.first(3)
    bring_c = bring(cots, c_all)
    ga.first(4)
    ga.assemble(0)
    ga.second(0)
    ga.assemble(1)
    ga.second(1)
    ga.second(2)
    pick = iota((8, D), 0)
    place16 = iota((PAD, D), 0)
    for src, dst in ((cls, x_all), (cot_cls, c_all)):
        wide8 = src[...].astype(F32)
        two = jnp.zeros((PAD, D), F32)
        for i in range(2):
            this = jnp.sum(jnp.where(pick == 2 * me.y + i, wide8, 0.0), 0, keepdims=True)
            two = jnp.where(place16 == i, this, two)
        dst[512:, :] = two.astype(BF)
    index0 = mask_index[pl.ds(2 * me.y, 1), :]
    index1 = mask_index[pl.ds(2 * me.y + 1, 1), :] + 256

    def mask_tile(i, carry):
        r = rows_at(i, TILE)
        at = iota((TILE, 154), 0) + TILE * i
        hit = jnp.where(at == index0, 1.0, 0.0) + jnp.where(at == index1, 1.0, 0.0)
        masks[r, :] = jnp.broadcast_to(jnp.max(hit, -1, keepdims=True), (TILE, 128))
        return carry

    lax.fori_loop(0, ROWS // TILE, mask_tile, 0)
    ga.assemble(2)
    ga.third(0)
    ga.fourth(0)
    ga.third(1)
    ga.third(2)
    ga.second(OUT)
    ga.second(UP[0])
    ga.assemble(3)
    ga.second(DOWN[0])
    ga.second(DOWN[1])
    wait_all(bring_x)
    ga.done(0)
    names[...] = jnp.transpose(in_v[0][0, :, :, :, 384:].reshape(D, 128).astype(F32))[:16]
    which = iota((96, 128), 0) % 6
    for pair in range(8):
        a, b = pair // 2, 2 * (pair % 2)
        block = in_v[0][1, a, pl.ds(b, 2), :, 384:].reshape(96, 128).astype(F32)
        for i in range(3):
            at = 384 * (pair % 2) + 128 * i
            bupv[pair // 2, :, at : at + 128] = jnp.sum(jnp.where(which == i, block, 0.0), 0, keepdims=True)

    def row(i):
        return names[i : i + 1, :]

    def norm_tile(i, carry):
        r = rows_at(i, TILE)
        x = jnp.where(masks[r, :1] > 0.5, row(TOKEN), x_all[r, :].astype(F32))
        hidden[r, :] = x
        attn[r, :] = (centre(x)[0] * row(GAIN_A) + row(SHIFT_A)).astype(BF)
        return carry

    lax.fori_loop(0, ROWS // TILE, norm_tile, 0)
    mixed[512:, :] = jnp.zeros((PAD, D), BF)

    def project(t):
        for h in range(2):
            p = 2 * t + h
            w = in_v[t][h, :, :, :, :384].reshape(D, 384)
            at = 384 * h + 128 * t
            bias_q, bias_v = names[B_Q : B_Q + 1, at : at + 128], names[B_V : B_V + 1, at : at + 128]
            for m in range(ROWS // MT):
                r = pl.ds(MT * m, MT)
                out = fdot(attn[r, :], w)
                q = (out[:, :128] + bias_q).astype(BF).astype(F32) * SCORE_SCALE
                qkv[p, r, :128] = q.astype(BF)
                qkv[p, r, 128:256] = out[:, 128:256].astype(BF)
                qkv[p, r, 256:] = (out[:, 256:] + bias_v).astype(BF)

    def heads(p, r, lo):
        patch = [qkv[p, r, 128 * s + lo : 128 * s + lo + 64] for s in range(3)]
        return patch + [qkv[p, 512:528, 128 * s + lo : 128 * s + lo + 64] for s in range(3)]

    def attend(p, at, i):
        r = rows_at(i, 256)
        own = iota((PAD, 256), 0) == i
        own1 = iota((PAD, 1), 0) == i
        turned_out, cls_out = [], []
        for hh in range(2):
            q, k, v, qc, kc, vc = heads(p, r, 64 * hh)
            s1 = dot_nt(k, q)
            s2 = jnp.where(own, dot_nt(kc, q), -1e30)
            top = jnp.maximum(jnp.max(s1, 0, keepdims=True), jnp.max(s2, 0, keepdims=True))
            e1, e2 = jnp.exp(s1 - top), jnp.exp(s2 - top)
            scale = 1.0 / (jnp.sum(e1, 0, keepdims=True) + jnp.sum(e2, 0, keepdims=True))
            p1, p2 = (e1 * scale).astype(BF), (e2 * scale).astype(BF)
            u = (p * 2 + i) * 2 + hh
            probs[u, :256, :] = p1
            probs[u, 256:, :] = p2
            turned_out.append(dot_tn(v, p1) + dot_tn(vc, p2))
            sc = dot_nt(qc, k)
            scc = jnp.sum(qc.astype(F32) * kc.astype(F32), -1, keepdims=True)
            topc = jnp.maximum(jnp.max(sc, -1, keepdims=True), scc)
            ec, ecc = jnp.exp(sc - topc), jnp.exp(scc - topc)
            total = jnp.sum(ec, -1, keepdims=True) + ecc
            pc = jnp.where(own, ec / total, 0.0)
            pcc = jnp.where(own1, ecc / total, 0.0)
            pcs[u, :, :256] = pc
            pcs[u, :, 256:] = jnp.broadcast_to(pcc, (PAD, 128))
            cls_out.append(fdot(pc.astype(BF), v) + pcc.astype(BF).astype(F32) * vc.astype(F32))
        mixed[r, at : at + 128] = jnp.transpose(jnp.concatenate(turned_out, 0)).astype(BF)
        kept = mixed[512:, at : at + 128].astype(F32)
        mixed[512:, at : at + 128] = (kept + jnp.concatenate(cls_out, -1)).astype(BF)

    loads = {}

    def load_out():
        ga.done(OUT)
        loads["out"] = [me.local(whole[OUT].at[h], wo.at[:, :, :, pl.ds(384 * h, 384)]) for h in range(2)]

    def load_chunk(i):
        k, s = i // 2, i % 2
        h = me.c if s == 1 else 1 - me.c
        n = 2 * h + k
        row = [me.local(whole[UP[k]].at[h], wu.at[i % 2])]
        for half in range(2):
            row.append(me.local(whole[DOWN[0]].at[half, n], wd.at[i % 2, :, :, pl.ds(384 * half, 256)]))
            row.append(me.local(whole[DOWN[1]].at[half, n], wd.at[i % 2, :, :, pl.ds(384 * half + 256, 128)]))
        loads[i] = row

    steps = {
        (0, 0): lambda: (ga.fourth(1), ga.fourth(2), ga.third(OUT), ga.third(UP[0]), ga.third(DOWN[0]), ga.third(DOWN[1])),
        (0, 1): lambda: (ga.assemble(4), ga.second(UP[1]), ga.done(1), ga.relay(OUT), ga.relay(UP[0])),
        (1, 0): lambda: (ga.relay(DOWN[0]), ga.relay(DOWN[1])),
        (1, 1): lambda: (ga.done(2), ga.third(UP[1]), ga.fourth(OUT)),
        (2, 0): lambda: (ga.fourth(UP[0]), ga.fourth(DOWN[0]), ga.fourth(DOWN[1]), ga.relay(UP[1])),
        (2, 1): lambda: (load_out(), ga.done(UP[0]), ga.done(DOWN[0]), ga.done(DOWN[1]), load_chunk(0), load_chunk(1)),
    }
    for t in range(3):
        project(t)
        for h in range(2):
            p = 2 * t + h
            at = 384 * h + 128 * t

            def one(i, carry, p=p, at=at):
                attend(p, at, i)
                return carry

            lax.fori_loop(0, 2, one, 0)
            steps[t, h]()

    wait_all(bring_c)
    wait_all(loads["out"])
    sums[...] = jnp.zeros_like(sums)
    w_out = wo[...].reshape(D, D)
    for m in range(ROWS // MT):
        r = pl.ds(MT * m, MT)
        branch[r, :] = fdot(mixed[r, :], w_out) + row(B_OUT)
    ga.fourth(UP[1])

    def pre_norm(i, carry):
        r = rows_at(i, TILE)
        nm, _ = centre(hidden[r, :] + row(SCALE_A) * branch[r, :])
        hi[r, :] = (nm * row(GAIN_H) + row(SHIFT_H)).astype(BF)
        g = (row(SCALE_H) * c_all[r, :].astype(F32)).astype(BF)
        gb[r, :] = g
        sums[B_DOWN] += fold(g.astype(F32))
        acc[r, :] = jnp.zeros((TILE, D), F32)
        gnorm[r, :] = jnp.zeros((TILE, D), F32)
        return carry

    lax.fori_loop(0, ROWS // TILE, pre_norm, 0)
    held = [gi[t].at[me.c] for t in range(3)]
    held += [g_out.at[me.c], held_far[0], held_far[1], held_far[2], held_far[3], gvec]
    sibs = list(sib) + [None]
    fars = {UP[0]: far[0], DOWN[0]: far[1], DOWN[1]: far[2], UP[1]: far[3]}
    sc = Scatter(me, held, sibs, fars, land, wide, cut, final)

    def chunk(i):
        k, s = i // 2, i % 2
        n = 2 * (me.c if s == 1 else 1 - me.c) + k
        wait_all(loads[i])
        up, down = wu[i % 2].reshape(D, CHUNK), wd[i % 2].reshape(CHUNK, D)
        bias = bupv[n]
        for m in range(ROWS // MT):
            r = pl.ds(MT * m, MT)
            pre = fdot(hi[r, :], up) + bias
            back = dot_nt(gb[r, :], down)
            cdf = 0.5 * (1.0 + lax.erf(pre * 0.7071067811865476))
            a = (pre * cdf).astype(BF)
            g = ((cdf + pre * (jnp.exp(-0.5 * pre * pre) * 0.3989422804014327)) * back).astype(BF)
            act[r, :] = a
            gpre[r, :] = g
            acc[r, :] += fdot(a, down)
            gnorm[r, :] += dot_nt(g, up)
        g = gpre[...]
        total = jnp.sum(g.astype(F32), 0, keepdims=True)
        bupg[2 * n] = total[:, :384]
        bupg[2 * n + 1] = total[:, 384:]
        grad_up = outer(hi[...], g).astype(BF).reshape(4, 4, 48, CHUNK)
        if s == 0:
            sc.drain(UP[0])
            snd_up[...] = grad_up
            sc.start(UP[k], snd_up)
        else:
            held_far[0 if k == 0 else 3][...] = grad_up
        grad_down = outer(act[...], gb[...])
        first = me.c == 0
        own = jnp.where(first, grad_down[:, :384], grad_down[:, 384:]).astype(BF)
        other = jnp.where(first, grad_down[:, 384:], grad_down[:, :384]).astype(BF)
        held_far[1][n] = own[:, :256].reshape(4, 192, 256)
        held_far[2][n] = own[:, 256:].reshape(4, 192, 128)
        sc.drain(DOWN[0])
        sc.drain(DOWN[1])
        snd_da[...] = other[:, :256].reshape(4, 192, 256)
        snd_db[...] = other[:, 256:].reshape(4, 192, 128)
        sc.start(DOWN[0], snd_da, sib[DOWN[0]].at[n])
        sc.start(DOWN[1], snd_db, sib[DOWN[1]].at[n])

    chunk(0)
    ga.done(UP[1])
    load_chunk(2)
    chunk(1)
    load_chunk(3)
    sc.pair(UP[0])
    chunk(2)
    sc.pass_on(UP[0])
    chunk(3)
    sc.pair(DOWN[0])
    sc.pair(DOWN[1])
    sc.pair(UP[1])
    sc.across(UP[0])
    b_sent = []
    for dx, dz in me.plane():
        x, z = (me.x + dx) % 4, (me.z + dz) % 4
        b_sent.append(me.send(bupg.at[2 * x + z // 2], bland.at[me.x * 4 + me.z], me.at(dx=dx, dz=dz)))
    res = x_all

    def post_norm(i, carry):
        r = rows_at(i, TILE)
        bh = acc[r, :] + row(B_DOWN)
        go = c_all[r, :].astype(F32)
        br = branch[r, :]
        mid = hidden[r, :] + row(SCALE_A) * br
        nm, inv = centre(mid)
        res[r, :] = (mid + row(SCALE_H) * bh).astype(BF)
        sums[SCALE_H] += fold(go * bh)
        gn = gnorm[r, :]
        sums[GAIN_H] += fold(gn * nm)
        sums[SHIFT_H] += fold(gn)
        gm = go + norm_back(gn * row(GAIN_H), nm, inv)
        acc[r, :] = gm
        sums[SCALE_A] += fold(gm * br)
        g = (row(SCALE_A) * gm).astype(BF)
        gb[r, :] = g
        sums[B_OUT] += fold(g.astype(F32))
        return carry

    lax.fori_loop(0, ROWS // TILE, post_norm, 0)
    shuffle = []

    def home(source, dst, last):
        for image in range(2):
            lane = dst.at[2 * me.y + image]
            shuffle.append(me.local(source.at[pl.ds(pl.multiple_of(256 * image + 64 * me.y, 64), 64)], lane))
            for k in (1, 3, 2):
                peer = pl.multiple_of(256 * image + 64 * ((me.y + k) % 4), 64)
                shuffle.append(me.send(source.at[pl.ds(peer, 64)], lane, me.at(dy=k)))
        block = source.at[pl.ds(512, PAD)]
        shuffle.append(me.local(block, last.at[me.y]))
        for k in (1, 3, 2):
            shuffle.append(me.send(block, last.at[me.y], me.at(dy=k)))

    home(res, o_res, cls_l)
    grad = outer(mixed[...], gb[...]).astype(BF)
    for h in range(2):
        g_out[h] = grad[:, 384 * h : 384 * (h + 1)].reshape(4, 4, 48, 384)
    sc.start(OUT, g_out.at[1 - me.c])
    g_mix = mixed
    for m in range(ROWS // MT):
        r = pl.ds(MT * m, MT)
        g_mix[r, :] = dot_nt(gb[r, :], w_out).astype(BF)
    sc.pass_on(DOWN[0])
    sc.pass_on(DOWN[1])
    sc.pass_on(UP[1])
    gpk = act

    def attend_back(p, at, lane, i):
        r = rows_at(i, 256)
        own1 = iota((PAD, 1), 0) == i
        dq_t, dk, dv, dqc, dkc, dvc = [], [], [], [], [], []
        for hh in range(2):
            lo = 64 * hh
            u = (p * 2 + i) * 2 + hh
            q, k, v, qc, kc, vc = heads(p, r, lo)
            do = g_mix[r, at + lo : at + lo + 64]
            doc = g_mix[512:, at + lo : at + lo + 64]
            p1, p2 = probs[u, :256, :], probs[u, 256:, :]
            f1, f2 = p1.astype(F32), p2.astype(F32)
            d1, d2 = dot_nt(v, do), dot_nt(vc, do)
            delta = jnp.sum(f1 * d1, 0, keepdims=True) + jnp.sum(f2 * d2, 0, keepdims=True)
            s1, s2 = (f1 * (d1 - delta)).astype(BF), (f2 * (d2 - delta)).astype(BF)
            dq_t.append(dot_tn(k, s1) + dot_tn(kc, s2))
            pc, pcc = pcs[u, :, :256], pcs[u, :, 256:257]
            qcf, kcf, vcf, docf = qc.astype(F32), kc.astype(F32), vc.astype(F32), doc.astype(F32)
            dc = dot_nt(doc, v)
            dcc = jnp.sum(docf * vcf, -1, keepdims=True)
            deltac = jnp.sum(pc * dc, -1, keepdims=True) + pcc * dcc
            scb = (pc * (dc - deltac)).astype(BF)
            scc = pcc * (dcc - deltac)
            dqc.append((fdot(scb, k) + scc * kcf) * SCORE_SCALE)
            dk.append(fdot(s1, q) + dot_tn(scb, qc))
            dkc.append(fdot(s2, q) + scc * qcf)
            dv.append(fdot(p1, do) + dot_tn(pc.astype(BF), doc))
            dvc.append(fdot(p2, do) + pcc * docf)
        gpk[r, lane : lane + 128] = (jnp.transpose(jnp.concatenate(dq_t, 0)) * SCORE_SCALE).astype(BF)
        gpk[r, lane + 128 : lane + 256] = jnp.concatenate(dk, -1).astype(BF)
        gpk[r, lane + 256 : lane + 384] = jnp.concatenate(dv, -1).astype(BF)
        for s, value in enumerate((dqc, dkc, dvc)):
            lanes = slice(lane + 128 * s, lane + 128 * (s + 1))
            keep = gpk[512:, lanes].astype(F32)
            gpk[512:, lanes] = jnp.where(own1, jnp.concatenate(value, -1), keep).astype(BF)

    b_last = []

    def b_deal():
        wait_all(b_sent)
        bland[me.x * 4 + me.z] = bupg[2 * me.x + me.z // 2]
        total = bland[0]
        for i in range(1, 16):
            total = total + bland[i]
        bsum[...] = total
        b_last.append(me.local(bsum, bfinal.at[me.slot]))
        for dy, flip in me.near():
            b_last.append(me.send(bsum, bfinal.at[me.slot], me.at(dy=dy, flip=flip)))

    back_steps = {
        (0, 0): lambda: (sc.pair(OUT), sc.deal(UP[0])),
        (0, 1): lambda: (sc.start(0, gi[0].at[1 - me.c]), sc.across(DOWN[0]), sc.across(DOWN[1])),
        (1, 0): lambda: (sc.pair(0), sc.across(UP[1]), b_deal()),
        (1, 1): lambda: (sc.start(1, gi[1].at[1 - me.c]), sc.deal(OUT)),
        (2, 0): lambda: (sc.pair(1), sc.deal(DOWN[0]), sc.deal(DOWN[1])),
        (2, 1): lambda: (sc.start(2, gi[2].at[1 - me.c]), sc.deal(0), sc.deal(UP[1])),
    }
    vtab[...] = jnp.zeros_like(vtab)
    for t in range(3):
        for h in range(2):
            p = 2 * t + h
            at = 384 * h + 128 * t
            lane = 384 * h
            gpk[512:, lane : lane + 384] = jnp.zeros((PAD, 384), BF)

            def one(i, carry, p=p, at=at, lane=lane):
                attend_back(p, at, lane, i)
                return carry

            lax.fori_loop(0, 2, one, 0)
            piece = gpk[:, lane : lane + 384]
            gi[t][h] = outer(attn[...], piece).astype(BF).reshape(4, 4, 48, 384)
            total = jnp.sum(piece.astype(F32), 0, keepdims=True)
            vtab[B_Q : B_Q + 1, at : at + 128] = total[:, :128]
            vtab[B_V : B_V + 1, at : at + 128] = total[:, 256:]
            w = in_v[t][h, :, :, :, :384].reshape(D, 384)
            for m in range(ROWS // MT):
                r = pl.ds(MT * m, MT)
                back = dot_nt(gpk[r, lane : lane + 384], w)
                gnorm[r, :] = back if p == 0 else gnorm[r, :] + back
            back_steps[t, h]()

    gp = hi

    def last_norm(i, carry):
        r = rows_at(i, TILE)
        nm, inv = centre(hidden[r, :])
        gn = gnorm[r, :]
        sums[GAIN_A] += fold(gn * nm)
        sums[SHIFT_A] += fold(gn)
        gh = acc[r, :] + norm_back(gn * row(GAIN_A), nm, inv)
        masked = masks[r, :1] > 0.5
        sums[TOKEN] += fold(jnp.where(masked, gh, 0.0))
        gp[r, :] = jnp.where(masked, 0.0, gh).astype(BF)
        return carry

    sc.pair(2)
    lax.fori_loop(0, ROWS // TILE, last_norm, 0)
    for i in (TOKEN, GAIN_A, SHIFT_A, B_OUT, SCALE_A, GAIN_H, SHIFT_H, B_DOWN, SCALE_H):
        vtab[i : i + 1, :] = jnp.sum(sums[i], 0, keepdims=True)
    gvec[...] = jnp.transpose(vtab[...]).astype(BF).reshape(4, 4, 48, 128)
    sc.pair(VEC, waits=False)
    home(gp, o_gp, gcls_l)
    sc.deal(1)
    for k in range(2):
        for half, total in enumerate(sc.finish(UP[k])):
            o_up[:, 1536 * half + 768 * k : 1536 * half + 768 * (k + 1)] = total
    for col, width, g in ((0, 256, DOWN[0]), (256, 128, DOWN[1])):
        for half, total in enumerate(sc.finish(g)):
            o_down[:, 384 * half + col : 384 * half + col + width] = total
    for half, total in enumerate(sc.finish(OUT)):
        o_out[:, 384 * half : 384 * (half + 1)] = total
    wait_all(b_last)
    flat = bfinal[0]
    for i in range(1, 8):
        flat = flat + bfinal[i]
    chosen = jnp.where(iota((384, 128), 0) == iota((384, 128), 1) + me.lane, 1.0, 0.0)
    line = lax.dot_general(
        jnp.broadcast_to(flat, (8, 384)), chosen, (((1,), (0,)), ((), ())), precision=lax.Precision.HIGHEST, preferred_element_type=F32
    )

    def finish_in(t):
        for half, total in enumerate(sc.finish(t)):
            for s in range(3):
                at = D * s + 384 * half + 128 * t
                o_in[:, at : at + 128] = total[:, 128 * s : 128 * (s + 1)]

    finish_in(0)
    sc.deal(2)
    sc.deal(VEC)
    finish_in(1)
    wait_all(shuffle)
    order = iota((8, D), 0)
    for landed, out in ((cls_l, o_cls), (gcls_l, o_gcls)):
        rows = jnp.zeros((8, D), F32)
        for y in range(4):
            two = landed[y].astype(F32)
            for i in range(2):
                rows = jnp.where(order == 2 * y + i, two[i : i + 1], rows)
        out[...] = rows.astype(BF)
    finish_in(2)
    low, high = sc.finish(VEC)
    vtab[:, :128] = jnp.zeros((128, 128), F32)
    vtab[:6, :128] = low + high
    turned = jnp.transpose(vtab[:, :128])
    o_vec[...] = jnp.where(iota((16, 128), 0) == 11, line[:1], turned[:16])


def layer(patches, cots, cls, cot_cls, mask_index, w_in, w_o, w_u, w_d, b_up, vectors):
    vm = pl.BlockSpec(memory_space=pltpu.VMEM)
    hb = pl.BlockSpec(memory_space=pl.ANY)
    S, V = jax.ShapeDtypeStruct, pltpu.VMEM
    outs = [S((6, 3 * D), F32), S((6, D), F32), S((6, FF), F32), S((24, D), F32), S((8, D), BF), S((8, D), BF), S((16, 128), F32)]
    far = [S((8, 64, D), BF)] * 2
    far += [S((2, 4, 4, 8 * rho, width), BF) for rho, width, _, _ in GROUPS[3:]]
    pack_width = [sum(GROUPS[g][1] for g in pack) for pack in PACKS]
    pack_rho = [GROUPS[pack[0]][0] for pack in PACKS]
    scratch = [V((2, 4, 4, 48, width), BF) for _, width, _, _ in GROUPS[:3]]
    scratch += [V((4, 4, 48, D), BF), V((2, 4, 4, 48, CHUNK), BF), V((2, 4, 192, D), BF)]
    wide_rows, low_rows = V((ROWS, D), F32), V((ROWS, D), BF)
    scratch += [low_rows, low_rows, wide_rows, low_rows, V((6, ROWS, 384), BF), V((24, KEYS, 256), BF), V((24, PAD, 384), F32)]
    scratch += [low_rows, wide_rows, low_rows, low_rows, wide_rows, wide_rows, low_rows, low_rows, V((ROWS, 128), F32)]
    scratch += [V((16, D), F32), V((128, D), F32), V((4, 1, CHUNK), F32), V((8, 1, 384), F32), V((16, 1, 384), F32)]
    scratch += [V((1, 384), F32), V((8, 1, 384), F32), V((16, 8, D), F32), V((4, PAD, D), BF), V((4, PAD, D), BF)]
    scratch += [V((2, r, w), BF) for r, w in zip(pack_rho, pack_width)]
    scratch += [V((8, r, w), BF) for r, w in zip(pack_rho, pack_width)]
    scratch += [V((8 * r, w), F32) for r, w in zip(pack_rho, pack_width)]
    scratch += [V((8 * rho, width), BF) for rho, width, _, _ in GROUPS]
    scratch += [V((2, 4, 4, 48, 384), BF)] * 4 + [V((4, 4, 48, 128), BF)]
    scratch += [V((4, 4, 48, CHUNK), BF), V((4, 192, 256), BF), V((4, 192, 128), BF)]
    blocks = [(8 * rho, width) for rho, width, _, _ in BACK]
    scratch += [V((4, 4) + blocks[g], BF) for g in (4, 5, 6, 7)]
    scratch += [V((4, 4) + blocks[g], BF) for g in range(8)]
    scratch += [V((2, 2) + blocks[g], BF) for g in (4, 5, 6, 7)]
    scratch += [V((16 if BACK[g][3] == "wide" else 3,) + blocks[g], BF) for g in range(9)]
    scratch += [V((8, rho, width), BF) for rho, width, _, _ in BACK] * 2
    scratch += [V((192, D), F32), pltpu.SemaphoreType.DMA((POOL,))]
    return pl.pallas_call(
        layer_kernel,
        out_shape=outs + far,
        in_specs=[hb] * 2 + [vm] * 19,
        out_specs=[vm] * len(outs) + [hb] * len(far),
        scratch_shapes=scratch,
        compiler_params=pltpu.CompilerParams(collective_id=0, has_side_effects=True, vmem_limit_bytes=63 * 2**20),
        name="layer",
    )(patches, cots, cls, cot_cls, mask_index, w_in, w_o, w_u, w_d, b_up, *vectors)[:9]


def finish_kernel(i_in, i_out, i_up, i_down, i_cls, i_gcls, i_vec, i_res, i_gp, *outs):
    for src, dst in zip((i_in, i_out, i_up, i_down, i_cls, i_gcls, i_res, i_gp), outs):
        dst[...] = src[...]
    for i in range(11):
        outs[8 + i][...] = i_vec[i : i + 1, :6]
    outs[19][...] = i_vec[11:12, :24]


def finish(parts):
    vm = pl.BlockSpec(memory_space=pltpu.VMEM)
    S = jax.ShapeDtypeStruct
    outs = [S(p.shape, p.dtype) for p in parts[:6]] + [S((8, 64, D), BF)] * 2 + [S((1, 6), F32)] * 11 + [S((1, 24), F32)]
    return pl.pallas_call(
        finish_kernel,
        out_shape=outs,
        in_specs=[vm] * 9,
        out_specs=[vm] * 20,
        name="finish",
    )(*parts)


def on_device(
    patches,
    cls_tokens,
    mask_index,
    mask_token,
    attention_gain,
    attention_shift,
    input_weight,
    query_bias,
    value_bias,
    output_weight,
    output_bias,
    attention_scale,
    hidden_gain,
    hidden_shift,
    expand_weight,
    expand_bias,
    reduce_weight,
    reduce_bias,
    hidden_scale,
    cotangent_patches,
    cotangent_cls,
):
    vectors = [mask_token, attention_gain, attention_shift, query_bias, value_bias, output_bias, attention_scale]
    vectors += [hidden_gain, hidden_shift, reduce_bias, hidden_scale]
    parts = layer(
        patches,
        cotangent_patches,
        cls_tokens,
        cotangent_cls,
        mask_index,
        input_weight,
        output_weight,
        expand_weight,
        reduce_weight,
        expand_bias.reshape(1, 24),
        [v.reshape(1, 6) for v in vectors],
    )
    g_in, g_o, g_u, g_d, o_cls, o_gcls, o_res, o_gp, *v = finish(parts)
    g_bup = v[11].reshape(24)
    v = [t.reshape(6) for t in v[:11]]
    return (
        o_res,
        o_cls,
        o_gp,
        o_gcls,
        v[TOKEN],
        v[GAIN_A],
        v[SHIFT_A],
        g_in,
        v[B_Q],
        v[B_V],
        g_o,
        v[B_OUT],
        v[SCALE_A],
        v[GAIN_H],
        v[SHIFT_H],
        g_u,
        g_bup,
        g_d,
        v[B_DOWN],
        v[SCALE_H],
    )


def solution(mesh):
    vector = P(("img", "row"))
    matrix = P(("img", "row"), None)
    image = P("img", "row", None)
    head = P("img", None)
    in_specs = (image, head, head, vector, vector, vector, matrix, vector, vector, matrix, vector, vector, vector, vector)
    in_specs += (matrix, vector, matrix, vector, vector, image, head)
    out_specs = (image, head, image, head, vector, vector, vector, matrix, vector, vector, matrix, vector, vector)
    out_specs += (vector, vector, matrix, vector, matrix, vector, vector)
    return jax.shard_map(on_device, mesh=mesh, in_specs=in_specs, out_specs=out_specs, check_vma=False)
```

```python
import jax
import jax.numpy as jnp
from jax import lax
from jax.experimental import pallas as pl
from jax.experimental.pallas import tpu as pltpu
from jax.sharding import PartitionSpec as P

D = 768
FF = 3072
EPSILON = 1e-06
SCORE_SCALE = 0.125
MESH = pl.DeviceIdType.MESH
BF = jnp.bfloat16
F32 = jnp.float32
ROWS = 528
KEYS = 272
PAD = 16
TILE = 176
MT = 264
CHUNK = 768
POOL = 300

TOKEN, GAIN_A, SHIFT_A, B_Q, B_V, B_OUT, SCALE_A, GAIN_H, SHIFT_H, B_DOWN, SCALE_H = range(11)

OUT, UP, DOWN = 3, 4, (5, 6)
GROUPS = (
    (6, 512, "xz", "two"),
    (6, 384, "zx", "two"),
    (6, 384, "zx", "two"),
    (6, 384, "xz", "ring"),
    (6, 384, "xz", "quarter"),
    (24, 256, "zx", "ring"),
    (24, 128, "xz", "ring"),
)
PACKS = ((0,), (1, 2), (4,), (5, 6), (3,))
B_UP, VEC = (4, 7), 8
BACK = (
    (6, 384, "xz", "ring"),
    (6, 384, "zx", "ring"),
    (6, 384, "xz", "wide"),
    (6, 384, "zx", "ring"),
    (6, 768, "xz", "ring"),
    (24, 256, "zx", "ring"),
    (24, 128, "xz", "ring"),
    (6, 768, "zx", "ring"),
    (6, 128, "xz", "wide"),
)
RING = tuple(g for g in range(len(BACK)) if BACK[g][3] == "ring")


def fdot(a, b):
    return jnp.dot(a, b, preferred_element_type=F32)


def dot_nt(a, b):
    return lax.dot_general(a, b, (((1,), (1,)), ((), ())), preferred_element_type=F32)


def dot_tn(a, b):
    return lax.dot_general(a, b, (((0,), (0,)), ((), ())), preferred_element_type=F32)


def outer(a, b):
    column = jnp.transpose(a[512:528].astype(F32))
    row = b[512:528].astype(F32)
    return dot_tn(a[:512], b[:512]) + column[:, 0:1] * row[0:1] + column[:, 1:2] * row[1:2]


def fold(v):
    return jnp.sum(v.reshape(-1, 8, v.shape[-1]), 0)


def iota(shape, dim):
    return lax.broadcasted_iota(jnp.int32, shape, dim)


def rows_at(i, size):
    return pl.ds(pl.multiple_of(i * size, size), size)


def centre(x):
    cen = x - jnp.mean(x, -1, keepdims=True)
    inv = lax.rsqrt(jnp.mean(cen * cen, -1, keepdims=True) + EPSILON)
    return cen * inv, inv


def norm_back(q, nm, inv):
    return inv * (q - jnp.mean(q, -1, keepdims=True) - nm * jnp.mean(q * nm, -1, keepdims=True))


class Many:
    def __init__(self, send_sem, recv_sem, total):
        self.send_sem, self.recv_sem, self.total = send_sem, recv_sem, total

    def wait_send(self):
        pltpu.make_async_copy(self.total, self.total, self.send_sem).wait()

    def wait_recv(self):
        pltpu.make_async_copy(self.total, self.total, self.recv_sem).wait()

    def wait(self):
        self.wait_send()
        self.wait_recv()


class Place:
    def __init__(self, pool):
        img = lax.axis_index("img")
        self.y = lax.axis_index("row")
        self.x = img // 8
        self.z = (img // 2) % 4
        self.c = img % 2
        self.slot = self.c * 4 + self.y
        self.lane = 192 * (self.z % 2) + 24 * self.slot
        self.pool, self.used = pool, 0

    def sem(self):
        self.used += 1
        assert self.used <= POOL
        return self.pool.at[self.used - 1]

    def at(self, dx=0, dz=0, dy=0, flip=0):
        x = (self.x + dx) % 4
        z = (self.z + dz) % 4
        y = (self.y + dy) % 4
        c = 1 - self.c if flip else self.c
        return ((x * 4 + z) * 2 + c, y)

    def near(self):
        return [(dy, flip) for flip in (0, 1) for dy in range(4) if (dy, flip) != (0, 0)]

    def plane(self):
        return [(dx, dz) for dx in range(4) for dz in range(4) if (dx, dz) != (0, 0)]

    def signal(self):
        barrier = pltpu.get_barrier_semaphore()
        for dy, flip in self.near():
            pl.semaphore_signal(barrier, inc=1, device_id=self.at(dy=dy, flip=flip), device_id_type=MESH)
        for dx, dz in self.plane():
            pl.semaphore_signal(barrier, inc=1, device_id=self.at(dx=dx, dz=dz), device_id_type=MESH)

    def await_all(self):
        pl.semaphore_wait(pltpu.get_barrier_semaphore(), 22)

    def send(self, src, dst, device):
        copy = pltpu.make_async_remote_copy(
            src_ref=src, dst_ref=dst, send_sem=self.sem(), recv_sem=self.sem(), device_id=device, device_id_type=MESH
        )
        copy.start()
        return copy

    def send_many(self, copies, total):
        many = Many(self.sem(), self.sem(), total)
        for src, dst, device in copies:
            pltpu.make_async_remote_copy(
                src_ref=src, dst_ref=dst, send_sem=many.send_sem, recv_sem=many.recv_sem, device_id=device, device_id_type=MESH
            ).start()
        return many

    def local(self, src, dst):
        copy = pltpu.make_async_copy(src, dst, self.sem())
        copy.start()
        return copy


def lane_of_rows(order, ref, second, lo=0, size=4):
    return ref.at[pl.ds(lo, size), second] if order == "xz" else ref.at[second, pl.ds(lo, size)]


def wait_all(copies):
    for copy in copies:
        copy.wait()


class Gather:
    def __init__(self, me, packs, got, wide, stage, whole):
        self.me, self.packs, self.got, self.wide, self.stage, self.whole = me, packs, got, wide, stage, whole
        self.one, self.two, self.three, self.five, self.four = {}, {}, {}, {}, {}

    def first(self, i):
        me, quarter = self.me, GROUPS[PACKS[i][0]][3] == "quarter"
        place = self.got[i].at[me.slot]

        def part(half, y):
            return self.packs[i].at[half, y] if quarter else self.packs[i].at[half]

        row = []
        for dy, flip in me.near():
            half = 1 - me.c if flip else me.c
            row.append((part(half, (me.y + dy) % 4), place, me.at(dy=dy, flip=flip)))
        self.one[i] = [me.local(part(me.c, me.y), place), me.send_many(row, self.got[i].at[pl.ds(0, 7)])]

    def assemble(self, i):
        rho = GROUPS[PACKS[i][0]][0]
        wait_all(self.one[i])
        for d in range(8):
            self.wide[i][d * rho : (d + 1) * rho, :] = self.got[i][d].astype(F32)
        col = 0
        for g in PACKS[i]:
            width = GROUPS[g][1]
            self.stage[g][...] = self.wide[i][:, col : col + width].astype(BF)
            col += width

    def mine(self, g):
        me = self.me
        return self.whole[g].at[me.y, me.c] if GROUPS[g][3] == "quarter" else self.whole[g].at[me.c]

    def second(self, g):
        me, order, mine = self.me, GROUPS[g][2], self.mine(g)
        place = mine.at[me.x, me.z]
        row = [(self.stage[g], place, me.at(dx=k) if order == "xz" else me.at(dz=k)) for k in (1, 3, 2)]
        self.two[g] = [me.local(self.stage[g], place), me.send_many(row, mine.at[0, pl.ds(0, 3)])]

    def on_axis(self, g):
        me = self.me
        if GROUPS[g][2] == "xz":
            return me.z, lambda k: me.at(dz=k)
        return me.x, lambda k: me.at(dx=k)

    def third(self, g):
        wait_all(self.two[g])
        at, device = self.on_axis(g)
        mine = self.mine(g)
        part = lane_of_rows(GROUPS[g][2], mine, at)
        if GROUPS[g][3] == "ring":
            self.three[g] = [self.me.send(part, part, device(k)) for k in (1, 3)]
        else:
            self.three[g] = [self.me.send_many([(part, part, device(k)) for k in (1, 3, 2)], mine.at[pl.ds(0, 3)])]

    def relay(self, g):
        at, device = self.on_axis(g)
        self.five[g] = []
        for j, k in enumerate((1, 3)):
            self.three[g][j].wait_recv()
            part = lane_of_rows(GROUPS[g][2], self.mine(g), (at + 4 - k) % 4, 2 * j, 2)
            self.five[g].append(self.me.send(part, part, device(k)))

    def fifth(self, g):
        wait_all(self.three[g])
        me, mine = self.me, self.mine(g)
        self.six = [me.send(mine, mine, me.at(dy=k)) for k in (1, 3)]
        self.four[g] = [me.send(mine, mine, me.at(flip=1))]

    def sixth(self, g):
        me = self.me
        self.seven = []
        for j, k in enumerate((1, 3)):
            self.six[j].wait_recv()
            quarter = self.whole[g].at[(me.y + 4 - k) % 4, me.c]
            half = quarter.at[pl.ds(2 * j, 2)]
            self.seven.append(me.send(half, half, me.at(dy=k)))
            self.four[g].append(me.send(quarter, quarter, me.at(flip=1)))

    def fourth(self, g):
        me = self.me
        if GROUPS[g][3] == "quarter":
            wait_all(self.seven)
            for copy in self.six:
                copy.wait_send()
            quarter = self.whole[g].at[(me.y + 2) % 4, me.c]
            self.four[g].append(me.send(quarter, quarter, me.at(flip=1)))
            return
        if GROUPS[g][3] == "ring":
            for copy in self.three[g]:
                copy.wait_send()
            wait_all(self.five[g])
        else:
            wait_all(self.three[g])
        self.four[g] = [me.send(self.mine(g), self.mine(g), me.at(flip=1))]

    def done(self, g):
        wait_all(self.four[g])


class Scatter:
    def __init__(self, me, held, sib, far, land, wide, cut, final):
        self.me, self.held, self.sib, self.far, self.land = me, held, sib, far, land
        self.wide, self.cut, self.final = wide, cut, final
        self.zero, self.open, self.a, self.b, self.two, self.three = {}, {}, {}, {}, {}, {}

    def on_axis(self, g):
        me = self.me
        if BACK[g][2] == "xz":
            return me.z, lambda k: me.at(dz=k)
        return me.x, lambda k: me.at(dx=k)

    def piece(self, g, first, second):
        return (first, second) if BACK[g][2] == "xz" else (second, first)

    def start(self, g, src, dst=None):
        copy = self.me.send(src, self.sib[g] if dst is None else dst, self.me.at(flip=1))
        self.zero.setdefault(g, []).append(copy)
        self.open.setdefault(g, []).append(copy)
        return copy

    def drain(self, g):
        for copy in self.open.pop(g, []):
            copy.wait_send()

    def pair(self, g, waits=True):
        me = self.me
        if waits:
            for copy in self.zero[g]:
                copy.wait_recv()
            held, sib = self.held[g], self.sib[g]

            def add(i, carry):
                a, b = i // 4, i % 4
                held[a, b] = (held[a, b].astype(F32) + sib[a, b].astype(F32)).astype(BF)
                return carry

            lax.fori_loop(0, 16, add, 0)
        if BACK[g][3] == "wide":
            row = []
            for dx, dz in me.plane():
                x, z = (me.x + dx) % 4, (me.z + dz) % 4
                row.append((self.held[g].at[x, z], self.land[g].at[me.x * 4 + me.z], me.at(dx=dx, dz=dz)))
            self.two[g] = me.send_many(row, self.land[g].at[pl.ds(0, 15)])
            return
        at, device = self.on_axis(g)
        far = (at + 2) % 4
        self.a[g] = [
            me.send(lane_of_rows(BACK[g][2], self.held[g], far, 2 * j, 2), self.far[g].at[j], device(k)) for j, k in enumerate((1, 3))
        ]

    def pass_on(self, g):
        at, device = self.on_axis(g)
        for copy in self.a[g]:
            copy.wait_recv()
        row = []
        for j, k in enumerate((1, 3)):
            near = (at + k) % 4

            def add(i, carry, j=j, near=near):
                p = self.piece(g, 2 * j + i, near)
                self.held[g][p] = (self.held[g][p].astype(F32) + self.far[g][j, i].astype(F32)).astype(BF)
                return carry

            lax.fori_loop(0, 2, add, 0)
            row.append(self.me.send(lane_of_rows(BACK[g][2], self.held[g], near), self.sib[g].at[j], device(k)))
        self.b[g] = row

    def across(self, g):
        wait_all(self.b[g])
        for copy in self.a[g]:
            copy.wait_send()
        me = self.me
        at, _ = self.on_axis(g)
        held, sib = self.held[g], self.sib[g]

        def add(i, carry):
            p = self.piece(g, i, at)
            held[p] = (held[p].astype(F32) + sib[0, i].astype(F32) + sib[1, i].astype(F32)).astype(BF)
            return carry

        lax.fori_loop(0, 4, add, 0)
        row = []
        for k in (1, 3, 2):
            if BACK[g][2] == "xz":
                src, device = held.at[(me.x + k) % 4, me.z], me.at(dx=k)
            else:
                src, device = held.at[me.x, (me.z + k) % 4], me.at(dz=k)
            row.append((src, self.land[g].at[k - 1], device))
        self.two[g] = me.send_many(row, self.land[g].at[pl.ds(0, 3)])

    def deal(self, g):
        me = self.me
        self.two[g].wait()
        rho, width = BACK[g][:2]
        size = 8 * rho
        own = self.held[g][me.x, me.z].astype(F32)
        land = self.land[g]
        if BACK[g][3] == "wide":
            land[me.x * 4 + me.z] = self.held[g][me.x, me.z]
            total = land[0].astype(F32)
            for i in range(1, 16):
                total = total + land[i].astype(F32)
        else:
            total = own + land[0].astype(F32) + land[1].astype(F32) + land[2].astype(F32)
        self.wide[:size, :width] = total
        for d in range(8):
            self.cut[g][d] = self.wide[d * rho : (d + 1) * rho, :width].astype(BF)
        place = self.final[g].at[me.slot]
        row = []
        for dy, flip in me.near():
            core = 1 - me.c if flip else me.c
            peer = core * 4 + (me.y + dy) % 4
            row.append((self.cut[g].at[peer], place, me.at(dy=dy, flip=flip)))
        self.three[g] = [me.local(self.cut[g].at[me.slot], place), me.send_many(row, self.final[g].at[pl.ds(0, 7)])]

    def finish(self, g):
        wait_all(self.three[g])
        self.drain(g)
        totals = []
        for half in range(2):
            total = self.final[g][half * 4].astype(F32)
            for y in range(1, 4):
                total = total + self.final[g][half * 4 + y].astype(F32)
            totals.append(total)
        return totals


def take(refs, n):
    return refs[:n], refs[n:]


def layer_kernel(*refs):
    ng, nb, npk = len(GROUPS), len(BACK), len(PACKS)
    (patches, cots, cls, cot_cls, mask_index, w_in, w_o, w_u, w_d, b_up_in), refs = take(refs, 10)
    vectors, refs = take(refs, 11)
    (o_in, o_out, o_up, o_down, o_cls, o_gcls, o_vec, o_res, o_gp), refs = take(refs, 9)
    weights_far, refs = take(refs, ng - 3)
    in_v, refs = take(refs, 3)
    (wo, wu, wd), refs = take(refs, 3)
    (x_all, c_all, hidden, attn, qkv, probs, pcs, mixed, branch, hi, gb, acc, gnorm, act, gpre, masks), refs = take(refs, 16)
    (names, vtab, bupv, bupg, bland, bsum, bfinal, sums, cls_l, gcls_l), refs = take(refs, 10)
    packs, refs = take(refs, npk)
    got, refs = take(refs, npk)
    pack_wide, refs = take(refs, npk)
    stage, refs = take(refs, ng)
    gi, refs = take(refs, 3)
    (g_out, gvec, snd_up, snd_da, snd_db), refs = take(refs, 5)
    held_far, refs = take(refs, 4)
    sib, refs = take(refs, nb - 1)
    far, refs = take(refs, len(RING))
    land, refs = take(refs, nb)
    cut, refs = take(refs, nb)
    final, refs = take(refs, nb)
    wide, pool = refs
    me = Place(pool)
    me.signal()

    vtab[...] = jnp.zeros_like(vtab)
    for i, v in enumerate(vectors):
        vtab[i : i + 1, :6] = v[...].astype(F32)
    turned = jnp.transpose(vtab[:, :128])
    spread = iota((8, 384), 1) - me.lane
    line = jnp.zeros((8, 384), F32)
    b_row = b_up_in[...].astype(F32)
    for t in range(24):
        line = jnp.where(spread == t, b_row[:, t : t + 1], line)
    rows = jnp.zeros((8, 128), F32)
    for i in range(3):
        rows = jnp.where(iota((8, 128), 0) == i, line[:, 128 * i : 128 * (i + 1)], rows)
    for h in range(2):
        for t in range(3):
            dst, col = (packs[0], 0) if t == 0 else (packs[1], 384 * (t - 1))
            for part in range(3):
                at = D * part + 384 * h + 128 * t
                dst[h, :, col + 128 * part : col + 128 * (part + 1)] = w_in[:, at : at + 128]
        packs[0][h, :, 384:] = (turned[:6] if h == 0 else rows[:6]).astype(BF)
        for y in range(4):
            packs[2][h, y] = w_u[:, 1536 * h + 384 * y : 1536 * h + 384 * (y + 1)]
        packs[3][h] = w_d[:, 384 * h : 384 * (h + 1)]
        packs[4][h] = w_o[:, 384 * h : 384 * (h + 1)]
    me.await_all()
    whole = tuple(in_v) + tuple(weights_far)
    ga = Gather(me, packs, got, pack_wide, stage, whole)
    def bring(src, dst):
        own, row = [], []
        for image in range(2):
            lane = dst.at[pl.ds(pl.multiple_of(256 * image + 64 * me.y, 64), 64)]
            own.append(me.local(src.at[2 * me.y + image], lane))
            row += [(src.at[2 * ((me.y + k) % 4) + image], lane, me.at(dy=k)) for k in (1, 3, 2)]
        return own + [me.send_many(row, dst.at[pl.ds(0, 384)])]

    for i in (2, 0, 1, 3, 4):
        ga.first(i)
    for i in (2, 0, 1, 3, 4):
        ga.assemble(i)
        for g in PACKS[i]:
            ga.second(g)
    bring_x = bring(patches, x_all)
    pick = iota((8, D), 0)
    place16 = iota((PAD, D), 0)
    for src, dst in ((cls, x_all), (cot_cls, c_all)):
        wide8 = src[...].astype(F32)
        two = jnp.zeros((PAD, D), F32)
        for i in range(2):
            this = jnp.sum(jnp.where(pick == 2 * me.y + i, wide8, 0.0), 0, keepdims=True)
            two = jnp.where(place16 == i, this, two)
        dst[512:, :] = two.astype(BF)
    index0 = mask_index[pl.ds(2 * me.y, 1), :]
    index1 = mask_index[pl.ds(2 * me.y + 1, 1), :] + 256

    def mask_tile(i, carry):
        r = rows_at(i, TILE)
        at = iota((TILE, 154), 0) + TILE * i
        hit = jnp.where(at == index0, 1.0, 0.0) + jnp.where(at == index1, 1.0, 0.0)
        masks[r, :] = jnp.broadcast_to(jnp.max(hit, -1, keepdims=True), (TILE, 128))
        return carry

    lax.fori_loop(0, ROWS // TILE, mask_tile, 0)
    for g in (UP, 0, 1, 2, DOWN[0], DOWN[1], OUT):
        ga.third(g)
    ga.fifth(UP)
    ga.fourth(0)
    ga.relay(DOWN[0])
    ga.relay(DOWN[1])
    wait_all(bring_x)
    ga.done(0)
    names[...] = jnp.transpose(in_v[0][0, :, :, :, 384:].reshape(D, 128).astype(F32))[:16]
    which = iota((96, 128), 0) % 6
    for pair in range(8):
        a, b = pair // 2, 2 * (pair % 2)
        block = in_v[0][1, a, pl.ds(b, 2), :, 384:].reshape(96, 128).astype(F32)
        for i in range(3):
            at = 384 * (pair % 2) + 128 * i
            bupv[pair // 2, :, at : at + 128] = jnp.sum(jnp.where(which == i, block, 0.0), 0, keepdims=True)

    def row(i):
        return names[i : i + 1, :]

    def norm_tile(i, carry):
        r = rows_at(i, TILE)
        x = jnp.where(masks[r, :1] > 0.5, row(TOKEN), x_all[r, :].astype(F32))
        hidden[r, :] = x
        attn[r, :] = (centre(x)[0] * row(GAIN_A) + row(SHIFT_A)).astype(BF)
        return carry

    lax.fori_loop(0, ROWS // TILE, norm_tile, 0)
    ga.relay(OUT)
    ga.sixth(UP)
    ga.fourth(1)
    ga.fourth(2)
    bring_c = bring(cots, c_all)
    mixed[512:, :] = jnp.zeros((PAD, D), BF)

    def project(t):
        for h in range(2):
            p = 2 * t + h
            w = in_v[t][h, :, :, :, :384].reshape(D, 384)
            at = 384 * h + 128 * t
            bias_q, bias_v = names[B_Q : B_Q + 1, at : at + 128], names[B_V : B_V + 1, at : at + 128]
            for m in range(ROWS // MT):
                r = pl.ds(MT * m, MT)
                out = fdot(attn[r, :], w)
                q = (out[:, :128] + bias_q).astype(BF).astype(F32) * SCORE_SCALE
                qkv[p, r, :128] = q.astype(BF)
                qkv[p, r, 128:256] = out[:, 128:256].astype(BF)
                qkv[p, r, 256:] = (out[:, 256:] + bias_v).astype(BF)

    lane_row = iota((1, 128), 1)
    half_low = [jnp.where(lane_row // 64 == hh, 1.0, 0.0).astype(BF) for hh in range(2)]

    def heads(p, r):
        patch = [qkv[p, r, 128 * s : 128 * (s + 1)] for s in range(3)]
        return patch + [qkv[p, 512:528, 128 * s : 128 * (s + 1)] for s in range(3)]

    def join(low, high):
        return jnp.where(lane_row < 64, low, high)

    def attend(p, at, i):
        r = rows_at(i, 256)
        own = iota((PAD, 256), 0) == i
        own1 = iota((PAD, 1), 0) == i
        q, k, v, qc, kc, vc = heads(p, r)
        kcf, vcf = kc.astype(F32), vc.astype(F32)
        turned_out, cls_out = [], []
        for hh in range(2):
            qh, qch = q * half_low[hh], qc * half_low[hh]
            s1 = dot_nt(k, qh)
            s2 = jnp.where(own, dot_nt(kc, qh), -1e30)
            top = jnp.maximum(jnp.max(s1, 0, keepdims=True), jnp.max(s2, 0, keepdims=True))
            e1, e2 = jnp.exp(s1 - top), jnp.exp(s2 - top)
            scale = 1.0 / (jnp.sum(e1, 0, keepdims=True) + jnp.sum(e2, 0, keepdims=True))
            p1, p2 = (e1 * scale).astype(BF), (e2 * scale).astype(BF)
            u = (p * 2 + i) * 2 + hh
            probs[u, :256, :] = p1
            probs[u, 256:, :] = p2
            turned_out.append((dot_tn(v, p1) + dot_tn(vc, p2))[64 * hh : 64 * (hh + 1)])
            sc = dot_nt(qch, k)
            scc = jnp.sum(qch.astype(F32) * kcf, -1, keepdims=True)
            topc = jnp.maximum(jnp.max(sc, -1, keepdims=True), scc)
            ec, ecc = jnp.exp(sc - topc), jnp.exp(scc - topc)
            total = jnp.sum(ec, -1, keepdims=True) + ecc
            pc = jnp.where(own, ec / total, 0.0)
            pcc = jnp.where(own1, ecc / total, 0.0)
            pcs[u, :, :256] = pc
            pcs[u, :, 256:] = jnp.broadcast_to(pcc, (PAD, 128))
            cls_out.append(fdot(pc.astype(BF), v) + pcc.astype(BF).astype(F32) * vcf)
        mixed[r, at : at + 128] = jnp.transpose(jnp.concatenate(turned_out, 0)).astype(BF)
        kept = mixed[512:, at : at + 128].astype(F32)
        mixed[512:, at : at + 128] = (kept + join(*cls_out)).astype(BF)

    loads = {}

    def load_out():
        ga.done(OUT)
        loads["out"] = [me.local(whole[OUT].at[h], wo.at[:, :, :, pl.ds(384 * h, 384)]) for h in range(2)]

    def load_chunk(i):
        k, s = i // 2, i % 2
        h = me.c if s == 1 else 1 - me.c
        n = 2 * h + k
        row = [me.local(whole[UP].at[2 * k + j, h], wu.at[i % 2, :, :, :, pl.ds(384 * j, 384)]) for j in range(2)]
        for half in range(2):
            row.append(me.local(whole[DOWN[0]].at[half, n], wd.at[i % 2, :, :, pl.ds(384 * half, 256)]))
            row.append(me.local(whole[DOWN[1]].at[half, n], wd.at[i % 2, :, :, pl.ds(384 * half + 256, 128)]))
        loads[i] = row

    steps = {
        (0, 0): lambda: (ga.fourth(DOWN[0]), ga.fourth(DOWN[1])),
        (0, 1): lambda: (ga.done(1), ga.fourth(OUT)),
        (1, 0): lambda: ga.fourth(UP),
        (1, 1): lambda: ga.done(2),
        (2, 0): lambda: load_out(),
        (2, 1): lambda: (ga.done(UP), ga.done(DOWN[0]), ga.done(DOWN[1]), load_chunk(0), load_chunk(1)),
    }
    for t in range(3):
        project(t)
        for h in range(2):
            p = 2 * t + h
            at = 384 * h + 128 * t

            def one(i, carry, p=p, at=at):
                attend(p, at, i)
                return carry

            lax.fori_loop(0, 2, one, 0, unroll=True)
            steps[t, h]()

    wait_all(bring_c)
    wait_all(loads["out"])
    sums[...] = jnp.zeros_like(sums)
    w_out = wo[...].reshape(D, D)
    for m in range(ROWS // MT):
        r = pl.ds(MT * m, MT)
        branch[r, :] = fdot(mixed[r, :], w_out) + row(B_OUT)

    def pre_norm(i, carry):
        r = rows_at(i, TILE)
        nm, _ = centre(hidden[r, :] + row(SCALE_A) * branch[r, :])
        hi[r, :] = (nm * row(GAIN_H) + row(SHIFT_H)).astype(BF)
        g = (row(SCALE_H) * c_all[r, :].astype(F32)).astype(BF)
        gb[r, :] = g
        sums[B_DOWN] += fold(g.astype(F32))
        acc[r, :] = jnp.zeros((TILE, D), F32)
        gnorm[r, :] = jnp.zeros((TILE, D), F32)
        return carry

    lax.fori_loop(0, ROWS // TILE, pre_norm, 0)
    held = [gi[t].at[me.c] for t in range(3)]
    held += [g_out.at[me.c], held_far[0], held_far[1], held_far[2], held_far[3], gvec]
    sibs = list(sib) + [None]
    fars = dict(zip(RING, far))
    sc = Scatter(me, held, sibs, fars, land, wide, cut, final)

    def chunk(i):
        k, s = i // 2, i % 2
        n = 2 * (me.c if s == 1 else 1 - me.c) + k
        wait_all(loads[i])
        up, down = wu[i % 2].reshape(D, CHUNK), wd[i % 2].reshape(CHUNK, D)
        bias = bupv[n]
        for m in range(ROWS // MT):
            r = pl.ds(MT * m, MT)
            pre = fdot(hi[r, :], up) + bias
            back = dot_nt(gb[r, :], down)
            cdf = 0.5 * (1.0 + lax.erf(pre * 0.7071067811865476))
            a = (pre * cdf).astype(BF)
            g = ((cdf + pre * (jnp.exp(-0.5 * pre * pre) * 0.3989422804014327)) * back).astype(BF)
            act[r, :] = a
            gpre[r, :] = g
            acc[r, :] += fdot(a, down)
            gnorm[r, :] += dot_nt(g, up)
        g = gpre[...]
        total = jnp.sum(g.astype(F32), 0, keepdims=True)
        bupg[2 * n] = total[:, :384]
        bupg[2 * n + 1] = total[:, 384:]
        grad_up = outer(hi[...], g).astype(BF).reshape(4, 4, 48, CHUNK)
        if s == 0:
            sc.drain(B_UP[0])
            snd_up[...] = grad_up
            sc.start(B_UP[k], snd_up)
        else:
            held_far[0 if k == 0 else 3][...] = grad_up
        grad_down = outer(act[...], gb[...])
        first = me.c == 0
        own = jnp.where(first, grad_down[:, :384], grad_down[:, 384:]).astype(BF)
        other = jnp.where(first, grad_down[:, 384:], grad_down[:, :384]).astype(BF)
        held_far[1][n] = own[:, :256].reshape(4, 192, 256)
        held_far[2][n] = own[:, 256:].reshape(4, 192, 128)
        sc.drain(DOWN[0])
        sc.drain(DOWN[1])
        snd_da[...] = other[:, :256].reshape(4, 192, 256)
        snd_db[...] = other[:, 256:].reshape(4, 192, 128)
        sc.start(DOWN[0], snd_da, sib[DOWN[0]].at[n])
        sc.start(DOWN[1], snd_db, sib[DOWN[1]].at[n])

    chunk(0)
    load_chunk(2)
    chunk(1)
    load_chunk(3)
    sc.pair(B_UP[0])
    chunk(2)
    sc.pass_on(B_UP[0])
    chunk(3)
    sc.pair(DOWN[0])
    sc.pair(DOWN[1])
    sc.pair(B_UP[1])
    b_row = []
    for dx, dz in me.plane():
        x, z = (me.x + dx) % 4, (me.z + dz) % 4
        b_row.append((bupg.at[2 * x + z // 2], bland.at[me.x * 4 + me.z], me.at(dx=dx, dz=dz)))
    b_sent = me.send_many(b_row, bland.at[pl.ds(0, 15)])
    res = x_all

    def post_norm(i, carry):
        r = rows_at(i, TILE)
        bh = acc[r, :] + row(B_DOWN)
        go = c_all[r, :].astype(F32)
        br = branch[r, :]
        mid = hidden[r, :] + row(SCALE_A) * br
        nm, inv = centre(mid)
        res[r, :] = (mid + row(SCALE_H) * bh).astype(BF)
        sums[SCALE_H] += fold(go * bh)
        gn = gnorm[r, :]
        sums[GAIN_H] += fold(gn * nm)
        sums[SHIFT_H] += fold(gn)
        gm = go + norm_back(gn * row(GAIN_H), nm, inv)
        acc[r, :] = gm
        sums[SCALE_A] += fold(gm * br)
        g = (row(SCALE_A) * gm).astype(BF)
        gb[r, :] = g
        sums[B_OUT] += fold(g.astype(F32))
        return carry

    lax.fori_loop(0, ROWS // TILE, post_norm, 0)
    shuffle = []

    def home(source, dst, last):
        row = []
        for image in range(2):
            lane = dst.at[2 * me.y + image]
            shuffle.append(me.local(source.at[pl.ds(pl.multiple_of(256 * image + 64 * me.y, 64), 64)], lane))
            for k in (1, 3, 2):
                peer = pl.multiple_of(256 * image + 64 * ((me.y + k) % 4), 64)
                row.append((source.at[pl.ds(peer, 64)], lane, me.at(dy=k)))
        shuffle.append(me.send_many(row, dst.at[pl.ds(0, 6)]))
        block, place = source.at[pl.ds(512, PAD)], last.at[me.y]
        shuffle.append(me.local(block, place))
        shuffle.append(me.send_many([(block, place, me.at(dy=k)) for k in (1, 3, 2)], last.at[pl.ds(0, 3)]))

    home(res, o_res, cls_l)
    grad = outer(mixed[...], gb[...]).astype(BF)
    for h in range(2):
        g_out[h] = grad[:, 384 * h : 384 * (h + 1)].reshape(4, 4, 48, 384)
    sc.start(OUT, g_out.at[1 - me.c])
    g_mix = mixed
    for m in range(ROWS // MT):
        r = pl.ds(MT * m, MT)
        g_mix[r, :] = dot_nt(gb[r, :], w_out).astype(BF)
    gpk = act

    def late(rows, c):
        return dot_tn(jnp.concatenate(rows, 0), jnp.concatenate([c * half_low[0], c * half_low[1]], 0))

    def attend_back(p, at, lane, i):
        r = rows_at(i, 256)
        own1 = iota((PAD, 1), 0) == i
        q, k, v, qc, kc, vc = heads(p, r)
        do, doc = g_mix[r, at : at + 128], g_mix[512:, at : at + 128]
        kcf, vcf, qcf, docf = kc.astype(F32), vc.astype(F32), qc.astype(F32), doc.astype(F32)
        dq_t, dk, dv, dqc, dkc, dvc, late_s, late_p = [], [], [], [], [], [], [], []
        for hh in range(2):
            u = (p * 2 + i) * 2 + hh
            doh, doch = do * half_low[hh], doc * half_low[hh]
            p1, p2 = probs[u, :256, :], probs[u, 256:, :]
            f1, f2 = p1.astype(F32), p2.astype(F32)
            d1, d2 = dot_nt(v, doh), dot_nt(vc, doh)
            delta = jnp.sum(f1 * d1, 0, keepdims=True) + jnp.sum(f2 * d2, 0, keepdims=True)
            s1, s2 = (f1 * (d1 - delta)).astype(BF), (f2 * (d2 - delta)).astype(BF)
            dq_t.append((dot_tn(k, s1) + dot_tn(kc, s2))[64 * hh : 64 * (hh + 1)])
            pc, pcc = pcs[u, :, :256], pcs[u, :, 256:257]
            dc = dot_nt(doch, v)
            dcc = jnp.sum(doch.astype(F32) * vcf, -1, keepdims=True)
            deltac = jnp.sum(pc * dc, -1, keepdims=True) + pcc * dcc
            scb = (pc * (dc - deltac)).astype(BF)
            scc = pcc * (dcc - deltac)
            dqc.append((fdot(scb, k) + scc * kcf) * SCORE_SCALE)
            dk.append(fdot(s1, q))
            late_s.append(scb)
            late_p.append(pc.astype(BF))
            dkc.append(fdot(s2, q) + scc * qcf)
            dv.append(fdot(p1, do))
            dvc.append(fdot(p2, do) + pcc * docf)
        gpk[r, lane : lane + 128] = (jnp.transpose(jnp.concatenate(dq_t, 0)) * SCORE_SCALE).astype(BF)
        gpk[r, lane + 128 : lane + 256] = (join(*dk) + late(late_s, qc)).astype(BF)
        gpk[r, lane + 256 : lane + 384] = (join(*dv) + late(late_p, doc)).astype(BF)
        for s, value in enumerate((dqc, dkc, dvc)):
            lanes = slice(lane + 128 * s, lane + 128 * (s + 1))
            keep = gpk[512:, lanes].astype(F32)
            gpk[512:, lanes] = jnp.where(own1, join(*value), keep).astype(BF)

    b_last = []

    def b_deal():
        b_sent.wait()
        bland[me.x * 4 + me.z] = bupg[2 * me.x + me.z // 2]
        total = bland[0]
        for i in range(1, 16):
            total = total + bland[i]
        bsum[...] = total
        place = bfinal.at[me.slot]
        b_last.append(me.local(bsum, place))
        b_last.append(me.send_many([(bsum, place, me.at(dy=dy, flip=flip)) for dy, flip in me.near()], bfinal.at[pl.ds(0, 7)]))

    back_steps = {
        (0, 0): lambda: (sc.pass_on(DOWN[0]), sc.pass_on(DOWN[1]), sc.pass_on(B_UP[1]), sc.across(B_UP[0])),
        (0, 1): lambda: (sc.start(0, gi[0].at[1 - me.c]), sc.pair(OUT)),
        (1, 0): lambda: (sc.pair(0), b_deal()),
        (1, 1): lambda: (sc.start(1, gi[1].at[1 - me.c]), sc.pass_on(OUT), sc.deal(B_UP[0])),
        (2, 0): lambda: (sc.pair(1), sc.across(DOWN[0]), sc.across(DOWN[1]), sc.across(B_UP[1])),
        (2, 1): lambda: (sc.start(2, gi[2].at[1 - me.c]), sc.pass_on(0)),
    }
    vtab[...] = jnp.zeros_like(vtab)
    for t in range(3):
        for h in range(2):
            p = 2 * t + h
            at = 384 * h + 128 * t
            lane = 384 * h
            gpk[512:, lane : lane + 384] = jnp.zeros((PAD, 384), BF)

            def one(i, carry, p=p, at=at, lane=lane):
                attend_back(p, at, lane, i)
                return carry

            lax.fori_loop(0, 2, one, 0, unroll=True)
            piece = gpk[:, lane : lane + 384]
            gi[t][h] = outer(attn[...], piece).astype(BF).reshape(4, 4, 48, 384)
            total = jnp.sum(piece.astype(F32), 0, keepdims=True)
            vtab[B_Q : B_Q + 1, at : at + 128] = total[:, :128]
            vtab[B_V : B_V + 1, at : at + 128] = total[:, 256:]
            w = in_v[t][h, :, :, :, :384].reshape(D, 384)
            for m in range(ROWS // MT):
                r = pl.ds(MT * m, MT)
                back = dot_nt(gpk[r, lane : lane + 384], w)
                gnorm[r, :] = back if p == 0 else gnorm[r, :] + back
            back_steps[t, h]()

    gp = hi

    def last_norm(i, carry):
        r = rows_at(i, TILE)
        nm, inv = centre(hidden[r, :])
        gn = gnorm[r, :]
        sums[GAIN_A] += fold(gn * nm)
        sums[SHIFT_A] += fold(gn)
        gh = acc[r, :] + norm_back(gn * row(GAIN_A), nm, inv)
        masked = masks[r, :1] > 0.5
        sums[TOKEN] += fold(jnp.where(masked, gh, 0.0))
        gp[r, :] = jnp.where(masked, 0.0, gh).astype(BF)
        return carry

    sc.pair(2)
    lax.fori_loop(0, ROWS // TILE, last_norm, 0)
    for i in (TOKEN, GAIN_A, SHIFT_A, B_OUT, SCALE_A, GAIN_H, SHIFT_H, B_DOWN, SCALE_H):
        vtab[i : i + 1, :] = jnp.sum(sums[i], 0, keepdims=True)
    gvec[...] = jnp.transpose(vtab[...]).astype(BF).reshape(4, 4, 48, 128)
    sc.pair(VEC, waits=False)
    home(gp, o_gp, gcls_l)
    sc.pass_on(1)
    sc.across(OUT)
    sc.across(0)
    for g in (DOWN[0], DOWN[1], B_UP[1]):
        sc.deal(g)
    sc.across(1)
    sc.deal(OUT)
    sc.deal(0)
    sc.deal(2)
    sc.deal(VEC)
    sc.deal(1)
    for k in range(2):
        for half, total in enumerate(sc.finish(B_UP[k])):
            o_up[:, 1536 * half + 768 * k : 1536 * half + 768 * (k + 1)] = total
    for col, width, g in ((0, 256, DOWN[0]), (256, 128, DOWN[1])):
        for half, total in enumerate(sc.finish(g)):
            o_down[:, 384 * half + col : 384 * half + col + width] = total
    for half, total in enumerate(sc.finish(OUT)):
        o_out[:, 384 * half : 384 * (half + 1)] = total
    wait_all(b_last)
    flat = bfinal[0]
    for i in range(1, 8):
        flat = flat + bfinal[i]
    chosen = jnp.where(iota((384, 128), 0) == iota((384, 128), 1) + me.lane, 1.0, 0.0)
    line = lax.dot_general(
        jnp.broadcast_to(flat, (8, 384)), chosen, (((1,), (0,)), ((), ())), precision=lax.Precision.HIGHEST, preferred_element_type=F32
    )

    def finish_in(t):
        for half, total in enumerate(sc.finish(t)):
            for s in range(3):
                at = D * s + 384 * half + 128 * t
                o_in[:, at : at + 128] = total[:, 128 * s : 128 * (s + 1)]

    finish_in(0)
    wait_all(shuffle)
    order = iota((8, D), 0)
    for landed, out in ((cls_l, o_cls), (gcls_l, o_gcls)):
        rows = jnp.zeros((8, D), F32)
        for y in range(4):
            two = landed[y].astype(F32)
            for i in range(2):
                rows = jnp.where(order == 2 * y + i, two[i : i + 1], rows)
        out[...] = rows.astype(BF)
    finish_in(2)
    finish_in(1)
    low, high = sc.finish(VEC)
    vtab[:, :128] = jnp.zeros((128, 128), F32)
    vtab[:6, :128] = low + high
    turned = jnp.transpose(vtab[:, :128])
    o_vec[...] = jnp.where(iota((16, 128), 0) == 11, line[:1], turned[:16])


def layer(patches, cots, cls, cot_cls, mask_index, w_in, w_o, w_u, w_d, b_up, vectors):
    vm = pl.BlockSpec(memory_space=pltpu.VMEM)
    hb = pl.BlockSpec(memory_space=pl.ANY)
    S, V = jax.ShapeDtypeStruct, pltpu.VMEM
    outs = [S((6, 3 * D), F32), S((6, D), F32), S((6, FF), F32), S((24, D), F32), S((8, D), BF), S((8, D), BF), S((16, 128), F32)]
    far = [S((8, 64, D), BF)] * 2
    far += [S(((4,) if mode == "quarter" else ()) + (2, 4, 4, 8 * rho, width), BF) for rho, width, _, mode in GROUPS[3:]]
    pack_width = [sum(GROUPS[g][1] for g in pack) for pack in PACKS]
    pack_rho = [GROUPS[pack[0]][0] for pack in PACKS]
    scratch = [V((2, 4, 4, 48, width), BF) for _, width, _, _ in GROUPS[:3]]
    scratch += [V((4, 4, 48, D), BF), V((2, 4, 4, 48, CHUNK), BF), V((2, 4, 192, D), BF)]
    wide_rows, low_rows = V((ROWS, D), F32), V((ROWS, D), BF)
    scratch += [low_rows, low_rows, wide_rows, low_rows, V((6, ROWS, 384), BF), V((24, KEYS, 256), BF), V((24, PAD, 384), F32)]
    scratch += [low_rows, wide_rows, low_rows, low_rows, wide_rows, wide_rows, low_rows, low_rows, V((ROWS, 128), F32)]
    scratch += [V((16, D), F32), V((128, D), F32), V((4, 1, CHUNK), F32), V((8, 1, 384), F32), V((16, 1, 384), F32)]
    scratch += [V((1, 384), F32), V((8, 1, 384), F32), V((16, 8, D), F32), V((4, PAD, D), BF), V((4, PAD, D), BF)]
    quarter = [GROUPS[pack[0]][3] == "quarter" for pack in PACKS]
    scratch += [V((2, 4, r, w) if q else (2, r, w), BF) for r, w, q in zip(pack_rho, pack_width, quarter)]
    scratch += [V((8, r, w), BF) for r, w in zip(pack_rho, pack_width)]
    scratch += [V((8 * r, w), F32) for r, w in zip(pack_rho, pack_width)]
    scratch += [V((8 * rho, width), BF) for rho, width, _, _ in GROUPS]
    scratch += [V((2, 4, 4, 48, 384), BF)] * 4 + [V((4, 4, 48, 128), BF)]
    scratch += [V((4, 4, 48, CHUNK), BF), V((4, 192, 256), BF), V((4, 192, 128), BF)]
    blocks = [(8 * rho, width) for rho, width, _, _ in BACK]
    scratch += [V((4, 4) + blocks[g], BF) for g in (4, 5, 6, 7)]
    scratch += [V((4, 4) + blocks[g], BF) for g in range(8)]
    scratch += [V((2, 2) + blocks[g], BF) for g in RING]
    scratch += [V((16 if BACK[g][3] == "wide" else 3,) + blocks[g], BF) for g in range(9)]
    scratch += [V((8, rho, width), BF) for rho, width, _, _ in BACK] * 2
    scratch += [V((192, D), F32), pltpu.SemaphoreType.DMA((POOL,))]
    return pl.pallas_call(
        layer_kernel,
        out_shape=outs + far,
        in_specs=[hb] * 2 + [vm] * 19,
        out_specs=[vm] * len(outs) + [hb] * len(far),
        scratch_shapes=scratch,
        compiler_params=pltpu.CompilerParams(collective_id=0, has_side_effects=True, vmem_limit_bytes=63 * 2**20),
        name="layer",
    )(patches, cots, cls, cot_cls, mask_index, w_in, w_o, w_u, w_d, b_up, *vectors)[:9]


def finish_kernel(i_in, i_out, i_up, i_down, i_cls, i_gcls, i_vec, i_res, i_gp, *outs):
    for src, dst in zip((i_in, i_out, i_up, i_down, i_cls, i_gcls, i_res, i_gp), outs):
        dst[...] = src[...]
    for i in range(11):
        outs[8 + i][...] = i_vec[i : i + 1, :6]
    outs[19][...] = i_vec[11:12, :24]


def finish(parts):
    vm = pl.BlockSpec(memory_space=pltpu.VMEM)
    S = jax.ShapeDtypeStruct
    outs = [S(p.shape, p.dtype) for p in parts[:6]] + [S((8, 64, D), BF)] * 2 + [S((1, 6), F32)] * 11 + [S((1, 24), F32)]
    return pl.pallas_call(
        finish_kernel,
        out_shape=outs,
        in_specs=[vm] * 9,
        out_specs=[vm] * 20,
        name="finish",
    )(*parts)


def on_device(
    patches,
    cls_tokens,
    mask_index,
    mask_token,
    attention_gain,
    attention_shift,
    input_weight,
    query_bias,
    value_bias,
    output_weight,
    output_bias,
    attention_scale,
    hidden_gain,
    hidden_shift,
    expand_weight,
    expand_bias,
    reduce_weight,
    reduce_bias,
    hidden_scale,
    cotangent_patches,
    cotangent_cls,
):
    vectors = [mask_token, attention_gain, attention_shift, query_bias, value_bias, output_bias, attention_scale]
    vectors += [hidden_gain, hidden_shift, reduce_bias, hidden_scale]
    parts = layer(
        patches,
        cotangent_patches,
        cls_tokens,
        cotangent_cls,
        mask_index,
        input_weight,
        output_weight,
        expand_weight,
        reduce_weight,
        expand_bias.reshape(1, 24),
        [v.reshape(1, 6) for v in vectors],
    )
    g_in, g_o, g_u, g_d, o_cls, o_gcls, o_res, o_gp, *v = finish(parts)
    g_bup = v[11].reshape(24)
    v = [t.reshape(6) for t in v[:11]]
    return (
        o_res,
        o_cls,
        o_gp,
        o_gcls,
        v[TOKEN],
        v[GAIN_A],
        v[SHIFT_A],
        g_in,
        v[B_Q],
        v[B_V],
        g_o,
        v[B_OUT],
        v[SCALE_A],
        v[GAIN_H],
        v[SHIFT_H],
        g_u,
        g_bup,
        g_d,
        v[B_DOWN],
        v[SCALE_H],
    )


def solution(mesh):
    vector = P(("img", "row"))
    matrix = P(("img", "row"), None)
    image = P("img", "row", None)
    head = P("img", None)
    in_specs = (image, head, head, vector, vector, vector, matrix, vector, vector, matrix, vector, vector, vector, vector)
    in_specs += (matrix, vector, matrix, vector, vector, image, head)
    out_specs = (image, head, image, head, vector, vector, vector, matrix, vector, vector, matrix, vector, vector)
    out_specs += (vector, vector, matrix, vector, matrix, vector, vector)
    return jax.shard_map(on_device, mesh=mesh, in_specs=in_specs, out_specs=out_specs, check_vma=False)
```

```python
import jax
import jax.numpy as jnp
from jax import lax
from jax.experimental import pallas as pl
from jax.experimental.pallas import tpu as pltpu
from jax.sharding import PartitionSpec as P

D = 768
FF = 3072
EPSILON = 1e-06
SCORE_SCALE = 0.125
MESH = pl.DeviceIdType.MESH
BF = jnp.bfloat16
F32 = jnp.float32
ROWS = 528
KEYS = 272
PAD = 16
TILE = 176
MT = 264
CHUNK = 768
POOL = 266

TOKEN, GAIN_A, SHIFT_A, B_Q, B_V, B_OUT, SCALE_A, GAIN_H, SHIFT_H, B_DOWN, SCALE_H = range(11)

OUT, UP, DOWN = 3, 4, (5, 6)
GROUPS = (
    (6, 512, "xz", "two"),
    (6, 384, "zx", "two"),
    (6, 384, "zx", "two"),
    (6, 384, "xz", "ring"),
    (6, 384, "xz", "quarter"),
    (24, 256, "zx", "ring"),
    (24, 128, "xz", "ring"),
)
PACKS = ((0,), (1, 2), (4,), (5, 6), (3,))
B_UP, VEC = (4, 7), 8
BACK = (
    (6, 384, "xz", "ring"),
    (6, 384, "zx", "ring"),
    (6, 384, "xz", "wide"),
    (6, 384, "zx", "ring"),
    (6, 768, "xz", "ring"),
    (24, 256, "zx", "ring"),
    (24, 128, "xz", "ring"),
    (6, 768, "zx", "ring"),
    (6, 128, "xz", "wide"),
)
RING = tuple(g for g in range(len(BACK)) if BACK[g][3] == "ring")


def fdot(a, b):
    return jnp.dot(a, b, preferred_element_type=F32)


def dot_nt(a, b):
    return lax.dot_general(a, b, (((1,), (1,)), ((), ())), preferred_element_type=F32)


def dot_tn(a, b):
    return lax.dot_general(a, b, (((0,), (0,)), ((), ())), preferred_element_type=F32)


def outer(a, b):
    column = jnp.transpose(a[512:528].astype(F32))
    row = b[512:528].astype(F32)
    return dot_tn(a[:512], b[:512]) + column[:, 0:1] * row[0:1] + column[:, 1:2] * row[1:2]


def fold(v):
    return jnp.sum(v.reshape(-1, 8, v.shape[-1]), 0)


def iota(shape, dim):
    return lax.broadcasted_iota(jnp.int32, shape, dim)


def rows_at(i, size):
    return pl.ds(pl.multiple_of(i * size, size), size)


def centre(x):
    cen = x - jnp.mean(x, -1, keepdims=True)
    inv = lax.rsqrt(jnp.mean(cen * cen, -1, keepdims=True) + EPSILON)
    return cen * inv, inv


def norm_back(q, nm, inv):
    return inv * (q - jnp.mean(q, -1, keepdims=True) - nm * jnp.mean(q * nm, -1, keepdims=True))


class Many:
    def __init__(self, send_sem, recv_sem, total):
        self.send_sem, self.recv_sem, self.total = send_sem, recv_sem, total

    def wait_send(self):
        pltpu.make_async_copy(self.total, self.total, self.send_sem).wait()

    def wait_recv(self):
        pltpu.make_async_copy(self.total, self.total, self.recv_sem).wait()

    def wait(self):
        self.wait_send()
        self.wait_recv()


class Place:
    def __init__(self, pool):
        img = lax.axis_index("img")
        self.y = lax.axis_index("row")
        self.x = img // 8
        self.z = (img // 2) % 4
        self.c = img % 2
        self.slot = self.c * 4 + self.y
        self.lane = 192 * (self.z % 2) + 24 * self.slot
        self.pool, self.used = pool, 0

    def sem(self):
        self.used += 1
        assert self.used <= POOL
        return self.pool.at[self.used - 1]

    def at(self, dx=0, dz=0, dy=0, flip=0):
        x = (self.x + dx) % 4
        z = (self.z + dz) % 4
        y = (self.y + dy) % 4
        c = 1 - self.c if flip else self.c
        return ((x * 4 + z) * 2 + c, y)

    def near(self):
        return [(dy, flip) for flip in (0, 1) for dy in range(4) if (dy, flip) != (0, 0)]

    def plane(self):
        return [(dx, dz) for dx in range(4) for dz in range(4) if (dx, dz) != (0, 0)]

    def signal(self):
        barrier = pltpu.get_barrier_semaphore()
        for dy, flip in self.near():
            pl.semaphore_signal(barrier, inc=1, device_id=self.at(dy=dy, flip=flip), device_id_type=MESH)
        for dx, dz in self.plane():
            pl.semaphore_signal(barrier, inc=1, device_id=self.at(dx=dx, dz=dz), device_id_type=MESH)

    def await_all(self):
        pl.semaphore_wait(pltpu.get_barrier_semaphore(), 22)

    def send(self, src, dst, device):
        copy = pltpu.make_async_remote_copy(
            src_ref=src, dst_ref=dst, send_sem=self.sem(), recv_sem=self.sem(), device_id=device, device_id_type=MESH
        )
        copy.start()
        return copy

    def send_many(self, copies, total):
        many = Many(self.sem(), self.sem(), total)
        for src, dst, device in copies:
            pltpu.make_async_remote_copy(
                src_ref=src, dst_ref=dst, send_sem=many.send_sem, recv_sem=many.recv_sem, device_id=device, device_id_type=MESH
            ).start()
        return many

    def local(self, src, dst, sem=None):
        copy = pltpu.make_async_copy(src, dst, self.sem() if sem is None else sem)
        copy.start()
        return copy


def lane_of_rows(order, ref, second, lo=0, size=4):
    return ref.at[pl.ds(lo, size), second] if order == "xz" else ref.at[second, pl.ds(lo, size)]


def wait_all(copies):
    for copy in copies:
        copy.wait()


class Gather:
    def __init__(self, me, packs, got, wide, stage, whole):
        self.me, self.packs, self.got, self.wide, self.stage, self.whole = me, packs, got, wide, stage, whole
        self.one, self.two, self.three, self.five, self.four = {}, {}, {}, {}, {}

    def first(self, i):
        me, quarter = self.me, GROUPS[PACKS[i][0]][3] == "quarter"
        place = self.got[i].at[me.slot]

        def part(half, y):
            return self.packs[i].at[half, y] if quarter else self.packs[i].at[half]

        row = []
        for dy, flip in me.near():
            half = 1 - me.c if flip else me.c
            row.append((part(half, (me.y + dy) % 4), place, me.at(dy=dy, flip=flip)))
        self.one[i] = [me.local(part(me.c, me.y), place), me.send_many(row, self.got[i].at[pl.ds(0, 7)])]

    def assemble(self, i):
        rho = GROUPS[PACKS[i][0]][0]
        wait_all(self.one[i])
        for d in range(8):
            self.wide[i][d * rho : (d + 1) * rho, :] = self.got[i][d].astype(F32)
        col = 0
        for g in PACKS[i]:
            width = GROUPS[g][1]
            self.stage[g][...] = self.wide[i][:, col : col + width].astype(BF)
            col += width

    def mine(self, g):
        me = self.me
        return self.whole[g].at[me.y, me.c] if GROUPS[g][3] == "quarter" else self.whole[g].at[me.c]

    def second(self, g):
        me, order, mine = self.me, GROUPS[g][2], self.mine(g)
        place = mine.at[me.x, me.z]
        row = [(self.stage[g], place, me.at(dx=k) if order == "xz" else me.at(dz=k)) for k in (1, 3, 2)]
        self.two[g] = [me.local(self.stage[g], place), me.send_many(row, mine.at[0, pl.ds(0, 3)])]

    def on_axis(self, g):
        me = self.me
        if GROUPS[g][2] == "xz":
            return me.z, lambda k: me.at(dz=k)
        return me.x, lambda k: me.at(dx=k)

    def third(self, g):
        wait_all(self.two[g])
        at, device = self.on_axis(g)
        mine = self.mine(g)
        part = lane_of_rows(GROUPS[g][2], mine, at)
        if GROUPS[g][3] == "ring":
            self.three[g] = [self.me.send(part, part, device(k)) for k in (1, 3)]
        else:
            self.three[g] = [self.me.send_many([(part, part, device(k)) for k in (1, 3, 2)], mine.at[pl.ds(0, 3)])]

    def relay(self, g):
        at, device = self.on_axis(g)
        self.five[g] = []
        for j, k in enumerate((1, 3)):
            self.three[g][j].wait_recv()
            part = lane_of_rows(GROUPS[g][2], self.mine(g), (at + 4 - k) % 4, 2 * j, 2)
            self.five[g].append(self.me.send(part, part, device(k)))

    def fifth(self, g):
        wait_all(self.three[g])
        me, mine = self.me, self.mine(g)
        self.six = [me.send(mine, mine, me.at(dy=k)) for k in (1, 3)]
        self.four[g] = [me.send(mine, mine, me.at(flip=1))]

    def sixth(self, g):
        me = self.me
        self.seven = []
        for j, k in enumerate((1, 3)):
            self.six[j].wait_recv()
            quarter = self.whole[g].at[(me.y + 4 - k) % 4, me.c]
            half = quarter.at[pl.ds(2 * j, 2)]
            self.seven.append(me.send(half, half, me.at(dy=k)))
            self.four[g].append(me.send(quarter, quarter, me.at(flip=1)))

    def fourth(self, g):
        me = self.me
        if GROUPS[g][3] == "quarter":
            wait_all(self.seven)
            for copy in self.six:
                copy.wait_send()
            quarter = self.whole[g].at[(me.y + 2) % 4, me.c]
            self.four[g].append(me.send(quarter, quarter, me.at(flip=1)))
            return
        if GROUPS[g][3] == "ring":
            for copy in self.three[g]:
                copy.wait_send()
            wait_all(self.five[g])
        else:
            wait_all(self.three[g])
        self.four[g] = [me.send(self.mine(g), self.mine(g), me.at(flip=1))]

    def done(self, g):
        wait_all(self.four[g])


class Scatter:
    def __init__(self, me, held, sib, far, land, wide, cut, final):
        self.me, self.held, self.sib, self.far, self.land = me, held, sib, far, land
        self.wide, self.cut, self.final = wide, cut, final
        self.zero, self.open, self.a, self.b, self.two, self.three = {}, {}, {}, {}, {}, {}

    def on_axis(self, g):
        me = self.me
        if BACK[g][2] == "xz":
            return me.z, lambda k: me.at(dz=k)
        return me.x, lambda k: me.at(dx=k)

    def piece(self, g, first, second):
        return (first, second) if BACK[g][2] == "xz" else (second, first)

    def start(self, g, src, dst=None):
        copy = self.me.send(src, self.sib[g] if dst is None else dst, self.me.at(flip=1))
        self.zero.setdefault(g, []).append(copy)
        self.open.setdefault(g, []).append(copy)
        return copy

    def drain(self, g):
        for copy in self.open.pop(g, []):
            copy.wait_send()

    def pair(self, g, waits=True):
        me = self.me
        if waits:
            for copy in self.zero[g]:
                copy.wait_recv()
            held, sib = self.held[g], self.sib[g]

            def add(i, carry):
                a, b = i // 4, i % 4
                held[a, b] = (held[a, b].astype(F32) + sib[a, b].astype(F32)).astype(BF)
                return carry

            lax.fori_loop(0, 16, add, 0)
        if BACK[g][3] == "wide":
            row = []
            for dx, dz in me.plane():
                x, z = (me.x + dx) % 4, (me.z + dz) % 4
                row.append((self.held[g].at[x, z], self.land[g].at[me.x * 4 + me.z], me.at(dx=dx, dz=dz)))
            self.two[g] = me.send_many(row, self.land[g].at[pl.ds(0, 15)])
            return
        at, device = self.on_axis(g)
        far = (at + 2) % 4
        self.a[g] = [
            me.send(lane_of_rows(BACK[g][2], self.held[g], far, 2 * j, 2), self.far[g].at[j], device(k)) for j, k in enumerate((1, 3))
        ]

    def pass_on(self, g):
        at, device = self.on_axis(g)
        for copy in self.a[g]:
            copy.wait_recv()
        row = []
        for j, k in enumerate((1, 3)):
            near = (at + k) % 4

            def add(i, carry, j=j, near=near):
                p = self.piece(g, 2 * j + i, near)
                self.held[g][p] = (self.held[g][p].astype(F32) + self.far[g][j, i].astype(F32)).astype(BF)
                return carry

            lax.fori_loop(0, 2, add, 0)
            row.append(self.me.send(lane_of_rows(BACK[g][2], self.held[g], near), self.sib[g].at[j], device(k)))
        self.b[g] = row

    def across(self, g):
        wait_all(self.b[g])
        for copy in self.a[g]:
            copy.wait_send()
        me = self.me
        at, _ = self.on_axis(g)
        held, sib = self.held[g], self.sib[g]

        def add(i, carry):
            p = self.piece(g, i, at)
            held[p] = (held[p].astype(F32) + sib[0, i].astype(F32) + sib[1, i].astype(F32)).astype(BF)
            return carry

        lax.fori_loop(0, 4, add, 0)
        row = []
        for k in (1, 3, 2):
            if BACK[g][2] == "xz":
                src, device = held.at[(me.x + k) % 4, me.z], me.at(dx=k)
            else:
                src, device = held.at[me.x, (me.z + k) % 4], me.at(dz=k)
            row.append((src, self.land[g].at[k - 1], device))
        self.two[g] = me.send_many(row, self.land[g].at[pl.ds(0, 3)])

    def deal(self, g):
        me = self.me
        self.two[g].wait()
        rho, width = BACK[g][:2]
        size = 8 * rho
        own = self.held[g][me.x, me.z].astype(F32)
        land = self.land[g]
        if BACK[g][3] == "wide":
            land[me.x * 4 + me.z] = self.held[g][me.x, me.z]
            total = land[0].astype(F32)
            for i in range(1, 16):
                total = total + land[i].astype(F32)
        else:
            total = own + land[0].astype(F32) + land[1].astype(F32) + land[2].astype(F32)
        self.wide[:size, :width] = total
        for d in range(8):
            self.cut[g][d] = self.wide[d * rho : (d + 1) * rho, :width].astype(BF)
        place = self.final[g].at[me.slot]
        row = []
        for dy, flip in me.near():
            core = 1 - me.c if flip else me.c
            peer = core * 4 + (me.y + dy) % 4
            row.append((self.cut[g].at[peer], place, me.at(dy=dy, flip=flip)))
        self.three[g] = [me.local(self.cut[g].at[me.slot], place), me.send_many(row, self.final[g].at[pl.ds(0, 7)])]

    def finish(self, g):
        wait_all(self.three[g])
        self.drain(g)
        totals = []
        for half in range(2):
            total = self.final[g][half * 4].astype(F32)
            for y in range(1, 4):
                total = total + self.final[g][half * 4 + y].astype(F32)
            totals.append(total)
        return totals


def take(refs, n):
    return refs[:n], refs[n:]


def layer_kernel(*refs):
    ng, nb, npk = len(GROUPS), len(BACK), len(PACKS)
    (patches, cots, cls, cot_cls, mask_index, w_in, w_o, w_u, w_d, b_up_in), refs = take(refs, 10)
    vectors, refs = take(refs, 11)
    (o_in, o_out, o_up, o_down, o_cls, o_gcls, o_vec, o_res, o_gp), refs = take(refs, 9)
    weights_far, refs = take(refs, ng - 3)
    in_v, refs = take(refs, 3)
    (wo, wu, wd), refs = take(refs, 3)
    (x_all, c_all, hidden, attn, qkv, probs, pcs, mixed, branch, hi, gb, acc, gnorm, act, gpre, masks), refs = take(refs, 16)
    (names, vtab, bupv, bupg, bland, bsum, bfinal, sums, cls_l, gcls_l), refs = take(refs, 10)
    packs, refs = take(refs, npk)
    got, refs = take(refs, npk)
    pack_wide, refs = take(refs, npk)
    stage, refs = take(refs, ng)
    gi, refs = take(refs, 3)
    (g_out, gvec, snd_up, snd_da, snd_db), refs = take(refs, 5)
    held_far, refs = take(refs, 4)
    sib, refs = take(refs, nb - 1)
    far, refs = take(refs, len(RING))
    land, refs = take(refs, nb)
    cut, refs = take(refs, nb)
    final, refs = take(refs, nb)
    wide, pool = refs
    me = Place(pool)
    me.signal()

    vtab[...] = jnp.zeros_like(vtab)
    for i, v in enumerate(vectors):
        vtab[i : i + 1, :6] = v[...].astype(F32)
    turned = jnp.transpose(vtab[:, :128])
    spread = iota((8, 384), 1) - me.lane
    line = jnp.zeros((8, 384), F32)
    b_row = b_up_in[...].astype(F32)
    for t in range(24):
        line = jnp.where(spread == t, b_row[:, t : t + 1], line)
    rows = jnp.zeros((8, 128), F32)
    for i in range(3):
        rows = jnp.where(iota((8, 128), 0) == i, line[:, 128 * i : 128 * (i + 1)], rows)
    for h in range(2):
        for t in range(3):
            dst, col = (packs[0], 0) if t == 0 else (packs[1], 384 * (t - 1))
            for part in range(3):
                at = D * part + 384 * h + 128 * t
                dst[h, :, col + 128 * part : col + 128 * (part + 1)] = w_in[:, at : at + 128]
        packs[0][h, :, 384:] = (turned[:6] if h == 0 else rows[:6]).astype(BF)
        for y in range(4):
            packs[2][h, y] = w_u[:, 1536 * h + 384 * y : 1536 * h + 384 * (y + 1)]
        packs[3][h] = w_d[:, 384 * h : 384 * (h + 1)]
        packs[4][h] = w_o[:, 384 * h : 384 * (h + 1)]
    me.await_all()
    whole = tuple(in_v) + tuple(weights_far)
    ga = Gather(me, packs, got, pack_wide, stage, whole)
    def bring(src, dst):
        own, row = [], []
        for image in range(2):
            lane = dst.at[pl.ds(pl.multiple_of(256 * image + 64 * me.y, 64), 64)]
            own.append(me.local(src.at[2 * me.y + image], lane))
            row += [(src.at[2 * ((me.y + k) % 4) + image], lane, me.at(dy=k)) for k in (1, 3, 2)]
        return own + [me.send_many(row, dst.at[pl.ds(0, 384)])]

    for i in (2, 0, 3, 4, 1):
        ga.first(i)
    for i in (2, 0, 3, 4, 1):
        ga.assemble(i)
        for g in PACKS[i]:
            ga.second(g)
    bring_x = bring(patches, x_all)
    pick = iota((8, D), 0)
    place16 = iota((PAD, D), 0)
    for src, dst in ((cls, x_all), (cot_cls, c_all)):
        wide8 = src[...].astype(F32)
        two = jnp.zeros((PAD, D), F32)
        for i in range(2):
            this = jnp.sum(jnp.where(pick == 2 * me.y + i, wide8, 0.0), 0, keepdims=True)
            two = jnp.where(place16 == i, this, two)
        dst[512:, :] = two.astype(BF)
    index0 = mask_index[pl.ds(2 * me.y, 1), :]
    index1 = mask_index[pl.ds(2 * me.y + 1, 1), :] + 256

    def mask_tile(i, carry):
        r = rows_at(i, TILE)
        at = iota((TILE, 154), 0) + TILE * i
        hit = jnp.where(at == index0, 1.0, 0.0) + jnp.where(at == index1, 1.0, 0.0)
        masks[r, :] = jnp.broadcast_to(jnp.max(hit, -1, keepdims=True), (TILE, 128))
        return carry

    lax.fori_loop(0, ROWS // TILE, mask_tile, 0)
    for g in (UP, 0, DOWN[0], DOWN[1], 1, 2, OUT):
        ga.third(g)
    ga.fifth(UP)
    ga.relay(DOWN[0])
    ga.relay(DOWN[1])
    ga.fourth(0)
    ga.sixth(UP)
    wait_all(bring_x)
    ga.done(0)
    names[...] = jnp.transpose(in_v[0][0, :, :, :, 384:].reshape(D, 128).astype(F32))[:16]
    which = iota((96, 128), 0) % 6
    for pair in range(8):
        a, b = pair // 2, 2 * (pair % 2)
        block = in_v[0][1, a, pl.ds(b, 2), :, 384:].reshape(96, 128).astype(F32)
        for i in range(3):
            at = 384 * (pair % 2) + 128 * i
            bupv[pair // 2, :, at : at + 128] = jnp.sum(jnp.where(which == i, block, 0.0), 0, keepdims=True)

    def row(i):
        return names[i : i + 1, :]

    def norm_tile(i, carry):
        r = rows_at(i, TILE)
        x = jnp.where(masks[r, :1] > 0.5, row(TOKEN), x_all[r, :].astype(F32))
        hidden[r, :] = x
        attn[r, :] = (centre(x)[0] * row(GAIN_A) + row(SHIFT_A)).astype(BF)
        return carry

    lax.fori_loop(0, ROWS // TILE, norm_tile, 0)
    ga.relay(OUT)
    ga.fourth(1)
    ga.fourth(2)
    bring_c = bring(cots, c_all)
    mixed[512:, :] = jnp.zeros((PAD, D), BF)

    def project(t):
        for h in range(2):
            p = 2 * t + h
            w = in_v[t][h, :, :, :, :384].reshape(D, 384)
            at = 384 * h + 128 * t
            bias_q, bias_v = names[B_Q : B_Q + 1, at : at + 128], names[B_V : B_V + 1, at : at + 128]
            for m in range(ROWS // MT):
                r = pl.ds(MT * m, MT)
                out = fdot(attn[r, :], w)
                q = (out[:, :128] + bias_q).astype(BF).astype(F32) * SCORE_SCALE
                qkv[p, r, :128] = q.astype(BF)
                qkv[p, r, 128:256] = out[:, 128:256].astype(BF)
                qkv[p, r, 256:] = (out[:, 256:] + bias_v).astype(BF)

    lane_row = iota((1, 128), 1)
    half_low = [jnp.where(lane_row // 64 == hh, 1.0, 0.0).astype(BF) for hh in range(2)]

    def heads(p, r):
        patch = [qkv[p, r, 128 * s : 128 * (s + 1)] for s in range(3)]
        return patch + [qkv[p, 512:528, 128 * s : 128 * (s + 1)] for s in range(3)]

    def join(low, high):
        return jnp.where(lane_row < 64, low, high)

    def attend(p, at, i):
        r = rows_at(i, 256)
        own = iota((PAD, 256), 0) == i
        own1 = iota((PAD, 1), 0) == i
        q, k, v, qc, kc, vc = heads(p, r)
        kcf, vcf = kc.astype(F32), vc.astype(F32)
        turned_out, cls_out = [], []
        for hh in range(2):
            qh, qch = q * half_low[hh], qc * half_low[hh]
            s1 = dot_nt(k, qh)
            s2 = jnp.where(own, dot_nt(kc, qh), -1e30)
            top = jnp.maximum(jnp.max(s1, 0, keepdims=True), jnp.max(s2, 0, keepdims=True))
            e1, e2 = jnp.exp(s1 - top), jnp.exp(s2 - top)
            scale = 1.0 / (jnp.sum(e1, 0, keepdims=True) + jnp.sum(e2, 0, keepdims=True))
            p1, p2 = (e1 * scale).astype(BF), (e2 * scale).astype(BF)
            u = (p * 2 + i) * 2 + hh
            probs[u, :256, :] = p1
            probs[u, 256:, :] = p2
            turned_out.append((dot_tn(v, p1) + dot_tn(vc, p2))[64 * hh : 64 * (hh + 1)])
            sc = dot_nt(qch, k)
            scc = jnp.sum(qch.astype(F32) * kcf, -1, keepdims=True)
            topc = jnp.maximum(jnp.max(sc, -1, keepdims=True), scc)
            ec, ecc = jnp.exp(sc - topc), jnp.exp(scc - topc)
            total = jnp.sum(ec, -1, keepdims=True) + ecc
            pc = jnp.where(own, ec / total, 0.0)
            pcc = jnp.where(own1, ecc / total, 0.0)
            pcs[u, :, :256] = pc
            pcs[u, :, 256:] = jnp.broadcast_to(pcc, (PAD, 128))
            cls_out.append(fdot(pc.astype(BF), v) + pcc.astype(BF).astype(F32) * vcf)
        mixed[r, at : at + 128] = jnp.transpose(jnp.concatenate(turned_out, 0)).astype(BF)
        kept = mixed[512:, at : at + 128].astype(F32)
        mixed[512:, at : at + 128] = (kept + join(*cls_out)).astype(BF)

    loads, load_sems = {}, [[me.sem() for _ in range(6)] for _ in range(2)]

    def load_out():
        ga.done(OUT)
        loads["out"] = [me.local(whole[OUT].at[h], wo.at[:, :, :, pl.ds(384 * h, 384)]) for h in range(2)]

    def load_chunk(i):
        k, s = i // 2 % 2, i % 2
        h = me.c if s == 1 else 1 - me.c
        n = 2 * h + k
        sems = load_sems[i % 2]
        row = [me.local(whole[UP].at[2 * k + j, h], wu.at[i % 2, :, :, :, pl.ds(384 * j, 384)], sems[j]) for j in range(2)]
        for half in range(2):
            row.append(me.local(whole[DOWN[0]].at[half, n], wd.at[i % 2, :, :, pl.ds(384 * half, 256)], sems[2 + 2 * half]))
            row.append(me.local(whole[DOWN[1]].at[half, n], wd.at[i % 2, :, :, pl.ds(384 * half + 256, 128)], sems[3 + 2 * half]))
        loads[i] = row

    steps = {
        (0, 0): lambda: (ga.fourth(DOWN[0]), ga.fourth(DOWN[1])),
        (0, 1): lambda: (ga.done(1), ga.fourth(OUT)),
        (1, 0): lambda: ga.fourth(UP),
        (1, 1): lambda: ga.done(2),
        (2, 0): lambda: load_out(),
        (2, 1): lambda: (ga.done(UP), ga.done(DOWN[0]), ga.done(DOWN[1]), load_chunk(0), load_chunk(1)),
    }
    for t in range(3):
        project(t)
        for h in range(2):
            p = 2 * t + h
            at = 384 * h + 128 * t

            def one(i, carry, p=p, at=at):
                attend(p, at, i)
                return carry

            lax.fori_loop(0, 2, one, 0, unroll=True)
            steps[t, h]()

    wait_all(bring_c)
    wait_all(loads["out"])
    sums[...] = jnp.zeros_like(sums)
    w_out = wo[...].reshape(D, D)
    for m in range(ROWS // MT):
        r = pl.ds(MT * m, MT)
        branch[r, :] = fdot(mixed[r, :], w_out) + row(B_OUT)

    def pre_norm(i, carry):
        r = rows_at(i, TILE)
        nm, _ = centre(hidden[r, :] + row(SCALE_A) * branch[r, :])
        hi[r, :] = (nm * row(GAIN_H) + row(SHIFT_H)).astype(BF)
        g = (row(SCALE_H) * c_all[r, :].astype(F32)).astype(BF)
        gb[r, :] = g
        sums[B_DOWN] += fold(g.astype(F32))
        acc[r, :] = jnp.zeros((TILE, D), F32)
        gnorm[r, :] = jnp.zeros((TILE, D), F32)
        return carry

    lax.fori_loop(0, ROWS // TILE, pre_norm, 0)
    held = [gi[t].at[me.c] for t in range(3)]
    held += [g_out.at[me.c], held_far[0], held_far[1], held_far[2], held_far[3], gvec]
    sibs = list(sib) + [None]
    fars = dict(zip(RING, far))
    sc = Scatter(me, held, sibs, fars, land, wide, cut, final)

    slopes = (gi[0], gi[1], gi[2], g_out)

    def slope_rows(i, m):
        for piece in range(MT * m // 48, MT * (m + 1) // 48 + 1):
            low, high = max(MT * m, 48 * piece), min(MT * (m + 1), 48 * (piece + 1))
            if low < high:
                for half in range(2):
                    place = (half, piece // 4, piece % 4, slice(low - 48 * piece, high - 48 * piece))
                    yield place, slice(low - MT * m, high - MT * m), slice(384 * half, 384 * (half + 1))

    def chunk_forward(i):
        k, s = i // 2, i % 2
        n = 2 * (me.c if s == 1 else 1 - me.c) + k
        wait_all(loads[i])
        up, down = wu[i % 2].reshape(D, CHUNK), wd[i % 2].reshape(CHUNK, D)
        bias = bupv[n]
        for m in range(ROWS // MT):
            r = pl.ds(MT * m, MT)
            pre = fdot(hi[r, :], up) + bias
            cdf = 0.5 * (1.0 + lax.erf(pre * 0.7071067811865476))
            a = (pre * cdf).astype(BF)
            slope = (cdf + pre * (jnp.exp(-0.5 * pre * pre) * 0.3989422804014327)).astype(BF)
            for place, rows, lanes in slope_rows(i, m):
                slopes[i][place] = slope[rows, lanes]
            act[r, :] = a
            acc[r, :] += fdot(a, down)
        grad_down = outer(act[...], gb[...])
        first = me.c == 0
        own = jnp.where(first, grad_down[:, :384], grad_down[:, 384:]).astype(BF)
        other = jnp.where(first, grad_down[:, 384:], grad_down[:, :384]).astype(BF)
        held_far[1][n] = own[:, :256].reshape(4, 192, 256)
        held_far[2][n] = own[:, 256:].reshape(4, 192, 128)
        sc.drain(DOWN[0])
        sc.drain(DOWN[1])
        snd_da[...] = other[:, :256].reshape(4, 192, 256)
        snd_db[...] = other[:, 256:].reshape(4, 192, 128)
        sc.start(DOWN[0], snd_da, sib[DOWN[0]].at[n])
        sc.start(DOWN[1], snd_db, sib[DOWN[1]].at[n])

    def chunk_backward(i):
        k, s = i // 2, i % 2
        n = 2 * (me.c if s == 1 else 1 - me.c) + k
        wait_all(loads[4 + i])
        up, down = wu[i % 2].reshape(D, CHUNK), wd[i % 2].reshape(CHUNK, D)
        for m in range(ROWS // MT):
            r = pl.ds(MT * m, MT)
            back = dot_nt(gb[r, :], down)
            for place, rows, lanes in slope_rows(i, m):
                here = slice(MT * m + rows.start, MT * m + rows.stop)
                gpre[here, lanes] = (slopes[i][place].astype(F32) * back[rows, lanes]).astype(BF)
            gnorm[r, :] += dot_nt(gpre[r, :], up)
        g = gpre[...]
        total = jnp.sum(g.astype(F32), 0, keepdims=True)
        bupg[2 * n] = total[:, :384]
        bupg[2 * n + 1] = total[:, 384:]
        grad_up = outer(hi[...], g).astype(BF).reshape(4, 4, 48, CHUNK)
        if s == 0:
            sc.drain(B_UP[0])
            snd_up[...] = grad_up
            sc.start(B_UP[k], snd_up)
        else:
            held_far[0 if k == 0 else 3][...] = grad_up

    for i in range(4):
        chunk_forward(i)
        load_chunk(i + 2)
    chunk_backward(0)
    load_chunk(6)
    sc.pair(DOWN[0])
    sc.pair(DOWN[1])
    chunk_backward(1)
    load_chunk(7)
    chunk_backward(2)
    sc.pair(B_UP[0])
    sc.pass_on(DOWN[0])
    sc.pass_on(DOWN[1])
    chunk_backward(3)
    sc.pair(B_UP[1])
    b_row = []
    for dx, dz in me.plane():
        x, z = (me.x + dx) % 4, (me.z + dz) % 4
        b_row.append((bupg.at[2 * x + z // 2], bland.at[me.x * 4 + me.z], me.at(dx=dx, dz=dz)))
    b_sent = me.send_many(b_row, bland.at[pl.ds(0, 15)])
    res = x_all

    def post_norm(i, carry):
        r = rows_at(i, TILE)
        bh = acc[r, :] + row(B_DOWN)
        go = c_all[r, :].astype(F32)
        br = branch[r, :]
        mid = hidden[r, :] + row(SCALE_A) * br
        nm, inv = centre(mid)
        res[r, :] = (mid + row(SCALE_H) * bh).astype(BF)
        sums[SCALE_H] += fold(go * bh)
        gn = gnorm[r, :]
        sums[GAIN_H] += fold(gn * nm)
        sums[SHIFT_H] += fold(gn)
        gm = go + norm_back(gn * row(GAIN_H), nm, inv)
        acc[r, :] = gm
        sums[SCALE_A] += fold(gm * br)
        g = (row(SCALE_A) * gm).astype(BF)
        gb[r, :] = g
        sums[B_OUT] += fold(g.astype(F32))
        return carry

    lax.fori_loop(0, ROWS // TILE, post_norm, 0)
    shuffle = []

    def home(source, dst, last):
        row = []
        for image in range(2):
            lane = dst.at[2 * me.y + image]
            shuffle.append(me.local(source.at[pl.ds(pl.multiple_of(256 * image + 64 * me.y, 64), 64)], lane))
            for k in (1, 3, 2):
                peer = pl.multiple_of(256 * image + 64 * ((me.y + k) % 4), 64)
                row.append((source.at[pl.ds(peer, 64)], lane, me.at(dy=k)))
        shuffle.append(me.send_many(row, dst.at[pl.ds(0, 6)]))
        block, place = source.at[pl.ds(512, PAD)], last.at[me.y]
        shuffle.append(me.local(block, place))
        shuffle.append(me.send_many([(block, place, me.at(dy=k)) for k in (1, 3, 2)], last.at[pl.ds(0, 3)]))

    home(res, o_res, cls_l)
    sc.pass_on(B_UP[0])
    grad = outer(mixed[...], gb[...]).astype(BF)
    for h in range(2):
        g_out[h] = grad[:, 384 * h : 384 * (h + 1)].reshape(4, 4, 48, 384)
    sc.start(OUT, g_out.at[1 - me.c])
    g_mix = mixed
    for m in range(ROWS // MT):
        r = pl.ds(MT * m, MT)
        g_mix[r, :] = dot_nt(gb[r, :], w_out).astype(BF)
    gpks = (act, gpre, gb)

    def late(rows, c):
        return dot_tn(jnp.concatenate(rows, 0), jnp.concatenate([c * half_low[0], c * half_low[1]], 0))

    def attend_back(gpk, p, at, lane, i):
        r = rows_at(i, 256)
        own1 = iota((PAD, 1), 0) == i
        q, k, v, qc, kc, vc = heads(p, r)
        do, doc = g_mix[r, at : at + 128], g_mix[512:, at : at + 128]
        kcf, vcf, qcf, docf = kc.astype(F32), vc.astype(F32), qc.astype(F32), doc.astype(F32)
        dq_t, dk, dv, dqc, dkc, dvc, late_s, late_p = [], [], [], [], [], [], [], []
        for hh in range(2):
            u = (p * 2 + i) * 2 + hh
            doh, doch = do * half_low[hh], doc * half_low[hh]
            p1, p2 = probs[u, :256, :], probs[u, 256:, :]
            f1, f2 = p1.astype(F32), p2.astype(F32)
            d1, d2 = dot_nt(v, doh), dot_nt(vc, doh)
            delta = jnp.sum(f1 * d1, 0, keepdims=True) + jnp.sum(f2 * d2, 0, keepdims=True)
            s1, s2 = (f1 * (d1 - delta)).astype(BF), (f2 * (d2 - delta)).astype(BF)
            dq_t.append((dot_tn(k, s1) + dot_tn(kc, s2))[64 * hh : 64 * (hh + 1)])
            pc, pcc = pcs[u, :, :256], pcs[u, :, 256:257]
            dc = dot_nt(doch, v)
            dcc = jnp.sum(doch.astype(F32) * vcf, -1, keepdims=True)
            deltac = jnp.sum(pc * dc, -1, keepdims=True) + pcc * dcc
            scb = (pc * (dc - deltac)).astype(BF)
            scc = pcc * (dcc - deltac)
            dqc.append((fdot(scb, k) + scc * kcf) * SCORE_SCALE)
            dk.append(fdot(s1, q))
            late_s.append(scb)
            late_p.append(pc.astype(BF))
            dkc.append(fdot(s2, q) + scc * qcf)
            dv.append(fdot(p1, do))
            dvc.append(fdot(p2, do) + pcc * docf)
        gpk[r, lane : lane + 128] = (jnp.transpose(jnp.concatenate(dq_t, 0)) * SCORE_SCALE).astype(BF)
        gpk[r, lane + 128 : lane + 256] = (join(*dk) + late(late_s, qc)).astype(BF)
        gpk[r, lane + 256 : lane + 384] = (join(*dv) + late(late_p, doc)).astype(BF)
        for s, value in enumerate((dqc, dkc, dvc)):
            lanes = slice(lane + 128 * s, lane + 128 * (s + 1))
            keep = gpk[512:, lanes].astype(F32)
            gpk[512:, lanes] = jnp.where(own1, join(*value), keep).astype(BF)

    b_last = []

    def b_deal():
        b_sent.wait()
        bland[me.x * 4 + me.z] = bupg[2 * me.x + me.z // 2]
        total = bland[0]
        for i in range(1, 16):
            total = total + bland[i]
        bsum[...] = total
        place = bfinal.at[me.slot]
        b_last.append(me.local(bsum, place))
        b_last.append(me.send_many([(bsum, place, me.at(dy=dy, flip=flip)) for dy, flip in me.near()], bfinal.at[pl.ds(0, 7)]))

    back_steps = {
        (0, 0): lambda: (sc.across(DOWN[0]), sc.across(DOWN[1]), sc.pair(OUT), sc.pass_on(B_UP[1])),
        (0, 1): lambda: (sc.start(0, gi[0].at[1 - me.c]), sc.across(B_UP[0])),
        (1, 0): lambda: (sc.pair(0), sc.deal(DOWN[0]), sc.deal(DOWN[1]), b_deal()),
        (1, 1): lambda: (sc.start(1, gi[1].at[1 - me.c]), sc.pass_on(OUT), sc.across(B_UP[1])),
        (2, 0): lambda: (sc.pair(1), sc.pass_on(0), sc.deal(B_UP[0])),
        (2, 1): lambda: (sc.start(2, gi[2].at[1 - me.c]),),
    }
    vtab[...] = jnp.zeros_like(vtab)
    for t in range(3):
        for h in range(2):
            p = 2 * t + h
            at = 384 * h + 128 * t
            lane = 384 * h
            gpk = gpks[t]
            gpk[512:, lane : lane + 384] = jnp.zeros((PAD, 384), BF)

            def one(i, carry, gpk=gpk, p=p, at=at, lane=lane):
                attend_back(gpk, p, at, lane, i)
                return carry

            lax.fori_loop(0, 2, one, 0, unroll=True)
            piece = gpk[:, lane : lane + 384]
            gi[t][h] = outer(attn[...], piece).astype(BF).reshape(4, 4, 48, 384)
            total = jnp.sum(piece.astype(F32), 0, keepdims=True)
            vtab[B_Q : B_Q + 1, at : at + 128] = total[:, :128]
            vtab[B_V : B_V + 1, at : at + 128] = total[:, 256:]
            back_steps[t, h]()

    def back_norm(t):
        for m in range(ROWS // MT):
            r = pl.ds(MT * m, MT)
            back = dot_nt(gpks[t][r, :384], in_v[t][0, :, :, :, :384].reshape(D, 384))
            back = back + dot_nt(gpks[t][r, 384:], in_v[t][1, :, :, :, :384].reshape(D, 384))
            gnorm[r, :] = back if t == 0 else gnorm[r, :] + back


    gp = hi

    def last_norm(i, carry):
        r = rows_at(i, TILE)
        nm, inv = centre(hidden[r, :])
        gn = gnorm[r, :]
        sums[GAIN_A] += fold(gn * nm)
        sums[SHIFT_A] += fold(gn)
        gh = acc[r, :] + norm_back(gn * row(GAIN_A), nm, inv)
        masked = masks[r, :1] > 0.5
        sums[TOKEN] += fold(jnp.where(masked, gh, 0.0))
        gp[r, :] = jnp.where(masked, 0.0, gh).astype(BF)
        return carry

    back_norm(0)
    sc.pair(2)
    sc.pass_on(1)
    back_norm(1)
    sc.across(OUT)
    back_norm(2)
    sc.across(0)
    sc.deal(B_UP[1])
    lax.fori_loop(0, ROWS // TILE, last_norm, 0)
    for i in (TOKEN, GAIN_A, SHIFT_A, B_OUT, SCALE_A, GAIN_H, SHIFT_H, B_DOWN, SCALE_H):
        vtab[i : i + 1, :] = jnp.sum(sums[i], 0, keepdims=True)
    gvec[...] = jnp.transpose(vtab[...]).astype(BF).reshape(4, 4, 48, 128)
    sc.pair(VEC, waits=False)
    home(gp, o_gp, gcls_l)
    sc.across(1)
    sc.deal(OUT)
    sc.deal(0)
    sc.deal(2)
    sc.deal(VEC)
    sc.deal(1)
    for k in range(2):
        for half, total in enumerate(sc.finish(B_UP[k])):
            o_up[:, 1536 * half + 768 * k : 1536 * half + 768 * (k + 1)] = total
    for col, width, g in ((0, 256, DOWN[0]), (256, 128, DOWN[1])):
        for half, total in enumerate(sc.finish(g)):
            o_down[:, 384 * half + col : 384 * half + col + width] = total
    for half, total in enumerate(sc.finish(OUT)):
        o_out[:, 384 * half : 384 * (half + 1)] = total
    wait_all(b_last)
    flat = bfinal[0]
    for i in range(1, 8):
        flat = flat + bfinal[i]
    chosen = jnp.where(iota((384, 128), 0) == iota((384, 128), 1) + me.lane, 1.0, 0.0)
    line = lax.dot_general(
        jnp.broadcast_to(flat, (8, 384)), chosen, (((1,), (0,)), ((), ())), precision=lax.Precision.HIGHEST, preferred_element_type=F32
    )

    def finish_in(t):
        for half, total in enumerate(sc.finish(t)):
            for s in range(3):
                at = D * s + 384 * half + 128 * t
                o_in[:, at : at + 128] = total[:, 128 * s : 128 * (s + 1)]

    finish_in(0)
    wait_all(shuffle)
    order = iota((8, D), 0)
    for landed, out in ((cls_l, o_cls), (gcls_l, o_gcls)):
        rows = jnp.zeros((8, D), F32)
        for y in range(4):
            two = landed[y].astype(F32)
            for i in range(2):
                rows = jnp.where(order == 2 * y + i, two[i : i + 1], rows)
        out[...] = rows.astype(BF)
    finish_in(2)
    finish_in(1)
    low, high = sc.finish(VEC)
    vtab[:, :128] = jnp.zeros((128, 128), F32)
    vtab[:6, :128] = low + high
    turned = jnp.transpose(vtab[:, :128])
    o_vec[...] = jnp.where(iota((16, 128), 0) == 11, line[:1], turned[:16])


def layer(patches, cots, cls, cot_cls, mask_index, w_in, w_o, w_u, w_d, b_up, vectors):
    vm = pl.BlockSpec(memory_space=pltpu.VMEM)
    hb = pl.BlockSpec(memory_space=pl.ANY)
    S, V = jax.ShapeDtypeStruct, pltpu.VMEM
    outs = [S((6, 3 * D), F32), S((6, D), F32), S((6, FF), F32), S((24, D), F32), S((8, D), BF), S((8, D), BF), S((16, 128), F32)]
    far = [S((8, 64, D), BF)] * 2
    far += [S(((4,) if mode == "quarter" else ()) + (2, 4, 4, 8 * rho, width), BF) for rho, width, _, mode in GROUPS[3:]]
    pack_width = [sum(GROUPS[g][1] for g in pack) for pack in PACKS]
    pack_rho = [GROUPS[pack[0]][0] for pack in PACKS]
    scratch = [V((2, 4, 4, 48, width), BF) for _, width, _, _ in GROUPS[:3]]
    scratch += [V((4, 4, 48, D), BF), V((2, 4, 4, 48, CHUNK), BF), V((2, 4, 192, D), BF)]
    wide_rows, low_rows = V((ROWS, D), F32), V((ROWS, D), BF)
    scratch += [low_rows, low_rows, wide_rows, low_rows, V((6, ROWS, 384), BF), V((24, KEYS, 256), BF), V((24, PAD, 384), F32)]
    scratch += [low_rows, wide_rows, low_rows, low_rows, wide_rows, wide_rows, low_rows, low_rows, V((ROWS, 128), F32)]
    scratch += [V((16, D), F32), V((128, D), F32), V((4, 1, CHUNK), F32), V((8, 1, 384), F32), V((16, 1, 384), F32)]
    scratch += [V((1, 384), F32), V((8, 1, 384), F32), V((16, 8, D), F32), V((4, PAD, D), BF), V((4, PAD, D), BF)]
    quarter = [GROUPS[pack[0]][3] == "quarter" for pack in PACKS]
    scratch += [V((2, 4, r, w) if q else (2, r, w), BF) for r, w, q in zip(pack_rho, pack_width, quarter)]
    scratch += [V((8, r, w), BF) for r, w in zip(pack_rho, pack_width)]
    scratch += [V((8 * r, w), F32) for r, w in zip(pack_rho, pack_width)]
    scratch += [V((8 * rho, width), BF) for rho, width, _, _ in GROUPS]
    scratch += [V((2, 4, 4, 48, 384), BF)] * 4 + [V((4, 4, 48, 128), BF)]
    scratch += [V((4, 4, 48, CHUNK), BF), V((4, 192, 256), BF), V((4, 192, 128), BF)]
    blocks = [(8 * rho, width) for rho, width, _, _ in BACK]
    scratch += [V((4, 4) + blocks[g], BF) for g in (4, 5, 6, 7)]
    scratch += [V((4, 4) + blocks[g], BF) for g in range(8)]
    scratch += [V((2, 2) + blocks[g], BF) for g in RING]
    scratch += [V((16 if BACK[g][3] == "wide" else 3,) + blocks[g], BF) for g in range(9)]
    scratch += [V((8, rho, width), BF) for rho, width, _, _ in BACK] * 2
    scratch += [V((192, D), F32), pltpu.SemaphoreType.DMA((POOL,))]
    return pl.pallas_call(
        layer_kernel,
        out_shape=outs + far,
        in_specs=[hb] * 2 + [vm] * 19,
        out_specs=[vm] * len(outs) + [hb] * len(far),
        scratch_shapes=scratch,
        compiler_params=pltpu.CompilerParams(collective_id=0, has_side_effects=True, vmem_limit_bytes=63 * 2**20),
        name="layer",
    )(patches, cots, cls, cot_cls, mask_index, w_in, w_o, w_u, w_d, b_up, *vectors)[:9]


def finish_kernel(i_in, i_out, i_up, i_down, i_cls, i_gcls, i_vec, i_res, i_gp, *outs):
    for src, dst in zip((i_in, i_out, i_up, i_down, i_cls, i_gcls, i_res, i_gp), outs):
        dst[...] = src[...]
    for i in range(11):
        outs[8 + i][...] = i_vec[i : i + 1, :6]
    outs[19][...] = i_vec[11:12, :24]


def finish(parts):
    vm = pl.BlockSpec(memory_space=pltpu.VMEM)
    S = jax.ShapeDtypeStruct
    outs = [S(p.shape, p.dtype) for p in parts[:6]] + [S((8, 64, D), BF)] * 2 + [S((1, 6), F32)] * 11 + [S((1, 24), F32)]
    return pl.pallas_call(
        finish_kernel,
        out_shape=outs,
        in_specs=[vm] * 9,
        out_specs=[vm] * 20,
        name="finish",
    )(*parts)


def on_device(
    patches,
    cls_tokens,
    mask_index,
    mask_token,
    attention_gain,
    attention_shift,
    input_weight,
    query_bias,
    value_bias,
    output_weight,
    output_bias,
    attention_scale,
    hidden_gain,
    hidden_shift,
    expand_weight,
    expand_bias,
    reduce_weight,
    reduce_bias,
    hidden_scale,
    cotangent_patches,
    cotangent_cls,
):
    vectors = [mask_token, attention_gain, attention_shift, query_bias, value_bias, output_bias, attention_scale]
    vectors += [hidden_gain, hidden_shift, reduce_bias, hidden_scale]
    parts = layer(
        patches,
        cotangent_patches,
        cls_tokens,
        cotangent_cls,
        mask_index,
        input_weight,
        output_weight,
        expand_weight,
        reduce_weight,
        expand_bias.reshape(1, 24),
        [v.reshape(1, 6) for v in vectors],
    )
    g_in, g_o, g_u, g_d, o_cls, o_gcls, o_res, o_gp, *v = finish(parts)
    g_bup = v[11].reshape(24)
    v = [t.reshape(6) for t in v[:11]]
    return (
        o_res,
        o_cls,
        o_gp,
        o_gcls,
        v[TOKEN],
        v[GAIN_A],
        v[SHIFT_A],
        g_in,
        v[B_Q],
        v[B_V],
        g_o,
        v[B_OUT],
        v[SCALE_A],
        v[GAIN_H],
        v[SHIFT_H],
        g_u,
        g_bup,
        g_d,
        v[B_DOWN],
        v[SCALE_H],
    )


def solution(mesh):
    vector = P(("img", "row"))
    matrix = P(("img", "row"), None)
    image = P("img", "row", None)
    head = P("img", None)
    in_specs = (image, head, head, vector, vector, vector, matrix, vector, vector, matrix, vector, vector, vector, vector)
    in_specs += (matrix, vector, matrix, vector, vector, image, head)
    out_specs = (image, head, image, head, vector, vector, vector, matrix, vector, vector, matrix, vector, vector)
    out_specs += (vector, vector, matrix, vector, matrix, vector, vector)
    return jax.shard_map(on_device, mesh=mesh, in_specs=in_specs, out_specs=out_specs, check_vma=False)
```

```python
import jax
import jax.numpy as jnp
from jax import lax
from jax.experimental import pallas as pl
from jax.experimental.pallas import tpu as pltpu
from jax.sharding import PartitionSpec as P

D = 768
FF = 3072
EPSILON = 1e-06
SCORE_SCALE = 0.125
MESH = pl.DeviceIdType.MESH
BF = jnp.bfloat16
F32 = jnp.float32
ROWS = 528
KEYS = 272
PAD = 16
TILE = 176
HALVES = ((0, 272), (272, 256))
CHUNK = 768
POOL = 266

TOKEN, GAIN_A, SHIFT_A, B_Q, B_V, B_OUT, SCALE_A, GAIN_H, SHIFT_H, B_DOWN, SCALE_H = range(11)

OUT, UP, DOWN = 3, 4, (5, 6)
GROUPS = (
    (6, 512, "xz", "two"),
    (6, 384, "zx", "two"),
    (6, 384, "zx", "two"),
    (6, 384, "xz", "ring"),
    (6, 384, "xz", "quarter"),
    (24, 256, "zx", "ring"),
    (24, 128, "xz", "ring"),
)
PACKS = ((0,), (1, 2), (4,), (5, 6), (3,))
B_UP, VEC = (4, 7), 8
BACK = (
    (6, 384, "xz", "ring"),
    (6, 384, "zx", "ring"),
    (6, 384, "xz", "wide"),
    (6, 384, "zx", "ring"),
    (6, 768, "xz", "ring"),
    (24, 256, "zx", "ring"),
    (24, 128, "xz", "ring"),
    (6, 768, "zx", "ring"),
    (6, 128, "xz", "wide"),
)
RING = tuple(g for g in range(len(BACK)) if BACK[g][3] == "ring")


def fdot(a, b):
    return jnp.dot(a, b, preferred_element_type=F32)


def dot_nt(a, b):
    return lax.dot_general(a, b, (((1,), (1,)), ((), ())), preferred_element_type=F32)


def dot_tn(a, b):
    return lax.dot_general(a, b, (((0,), (0,)), ((), ())), preferred_element_type=F32)


def outer(a, b):
    column = jnp.transpose(a[512:528].astype(F32))
    row = b[512:528].astype(F32)
    return dot_tn(a[:512], b[:512]) + column[:, 0:1] * row[0:1] + column[:, 1:2] * row[1:2]


def fold(v):
    return jnp.sum(v.reshape(-1, 8, v.shape[-1]), 0)


def iota(shape, dim):
    return lax.broadcasted_iota(jnp.int32, shape, dim)


def rows_at(i, size):
    return pl.ds(pl.multiple_of(i * size, size), size)


def centre(x):
    cen = x - jnp.mean(x, -1, keepdims=True)
    inv = lax.rsqrt(jnp.mean(cen * cen, -1, keepdims=True) + EPSILON)
    return cen * inv, inv


def norm_back(q, nm, inv):
    return inv * (q - jnp.mean(q, -1, keepdims=True) - nm * jnp.mean(q * nm, -1, keepdims=True))


class Many:
    def __init__(self, send_sem, recv_sem, total):
        self.send_sem, self.recv_sem, self.total = send_sem, recv_sem, total

    def wait_send(self):
        pltpu.make_async_copy(self.total, self.total, self.send_sem).wait()

    def wait_recv(self):
        pltpu.make_async_copy(self.total, self.total, self.recv_sem).wait()

    def wait(self):
        self.wait_send()
        self.wait_recv()


class Place:
    def __init__(self, pool):
        img = lax.axis_index("img")
        self.y = lax.axis_index("row")
        self.x = img // 8
        self.z = (img // 2) % 4
        self.c = img % 2
        self.slot = self.c * 4 + self.y
        self.lane = 192 * (self.z % 2) + 24 * self.slot
        self.pool, self.used = pool, 0

    def sem(self):
        self.used += 1
        assert self.used <= POOL
        return self.pool.at[self.used - 1]

    def at(self, dx=0, dz=0, dy=0, flip=0):
        x = (self.x + dx) % 4
        z = (self.z + dz) % 4
        y = (self.y + dy) % 4
        c = 1 - self.c if flip else self.c
        return ((x * 4 + z) * 2 + c, y)

    def near(self):
        return [(dy, flip) for flip in (0, 1) for dy in range(4) if (dy, flip) != (0, 0)]

    def plane(self):
        return [(dx, dz) for dx in range(4) for dz in range(4) if (dx, dz) != (0, 0)]

    def signal(self):
        barrier = pltpu.get_barrier_semaphore()
        for dy, flip in self.near():
            pl.semaphore_signal(barrier, inc=1, device_id=self.at(dy=dy, flip=flip), device_id_type=MESH)
        for dx, dz in self.plane():
            pl.semaphore_signal(barrier, inc=1, device_id=self.at(dx=dx, dz=dz), device_id_type=MESH)

    def await_all(self):
        pl.semaphore_wait(pltpu.get_barrier_semaphore(), 22)

    def send(self, src, dst, device):
        copy = pltpu.make_async_remote_copy(
            src_ref=src, dst_ref=dst, send_sem=self.sem(), recv_sem=self.sem(), device_id=device, device_id_type=MESH
        )
        copy.start()
        return copy

    def send_many(self, copies, total):
        many = Many(self.sem(), self.sem(), total)
        for src, dst, device in copies:
            pltpu.make_async_remote_copy(
                src_ref=src, dst_ref=dst, send_sem=many.send_sem, recv_sem=many.recv_sem, device_id=device, device_id_type=MESH
            ).start()
        return many

    def local(self, src, dst, sem=None):
        copy = pltpu.make_async_copy(src, dst, self.sem() if sem is None else sem)
        copy.start()
        return copy


def lane_of_rows(order, ref, second, lo=0, size=4):
    return ref.at[pl.ds(lo, size), second] if order == "xz" else ref.at[second, pl.ds(lo, size)]


def wait_all(copies):
    for copy in copies:
        copy.wait()


class Gather:
    def __init__(self, me, packs, got, wide, stage, whole):
        self.me, self.packs, self.got, self.wide, self.stage, self.whole = me, packs, got, wide, stage, whole
        self.one, self.two, self.three, self.five, self.four = {}, {}, {}, {}, {}

    def first(self, i):
        me, quarter = self.me, GROUPS[PACKS[i][0]][3] == "quarter"
        place = self.got[i].at[me.slot]

        def part(half, y):
            return self.packs[i].at[half, y] if quarter else self.packs[i].at[half]

        row = []
        for dy, flip in me.near():
            half = 1 - me.c if flip else me.c
            row.append((part(half, (me.y + dy) % 4), place, me.at(dy=dy, flip=flip)))
        self.one[i] = [me.local(part(me.c, me.y), place), me.send_many(row, self.got[i].at[pl.ds(0, 7)])]

    def assemble(self, i):
        rho = GROUPS[PACKS[i][0]][0]
        wait_all(self.one[i])
        for d in range(8):
            self.wide[i][d * rho : (d + 1) * rho, :] = self.got[i][d].astype(F32)
        col = 0
        for g in PACKS[i]:
            width = GROUPS[g][1]
            self.stage[g][...] = self.wide[i][:, col : col + width].astype(BF)
            col += width

    def mine(self, g):
        me = self.me
        return self.whole[g].at[me.y, me.c] if GROUPS[g][3] == "quarter" else self.whole[g].at[me.c]

    def second(self, g):
        me, order, mine = self.me, GROUPS[g][2], self.mine(g)
        place = mine.at[me.x, me.z]
        row = [(self.stage[g], place, me.at(dx=k) if order == "xz" else me.at(dz=k)) for k in (1, 3, 2)]
        self.two[g] = [me.local(self.stage[g], place), me.send_many(row, mine.at[0, pl.ds(0, 3)])]

    def on_axis(self, g):
        me = self.me
        if GROUPS[g][2] == "xz":
            return me.z, lambda k: me.at(dz=k)
        return me.x, lambda k: me.at(dx=k)

    def third(self, g):
        wait_all(self.two[g])
        at, device = self.on_axis(g)
        mine = self.mine(g)
        part = lane_of_rows(GROUPS[g][2], mine, at)
        if GROUPS[g][3] == "ring":
            self.three[g] = [self.me.send(part, part, device(k)) for k in (1, 3)]
        else:
            self.three[g] = [self.me.send_many([(part, part, device(k)) for k in (1, 3, 2)], mine.at[pl.ds(0, 3)])]

    def relay(self, g):
        at, device = self.on_axis(g)
        self.five[g] = []
        for j, k in enumerate((1, 3)):
            self.three[g][j].wait_recv()
            part = lane_of_rows(GROUPS[g][2], self.mine(g), (at + 4 - k) % 4, 2 * j, 2)
            self.five[g].append(self.me.send(part, part, device(k)))

    def fifth(self, g):
        wait_all(self.three[g])
        me, mine = self.me, self.mine(g)
        self.six = [me.send(mine, mine, me.at(dy=k)) for k in (1, 3)]
        self.four[g] = [me.send(mine, mine, me.at(flip=1))]

    def sixth(self, g):
        me = self.me
        self.seven = []
        for j, k in enumerate((1, 3)):
            self.six[j].wait_recv()
            quarter = self.whole[g].at[(me.y + 4 - k) % 4, me.c]
            half = quarter.at[pl.ds(2 * j, 2)]
            self.seven.append(me.send(half, half, me.at(dy=k)))
            self.four[g].append(me.send(quarter, quarter, me.at(flip=1)))

    def fourth(self, g):
        me = self.me
        if GROUPS[g][3] == "quarter":
            wait_all(self.seven)
            for copy in self.six:
                copy.wait_send()
            quarter = self.whole[g].at[(me.y + 2) % 4, me.c]
            self.four[g].append(me.send(quarter, quarter, me.at(flip=1)))
            return
        if GROUPS[g][3] == "ring":
            for copy in self.three[g]:
                copy.wait_send()
            wait_all(self.five[g])
        else:
            wait_all(self.three[g])
        self.four[g] = [me.send(self.mine(g), self.mine(g), me.at(flip=1))]

    def done(self, g):
        wait_all(self.four[g])


class Scatter:
    def __init__(self, me, held, sib, far, land, wide, cut, final):
        self.me, self.held, self.sib, self.far, self.land = me, held, sib, far, land
        self.wide, self.cut, self.final = wide, cut, final
        self.zero, self.open, self.a, self.b, self.two, self.three = {}, {}, {}, {}, {}, {}

    def on_axis(self, g):
        me = self.me
        if BACK[g][2] == "xz":
            return me.z, lambda k: me.at(dz=k)
        return me.x, lambda k: me.at(dx=k)

    def piece(self, g, first, second):
        return (first, second) if BACK[g][2] == "xz" else (second, first)

    def start(self, g, src, dst=None):
        copy = self.me.send(src, self.sib[g] if dst is None else dst, self.me.at(flip=1))
        self.zero.setdefault(g, []).append(copy)
        self.open.setdefault(g, []).append(copy)
        return copy

    def drain(self, g):
        for copy in self.open.pop(g, []):
            copy.wait_send()

    def pair(self, g, waits=True):
        me = self.me
        if waits:
            for copy in self.zero[g]:
                copy.wait_recv()
            held, sib = self.held[g], self.sib[g]

            def add(i, carry):
                a, b = i // 4, i % 4
                held[a, b] = (held[a, b].astype(F32) + sib[a, b].astype(F32)).astype(BF)
                return carry

            lax.fori_loop(0, 16, add, 0)
        if BACK[g][3] == "wide":
            row = []
            for dx, dz in me.plane():
                x, z = (me.x + dx) % 4, (me.z + dz) % 4
                row.append((self.held[g].at[x, z], self.land[g].at[me.x * 4 + me.z], me.at(dx=dx, dz=dz)))
            self.two[g] = me.send_many(row, self.land[g].at[pl.ds(0, 15)])
            return
        at, device = self.on_axis(g)
        far = (at + 2) % 4
        self.a[g] = [
            me.send(lane_of_rows(BACK[g][2], self.held[g], far, 2 * j, 2), self.far[g].at[j], device(k)) for j, k in enumerate((1, 3))
        ]

    def pass_on(self, g):
        at, device = self.on_axis(g)
        for copy in self.a[g]:
            copy.wait_recv()
        row = []
        for j, k in enumerate((1, 3)):
            near = (at + k) % 4

            def add(i, carry, j=j, near=near):
                p = self.piece(g, 2 * j + i, near)
                self.held[g][p] = (self.held[g][p].astype(F32) + self.far[g][j, i].astype(F32)).astype(BF)
                return carry

            lax.fori_loop(0, 2, add, 0)
            row.append(self.me.send(lane_of_rows(BACK[g][2], self.held[g], near), self.sib[g].at[j], device(k)))
        self.b[g] = row

    def across(self, g):
        wait_all(self.b[g])
        for copy in self.a[g]:
            copy.wait_send()
        me = self.me
        at, _ = self.on_axis(g)
        held, sib = self.held[g], self.sib[g]

        def add(i, carry):
            p = self.piece(g, i, at)
            held[p] = (held[p].astype(F32) + sib[0, i].astype(F32) + sib[1, i].astype(F32)).astype(BF)
            return carry

        lax.fori_loop(0, 4, add, 0)
        row = []
        for k in (1, 3, 2):
            if BACK[g][2] == "xz":
                src, device = held.at[(me.x + k) % 4, me.z], me.at(dx=k)
            else:
                src, device = held.at[me.x, (me.z + k) % 4], me.at(dz=k)
            row.append((src, self.land[g].at[k - 1], device))
        self.two[g] = me.send_many(row, self.land[g].at[pl.ds(0, 3)])

    def deal(self, g):
        me = self.me
        self.two[g].wait()
        rho, width = BACK[g][:2]
        size = 8 * rho
        own = self.held[g][me.x, me.z].astype(F32)
        land = self.land[g]
        if BACK[g][3] == "wide":
            land[me.x * 4 + me.z] = self.held[g][me.x, me.z]
            total = land[0].astype(F32)
            for i in range(1, 16):
                total = total + land[i].astype(F32)
        else:
            total = own + land[0].astype(F32) + land[1].astype(F32) + land[2].astype(F32)
        self.wide[:size, :width] = total
        for d in range(8):
            self.cut[g][d] = self.wide[d * rho : (d + 1) * rho, :width].astype(BF)
        place = self.final[g].at[me.slot]
        row = []
        for dy, flip in me.near():
            core = 1 - me.c if flip else me.c
            peer = core * 4 + (me.y + dy) % 4
            row.append((self.cut[g].at[peer], place, me.at(dy=dy, flip=flip)))
        self.three[g] = [me.local(self.cut[g].at[me.slot], place), me.send_many(row, self.final[g].at[pl.ds(0, 7)])]

    def finish(self, g):
        wait_all(self.three[g])
        self.drain(g)
        totals = []
        for half in range(2):
            total = self.final[g][half * 4].astype(F32)
            for y in range(1, 4):
                total = total + self.final[g][half * 4 + y].astype(F32)
            totals.append(total)
        return totals


def take(refs, n):
    return refs[:n], refs[n:]


def layer_kernel(*refs):
    ng, nb, npk = len(GROUPS), len(BACK), len(PACKS)
    (patches, cots, cls, cot_cls, mask_index, w_in, w_o, w_u, w_d, b_up_in), refs = take(refs, 10)
    vectors, refs = take(refs, 11)
    (o_in, o_out, o_up, o_down, o_cls, o_gcls, o_vec, o_res, o_gp), refs = take(refs, 9)
    weights_far, refs = take(refs, ng - 3)
    in_v, refs = take(refs, 3)
    (wo, wu, wd), refs = take(refs, 3)
    (x_all, c_all, hidden, attn, qkv, probs, pcs, mixed, branch, hi, gb, acc, gnorm, act, gpre, masks), refs = take(refs, 16)
    (names, vtab, bupv, bupg, bland, bsum, bfinal, sums, cls_l, gcls_l), refs = take(refs, 10)
    packs, refs = take(refs, npk)
    got, refs = take(refs, npk)
    pack_wide, refs = take(refs, npk)
    stage, refs = take(refs, ng)
    gi, refs = take(refs, 3)
    (g_out, gvec, snd_up, snd_da, snd_db), refs = take(refs, 5)
    held_far, refs = take(refs, 4)
    sib, refs = take(refs, nb - 1)
    far, refs = take(refs, len(RING))
    land, refs = take(refs, nb)
    cut, refs = take(refs, nb)
    final, refs = take(refs, nb)
    wide, pool = refs
    me = Place(pool)
    me.signal()

    vtab[...] = jnp.zeros_like(vtab)
    for i, v in enumerate(vectors):
        vtab[i : i + 1, :6] = v[...].astype(F32)
    turned = jnp.transpose(vtab[:, :128])
    spread = iota((8, 384), 1) - me.lane
    line = jnp.zeros((8, 384), F32)
    b_row = b_up_in[...].astype(F32)
    for t in range(24):
        line = jnp.where(spread == t, b_row[:, t : t + 1], line)
    rows = jnp.zeros((8, 128), F32)
    for i in range(3):
        rows = jnp.where(iota((8, 128), 0) == i, line[:, 128 * i : 128 * (i + 1)], rows)
    for h in range(2):
        for t in range(3):
            dst, col = (packs[0], 0) if t == 0 else (packs[1], 384 * (t - 1))
            for part in range(3):
                at = D * part + 384 * h + 128 * t
                dst[h, :, col + 128 * part : col + 128 * (part + 1)] = w_in[:, at : at + 128]
        packs[0][h, :, 384:] = (turned[:6] if h == 0 else rows[:6]).astype(BF)
        for y in range(4):
            packs[2][h, y] = w_u[:, 1536 * h + 384 * y : 1536 * h + 384 * (y + 1)]
        packs[3][h] = w_d[:, 384 * h : 384 * (h + 1)]
        packs[4][h] = w_o[:, 384 * h : 384 * (h + 1)]
    me.await_all()
    whole = tuple(in_v) + tuple(weights_far)
    ga = Gather(me, packs, got, pack_wide, stage, whole)
    def bring(src, dst):
        own, row = [], []
        for image in range(2):
            lane = dst.at[pl.ds(pl.multiple_of(256 * image + 64 * me.y, 64), 64)]
            own.append(me.local(src.at[2 * me.y + image], lane))
            row += [(src.at[2 * ((me.y + k) % 4) + image], lane, me.at(dy=k)) for k in (1, 3, 2)]
        return own + [me.send_many(row, dst.at[pl.ds(0, 384)])]

    for i in (2, 0, 3, 4, 1):
        ga.first(i)
    for i in (2, 0, 3, 4, 1):
        ga.assemble(i)
        for g in PACKS[i]:
            ga.second(g)
    bring_x = bring(patches, x_all)
    pick = iota((8, D), 0)
    place16 = iota((PAD, D), 0)
    for src, dst in ((cls, x_all), (cot_cls, c_all)):
        wide8 = src[...].astype(F32)
        two = jnp.zeros((PAD, D), F32)
        for i in range(2):
            this = jnp.sum(jnp.where(pick == 2 * me.y + i, wide8, 0.0), 0, keepdims=True)
            two = jnp.where(place16 == i, this, two)
        dst[512:, :] = two.astype(BF)
    index0 = mask_index[pl.ds(2 * me.y, 1), :]
    index1 = mask_index[pl.ds(2 * me.y + 1, 1), :] + 256

    def mask_tile(i, carry):
        r = rows_at(i, TILE)
        at = iota((TILE, 154), 0) + TILE * i
        hit = jnp.where(at == index0, 1.0, 0.0) + jnp.where(at == index1, 1.0, 0.0)
        masks[r, :] = jnp.broadcast_to(jnp.max(hit, -1, keepdims=True), (TILE, 128))
        return carry

    lax.fori_loop(0, ROWS // TILE, mask_tile, 0)
    for g in (UP, 0, DOWN[0], DOWN[1], 1, 2, OUT):
        ga.third(g)
    ga.fifth(UP)
    ga.relay(DOWN[0])
    ga.relay(DOWN[1])
    ga.fourth(0)
    ga.sixth(UP)
    wait_all(bring_x)
    ga.done(0)
    names[...] = jnp.transpose(in_v[0][0, :, :, :, 384:].reshape(D, 128).astype(F32))[:16]
    which = iota((96, 128), 0) % 6
    for pair in range(8):
        a, b = pair // 2, 2 * (pair % 2)
        block = in_v[0][1, a, pl.ds(b, 2), :, 384:].reshape(96, 128).astype(F32)
        for i in range(3):
            at = 384 * (pair % 2) + 128 * i
            bupv[pair // 2, :, at : at + 128] = jnp.sum(jnp.where(which == i, block, 0.0), 0, keepdims=True)

    def row(i):
        return names[i : i + 1, :]

    def norm_tile(i, carry):
        r = rows_at(i, TILE)
        x = jnp.where(masks[r, :1] > 0.5, row(TOKEN), x_all[r, :].astype(F32))
        hidden[r, :] = x
        attn[r, :] = (centre(x)[0] * row(GAIN_A) + row(SHIFT_A)).astype(BF)
        return carry

    lax.fori_loop(0, ROWS // TILE, norm_tile, 0)
    ga.relay(OUT)
    ga.fourth(1)
    ga.fourth(2)
    bring_c = bring(cots, c_all)
    mixed[512:, :] = jnp.zeros((PAD, D), BF)

    def project(t):
        for h in range(2):
            p = 2 * t + h
            w = in_v[t][h, :, :, :, :384].reshape(D, 384)
            at = 384 * h + 128 * t
            bias_q, bias_v = names[B_Q : B_Q + 1, at : at + 128], names[B_V : B_V + 1, at : at + 128]
            for top_row, size in HALVES:
                r = pl.ds(top_row, size)
                out = fdot(attn[r, :], w)
                q = (out[:, :128] + bias_q).astype(BF).astype(F32) * SCORE_SCALE
                qkv[p, r, :128] = q.astype(BF)
                qkv[p, r, 128:256] = out[:, 128:256].astype(BF)
                qkv[p, r, 256:] = (out[:, 256:] + bias_v).astype(BF)

    lane_row = iota((1, 128), 1)
    half_low = [jnp.where(lane_row // 64 == hh, 1.0, 0.0).astype(BF) for hh in range(2)]

    def heads(p, r):
        patch = [qkv[p, r, 128 * s : 128 * (s + 1)] for s in range(3)]
        return patch + [qkv[p, 512:528, 128 * s : 128 * (s + 1)] for s in range(3)]

    def join(low, high):
        return jnp.where(lane_row < 64, low, high)

    def attend(p, at, i):
        r = rows_at(i, 256)
        own = iota((PAD, 256), 0) == i
        own1 = iota((PAD, 1), 0) == i
        q, k, v, qc, kc, vc = heads(p, r)
        kcf, vcf = kc.astype(F32), vc.astype(F32)
        turned_out, cls_out = [], []
        for hh in range(2):
            qh, qch = q * half_low[hh], qc * half_low[hh]
            s1 = dot_nt(k, qh)
            s2 = jnp.where(own, dot_nt(kc, qh), -1e30)
            top = jnp.maximum(jnp.max(s1, 0, keepdims=True), jnp.max(s2, 0, keepdims=True))
            e1, e2 = jnp.exp(s1 - top), jnp.exp(s2 - top)
            scale = 1.0 / (jnp.sum(e1, 0, keepdims=True) + jnp.sum(e2, 0, keepdims=True))
            p1, p2 = (e1 * scale).astype(BF), (e2 * scale).astype(BF)
            u = (p * 2 + i) * 2 + hh
            probs[u, :256, :] = p1
            probs[u, 256:, :] = p2
            turned_out.append((dot_tn(v, p1) + dot_tn(vc, p2))[64 * hh : 64 * (hh + 1)])
            sc = dot_nt(qch, k)
            scc = jnp.sum(qch.astype(F32) * kcf, -1, keepdims=True)
            topc = jnp.maximum(jnp.max(sc, -1, keepdims=True), scc)
            ec, ecc = jnp.exp(sc - topc), jnp.exp(scc - topc)
            total = jnp.sum(ec, -1, keepdims=True) + ecc
            pc = jnp.where(own, ec / total, 0.0)
            pcc = jnp.where(own1, ecc / total, 0.0)
            pcs[u, :, :256] = pc
            pcs[u, :, 256:] = jnp.broadcast_to(pcc, (PAD, 128))
            cls_out.append(fdot(pc.astype(BF), v) + pcc.astype(BF).astype(F32) * vcf)
        mixed[r, at : at + 128] = jnp.transpose(jnp.concatenate(turned_out, 0)).astype(BF)
        kept = mixed[512:, at : at + 128].astype(F32)
        mixed[512:, at : at + 128] = (kept + join(*cls_out)).astype(BF)

    loads, load_sems = {}, [[me.sem() for _ in range(6)] for _ in range(2)]

    def load_out():
        ga.done(OUT)
        loads["out"] = [me.local(whole[OUT].at[h], wo.at[:, :, :, pl.ds(384 * h, 384)]) for h in range(2)]

    def load_chunk(i):
        k, s = i // 2 % 2, i % 2
        h = me.c if s == 1 else 1 - me.c
        n = 2 * h + k
        sems = load_sems[i % 2]
        row = [me.local(whole[UP].at[2 * k + j, h], wu.at[i % 2, :, :, :, pl.ds(384 * j, 384)], sems[j]) for j in range(2)]
        for half in range(2):
            row.append(me.local(whole[DOWN[0]].at[half, n], wd.at[i % 2, :, :, pl.ds(384 * half, 256)], sems[2 + 2 * half]))
            row.append(me.local(whole[DOWN[1]].at[half, n], wd.at[i % 2, :, :, pl.ds(384 * half + 256, 128)], sems[3 + 2 * half]))
        loads[i] = row

    steps = {
        (0, 0): lambda: (ga.fourth(DOWN[0]), ga.fourth(DOWN[1])),
        (0, 1): lambda: (ga.done(1), ga.fourth(OUT)),
        (1, 0): lambda: ga.fourth(UP),
        (1, 1): lambda: ga.done(2),
        (2, 0): lambda: load_out(),
        (2, 1): lambda: (ga.done(UP), ga.done(DOWN[0]), ga.done(DOWN[1]), load_chunk(0), load_chunk(1)),
    }
    for t in range(3):
        project(t)
        for h in range(2):
            p = 2 * t + h
            at = 384 * h + 128 * t

            def one(i, carry, p=p, at=at):
                attend(p, at, i)
                return carry

            lax.fori_loop(0, 2, one, 0, unroll=True)
            steps[t, h]()

    wait_all(bring_c)
    wait_all(loads["out"])
    sums[...] = jnp.zeros_like(sums)
    w_out = wo[...].reshape(D, D)
    for top_row, size in HALVES:
        r = pl.ds(top_row, size)
        branch[r, :] = fdot(mixed[r, :], w_out) + row(B_OUT)

    def pre_norm(i, carry):
        r = rows_at(i, TILE)
        nm, _ = centre(hidden[r, :] + row(SCALE_A) * branch[r, :])
        hi[r, :] = (nm * row(GAIN_H) + row(SHIFT_H)).astype(BF)
        g = (row(SCALE_H) * c_all[r, :].astype(F32)).astype(BF)
        gb[r, :] = g
        sums[B_DOWN] += fold(g.astype(F32))
        acc[r, :] = jnp.zeros((TILE, D), F32)
        gnorm[r, :] = jnp.zeros((TILE, D), F32)
        return carry

    lax.fori_loop(0, ROWS // TILE, pre_norm, 0)
    held = [gi[t].at[me.c] for t in range(3)]
    held += [g_out.at[me.c], held_far[0], held_far[1], held_far[2], held_far[3], gvec]
    sibs = list(sib) + [None]
    fars = dict(zip(RING, far))
    sc = Scatter(me, held, sibs, fars, land, wide, cut, final)

    slopes = (gi[0], gi[1], gi[2], g_out)

    def slope_rows(top_row, size):
        for piece in range(top_row // 48, (top_row + size) // 48 + 1):
            low, high = max(top_row, 48 * piece), min(top_row + size, 48 * (piece + 1))
            if low < high:
                for half in range(2):
                    place = (half, piece // 4, piece % 4, slice(low - 48 * piece, high - 48 * piece))
                    yield place, slice(low - top_row, high - top_row), slice(384 * half, 384 * (half + 1))

    def chunk_forward(i):
        k, s = i // 2, i % 2
        n = 2 * (me.c if s == 1 else 1 - me.c) + k
        wait_all(loads[i])
        up, down = wu[i % 2].reshape(D, CHUNK), wd[i % 2].reshape(CHUNK, D)
        bias = bupv[n]
        for top_row, size in HALVES:
            r = pl.ds(top_row, size)
            pre = fdot(hi[r, :], up) + bias
            cdf = 0.5 * (1.0 + lax.erf(pre * 0.7071067811865476))
            a = (pre * cdf).astype(BF)
            slope = (cdf + pre * (jnp.exp(-0.5 * pre * pre) * 0.3989422804014327)).astype(BF)
            for place, rows, lanes in slope_rows(top_row, size):
                slopes[i][place] = slope[rows, lanes]
            act[r, :] = a
            acc[r, :] += fdot(a, down)
        grad_down = outer(act[...], gb[...])
        first = me.c == 0
        own = jnp.where(first, grad_down[:, :384], grad_down[:, 384:]).astype(BF)
        other = jnp.where(first, grad_down[:, 384:], grad_down[:, :384]).astype(BF)
        held_far[1][n] = own[:, :256].reshape(4, 192, 256)
        held_far[2][n] = own[:, 256:].reshape(4, 192, 128)
        sc.drain(DOWN[0])
        sc.drain(DOWN[1])
        snd_da[...] = other[:, :256].reshape(4, 192, 256)
        snd_db[...] = other[:, 256:].reshape(4, 192, 128)
        sc.start(DOWN[0], snd_da, sib[DOWN[0]].at[n])
        sc.start(DOWN[1], snd_db, sib[DOWN[1]].at[n])

    def chunk_backward(i):
        k, s = i // 2, i % 2
        n = 2 * (me.c if s == 1 else 1 - me.c) + k
        wait_all(loads[4 + i])
        up, down = wu[i % 2].reshape(D, CHUNK), wd[i % 2].reshape(CHUNK, D)
        for top_row, size in HALVES:
            r = pl.ds(top_row, size)
            back = dot_nt(gb[r, :], down)
            for place, rows, lanes in slope_rows(top_row, size):
                here = slice(top_row + rows.start, top_row + rows.stop)
                gpre[here, lanes] = (slopes[i][place].astype(F32) * back[rows, lanes]).astype(BF)
            gnorm[r, :] += dot_nt(gpre[r, :], up)
        g = gpre[...]
        total = jnp.sum(g.astype(F32), 0, keepdims=True)
        bupg[2 * n] = total[:, :384]
        bupg[2 * n + 1] = total[:, 384:]
        grad_up = outer(hi[...], g).astype(BF).reshape(4, 4, 48, CHUNK)
        if s == 0:
            sc.drain(B_UP[0])
            snd_up[...] = grad_up
            sc.start(B_UP[k], snd_up)
        else:
            held_far[0 if k == 0 else 3][...] = grad_up

    for i in range(4):
        chunk_forward(i)
        load_chunk(i + 2)
    chunk_backward(0)
    load_chunk(6)
    sc.pair(DOWN[0])
    sc.pair(DOWN[1])
    chunk_backward(1)
    load_chunk(7)
    chunk_backward(2)
    sc.pair(B_UP[0])
    sc.pass_on(DOWN[0])
    sc.pass_on(DOWN[1])
    chunk_backward(3)
    sc.pair(B_UP[1])
    b_row = []
    for dx, dz in me.plane():
        x, z = (me.x + dx) % 4, (me.z + dz) % 4
        b_row.append((bupg.at[2 * x + z // 2], bland.at[me.x * 4 + me.z], me.at(dx=dx, dz=dz)))
    b_sent = me.send_many(b_row, bland.at[pl.ds(0, 15)])
    res = x_all

    def post_norm(i, carry):
        r = rows_at(i, TILE)
        bh = acc[r, :] + row(B_DOWN)
        go = c_all[r, :].astype(F32)
        br = branch[r, :]
        mid = hidden[r, :] + row(SCALE_A) * br
        nm, inv = centre(mid)
        res[r, :] = (mid + row(SCALE_H) * bh).astype(BF)
        sums[SCALE_H] += fold(go * bh)
        gn = gnorm[r, :]
        sums[GAIN_H] += fold(gn * nm)
        sums[SHIFT_H] += fold(gn)
        gm = go + norm_back(gn * row(GAIN_H), nm, inv)
        acc[r, :] = gm
        sums[SCALE_A] += fold(gm * br)
        g = (row(SCALE_A) * gm).astype(BF)
        gb[r, :] = g
        sums[B_OUT] += fold(g.astype(F32))
        return carry

    lax.fori_loop(0, ROWS // TILE, post_norm, 0)
    shuffle = []

    def home(source, dst, last):
        row = []
        for image in range(2):
            lane = dst.at[2 * me.y + image]
            shuffle.append(me.local(source.at[pl.ds(pl.multiple_of(256 * image + 64 * me.y, 64), 64)], lane))
            for k in (1, 3, 2):
                peer = pl.multiple_of(256 * image + 64 * ((me.y + k) % 4), 64)
                row.append((source.at[pl.ds(peer, 64)], lane, me.at(dy=k)))
        shuffle.append(me.send_many(row, dst.at[pl.ds(0, 6)]))
        block, place = source.at[pl.ds(512, PAD)], last.at[me.y]
        shuffle.append(me.local(block, place))
        shuffle.append(me.send_many([(block, place, me.at(dy=k)) for k in (1, 3, 2)], last.at[pl.ds(0, 3)]))

    home(res, o_res, cls_l)
    sc.pass_on(B_UP[0])
    grad = outer(mixed[...], gb[...]).astype(BF)
    for h in range(2):
        g_out[h] = grad[:, 384 * h : 384 * (h + 1)].reshape(4, 4, 48, 384)
    sc.start(OUT, g_out.at[1 - me.c])
    g_mix = mixed
    for top_row, size in HALVES:
        r = pl.ds(top_row, size)
        g_mix[r, :] = dot_nt(gb[r, :], w_out).astype(BF)
    gpks = (act, gpre, gb)

    def late(rows, c):
        return dot_tn(jnp.concatenate(rows, 0), jnp.concatenate([c * half_low[0], c * half_low[1]], 0))

    def attend_back(gpk, p, at, lane, i):
        r = rows_at(i, 256)
        own1 = iota((PAD, 1), 0) == i
        q, k, v, qc, kc, vc = heads(p, r)
        do, doc = g_mix[r, at : at + 128], g_mix[512:, at : at + 128]
        kcf, vcf, qcf, docf = kc.astype(F32), vc.astype(F32), qc.astype(F32), doc.astype(F32)
        dq_t, dk, dv, dqc, dkc, dvc, late_s, late_p = [], [], [], [], [], [], [], []
        for hh in range(2):
            u = (p * 2 + i) * 2 + hh
            doh, doch = do * half_low[hh], doc * half_low[hh]
            p1, p2 = probs[u, :256, :], probs[u, 256:, :]
            f1, f2 = p1.astype(F32), p2.astype(F32)
            d1, d2 = dot_nt(v, doh), dot_nt(vc, doh)
            delta = jnp.sum(f1 * d1, 0, keepdims=True) + jnp.sum(f2 * d2, 0, keepdims=True)
            s1, s2 = (f1 * (d1 - delta)).astype(BF), (f2 * (d2 - delta)).astype(BF)
            dq_t.append((dot_tn(k, s1) + dot_tn(kc, s2))[64 * hh : 64 * (hh + 1)])
            pc, pcc = pcs[u, :, :256], pcs[u, :, 256:257]
            dc = dot_nt(doch, v)
            dcc = jnp.sum(doch.astype(F32) * vcf, -1, keepdims=True)
            deltac = jnp.sum(pc * dc, -1, keepdims=True) + pcc * dcc
            scb = (pc * (dc - deltac)).astype(BF)
            scc = pcc * (dcc - deltac)
            dqc.append((fdot(scb, k) + scc * kcf) * SCORE_SCALE)
            dk.append(fdot(s1, q))
            late_s.append(scb)
            late_p.append(pc.astype(BF))
            dkc.append(fdot(s2, q) + scc * qcf)
            dv.append(fdot(p1, do))
            dvc.append(fdot(p2, do) + pcc * docf)
        gpk[r, lane : lane + 128] = (jnp.transpose(jnp.concatenate(dq_t, 0)) * SCORE_SCALE).astype(BF)
        gpk[r, lane + 128 : lane + 256] = (join(*dk) + late(late_s, qc)).astype(BF)
        gpk[r, lane + 256 : lane + 384] = (join(*dv) + late(late_p, doc)).astype(BF)
        for s, value in enumerate((dqc, dkc, dvc)):
            lanes = slice(lane + 128 * s, lane + 128 * (s + 1))
            keep = gpk[512:, lanes].astype(F32)
            gpk[512:, lanes] = jnp.where(own1, join(*value), keep).astype(BF)

    b_last = []

    def b_deal():
        b_sent.wait()
        bland[me.x * 4 + me.z] = bupg[2 * me.x + me.z // 2]
        total = bland[0]
        for i in range(1, 16):
            total = total + bland[i]
        bsum[...] = total
        place = bfinal.at[me.slot]
        b_last.append(me.local(bsum, place))
        b_last.append(me.send_many([(bsum, place, me.at(dy=dy, flip=flip)) for dy, flip in me.near()], bfinal.at[pl.ds(0, 7)]))

    back_steps = {
        (0, 0): lambda: (sc.across(DOWN[0]), sc.across(DOWN[1]), sc.pair(OUT), sc.pass_on(B_UP[1])),
        (0, 1): lambda: (sc.start(0, gi[0].at[1 - me.c]), sc.across(B_UP[0])),
        (1, 0): lambda: (sc.pair(0), sc.deal(DOWN[0]), sc.deal(DOWN[1]), b_deal()),
        (1, 1): lambda: (sc.start(1, gi[1].at[1 - me.c]), sc.pass_on(OUT), sc.across(B_UP[1])),
        (2, 0): lambda: (sc.pair(1), sc.pass_on(0), sc.deal(B_UP[0])),
        (2, 1): lambda: (sc.start(2, gi[2].at[1 - me.c]),),
    }
    vtab[...] = jnp.zeros_like(vtab)
    for t in range(3):
        for h in range(2):
            p = 2 * t + h
            at = 384 * h + 128 * t
            lane = 384 * h
            gpk = gpks[t]
            gpk[512:, lane : lane + 384] = jnp.zeros((PAD, 384), BF)

            def one(i, carry, gpk=gpk, p=p, at=at, lane=lane):
                attend_back(gpk, p, at, lane, i)
                return carry

            lax.fori_loop(0, 2, one, 0, unroll=True)
            piece = gpk[:, lane : lane + 384]
            gi[t][h] = outer(attn[...], piece).astype(BF).reshape(4, 4, 48, 384)
            total = jnp.sum(piece.astype(F32), 0, keepdims=True)
            vtab[B_Q : B_Q + 1, at : at + 128] = total[:, :128]
            vtab[B_V : B_V + 1, at : at + 128] = total[:, 256:]
            back_steps[t, h]()

    def back_norm(t):
        for top_row, size in HALVES:
            r = pl.ds(top_row, size)
            back = dot_nt(gpks[t][r, :384], in_v[t][0, :, :, :, :384].reshape(D, 384))
            back = back + dot_nt(gpks[t][r, 384:], in_v[t][1, :, :, :, :384].reshape(D, 384))
            gnorm[r, :] = back if t == 0 else gnorm[r, :] + back


    gp = hi

    def last_norm(i, carry):
        r = rows_at(i, TILE)
        nm, inv = centre(hidden[r, :])
        gn = gnorm[r, :]
        sums[GAIN_A] += fold(gn * nm)
        sums[SHIFT_A] += fold(gn)
        gh = acc[r, :] + norm_back(gn * row(GAIN_A), nm, inv)
        masked = masks[r, :1] > 0.5
        sums[TOKEN] += fold(jnp.where(masked, gh, 0.0))
        gp[r, :] = jnp.where(masked, 0.0, gh).astype(BF)
        return carry

    back_norm(0)
    sc.pair(2)
    sc.pass_on(1)
    back_norm(1)
    sc.across(OUT)
    back_norm(2)
    sc.across(0)
    sc.deal(B_UP[1])
    lax.fori_loop(0, ROWS // TILE, last_norm, 0)
    for i in (TOKEN, GAIN_A, SHIFT_A, B_OUT, SCALE_A, GAIN_H, SHIFT_H, B_DOWN, SCALE_H):
        vtab[i : i + 1, :] = jnp.sum(sums[i], 0, keepdims=True)
    gvec[...] = jnp.transpose(vtab[...]).astype(BF).reshape(4, 4, 48, 128)
    sc.pair(VEC, waits=False)
    home(gp, o_gp, gcls_l)
    sc.across(1)
    sc.deal(OUT)
    sc.deal(0)
    sc.deal(2)
    sc.deal(VEC)
    sc.deal(1)
    for k in range(2):
        for half, total in enumerate(sc.finish(B_UP[k])):
            o_up[:, 1536 * half + 768 * k : 1536 * half + 768 * (k + 1)] = total
    for col, width, g in ((0, 256, DOWN[0]), (256, 128, DOWN[1])):
        for half, total in enumerate(sc.finish(g)):
            o_down[:, 384 * half + col : 384 * half + col + width] = total
    for half, total in enumerate(sc.finish(OUT)):
        o_out[:, 384 * half : 384 * (half + 1)] = total
    wait_all(b_last)
    flat = bfinal[0]
    for i in range(1, 8):
        flat = flat + bfinal[i]
    chosen = jnp.where(iota((384, 128), 0) == iota((384, 128), 1) + me.lane, 1.0, 0.0)
    line = lax.dot_general(
        jnp.broadcast_to(flat, (8, 384)), chosen, (((1,), (0,)), ((), ())), precision=lax.Precision.HIGHEST, preferred_element_type=F32
    )

    def finish_in(t):
        for half, total in enumerate(sc.finish(t)):
            for s in range(3):
                at = D * s + 384 * half + 128 * t
                o_in[:, at : at + 128] = total[:, 128 * s : 128 * (s + 1)]

    finish_in(0)
    wait_all(shuffle)
    order = iota((8, D), 0)
    for landed, out in ((cls_l, o_cls), (gcls_l, o_gcls)):
        rows = jnp.zeros((8, D), F32)
        for y in range(4):
            two = landed[y].astype(F32)
            for i in range(2):
                rows = jnp.where(order == 2 * y + i, two[i : i + 1], rows)
        out[...] = rows.astype(BF)
    finish_in(2)
    finish_in(1)
    low, high = sc.finish(VEC)
    vtab[:, :128] = jnp.zeros((128, 128), F32)
    vtab[:6, :128] = low + high
    turned = jnp.transpose(vtab[:, :128])
    o_vec[...] = jnp.where(iota((16, 128), 0) == 11, line[:1], turned[:16])


def layer(patches, cots, cls, cot_cls, mask_index, w_in, w_o, w_u, w_d, b_up, vectors):
    vm = pl.BlockSpec(memory_space=pltpu.VMEM)
    hb = pl.BlockSpec(memory_space=pl.ANY)
    S, V = jax.ShapeDtypeStruct, pltpu.VMEM
    outs = [S((6, 3 * D), F32), S((6, D), F32), S((6, FF), F32), S((24, D), F32), S((8, D), BF), S((8, D), BF), S((16, 128), F32)]
    far = [S((8, 64, D), BF)] * 2
    far += [S(((4,) if mode == "quarter" else ()) + (2, 4, 4, 8 * rho, width), BF) for rho, width, _, mode in GROUPS[3:]]
    pack_width = [sum(GROUPS[g][1] for g in pack) for pack in PACKS]
    pack_rho = [GROUPS[pack[0]][0] for pack in PACKS]
    scratch = [V((2, 4, 4, 48, width), BF) for _, width, _, _ in GROUPS[:3]]
    scratch += [V((4, 4, 48, D), BF), V((2, 4, 4, 48, CHUNK), BF), V((2, 4, 192, D), BF)]
    wide_rows, low_rows = V((ROWS, D), F32), V((ROWS, D), BF)
    scratch += [low_rows, low_rows, wide_rows, low_rows, V((6, ROWS, 384), BF), V((24, KEYS, 256), BF), V((24, PAD, 384), F32)]
    scratch += [low_rows, wide_rows, low_rows, low_rows, wide_rows, wide_rows, low_rows, low_rows, V((ROWS, 128), F32)]
    scratch += [V((16, D), F32), V((128, D), F32), V((4, 1, CHUNK), F32), V((8, 1, 384), F32), V((16, 1, 384), F32)]
    scratch += [V((1, 384), F32), V((8, 1, 384), F32), V((16, 8, D), F32), V((4, PAD, D), BF), V((4, PAD, D), BF)]
    quarter = [GROUPS[pack[0]][3] == "quarter" for pack in PACKS]
    scratch += [V((2, 4, r, w) if q else (2, r, w), BF) for r, w, q in zip(pack_rho, pack_width, quarter)]
    scratch += [V((8, r, w), BF) for r, w in zip(pack_rho, pack_width)]
    scratch += [V((8 * r, w), F32) for r, w in zip(pack_rho, pack_width)]
    scratch += [V((8 * rho, width), BF) for rho, width, _, _ in GROUPS]
    scratch += [V((2, 4, 4, 48, 384), BF)] * 4 + [V((4, 4, 48, 128), BF)]
    scratch += [V((4, 4, 48, CHUNK), BF), V((4, 192, 256), BF), V((4, 192, 128), BF)]
    blocks = [(8 * rho, width) for rho, width, _, _ in BACK]
    scratch += [V((4, 4) + blocks[g], BF) for g in (4, 5, 6, 7)]
    scratch += [V((4, 4) + blocks[g], BF) for g in range(8)]
    scratch += [V((2, 2) + blocks[g], BF) for g in RING]
    scratch += [V((16 if BACK[g][3] == "wide" else 3,) + blocks[g], BF) for g in range(9)]
    scratch += [V((8, rho, width), BF) for rho, width, _, _ in BACK] * 2
    scratch += [V((192, D), F32), pltpu.SemaphoreType.DMA((POOL,))]
    return pl.pallas_call(
        layer_kernel,
        out_shape=outs + far,
        in_specs=[hb] * 2 + [vm] * 19,
        out_specs=[vm] * len(outs) + [hb] * len(far),
        scratch_shapes=scratch,
        compiler_params=pltpu.CompilerParams(collective_id=0, has_side_effects=True, vmem_limit_bytes=63 * 2**20),
        name="layer",
    )(patches, cots, cls, cot_cls, mask_index, w_in, w_o, w_u, w_d, b_up, *vectors)[:9]


def finish_kernel(i_in, i_out, i_up, i_down, i_cls, i_gcls, i_vec, i_res, i_gp, *outs):
    for src, dst in zip((i_in, i_out, i_up, i_down, i_cls, i_gcls, i_res, i_gp), outs):
        dst[...] = src[...]
    for i in range(11):
        outs[8 + i][...] = i_vec[i : i + 1, :6]
    outs[19][...] = i_vec[11:12, :24]


def finish(parts):
    vm = pl.BlockSpec(memory_space=pltpu.VMEM)
    S = jax.ShapeDtypeStruct
    outs = [S(p.shape, p.dtype) for p in parts[:6]] + [S((8, 64, D), BF)] * 2 + [S((1, 6), F32)] * 11 + [S((1, 24), F32)]
    return pl.pallas_call(
        finish_kernel,
        out_shape=outs,
        in_specs=[vm] * 9,
        out_specs=[vm] * 20,
        name="finish",
    )(*parts)


def on_device(
    patches,
    cls_tokens,
    mask_index,
    mask_token,
    attention_gain,
    attention_shift,
    input_weight,
    query_bias,
    value_bias,
    output_weight,
    output_bias,
    attention_scale,
    hidden_gain,
    hidden_shift,
    expand_weight,
    expand_bias,
    reduce_weight,
    reduce_bias,
    hidden_scale,
    cotangent_patches,
    cotangent_cls,
):
    vectors = [mask_token, attention_gain, attention_shift, query_bias, value_bias, output_bias, attention_scale]
    vectors += [hidden_gain, hidden_shift, reduce_bias, hidden_scale]
    parts = layer(
        patches,
        cotangent_patches,
        cls_tokens,
        cotangent_cls,
        mask_index,
        input_weight,
        output_weight,
        expand_weight,
        reduce_weight,
        expand_bias.reshape(1, 24),
        [v.reshape(1, 6) for v in vectors],
    )
    g_in, g_o, g_u, g_d, o_cls, o_gcls, o_res, o_gp, *v = finish(parts)
    g_bup = v[11].reshape(24)
    v = [t.reshape(6) for t in v[:11]]
    return (
        o_res,
        o_cls,
        o_gp,
        o_gcls,
        v[TOKEN],
        v[GAIN_A],
        v[SHIFT_A],
        g_in,
        v[B_Q],
        v[B_V],
        g_o,
        v[B_OUT],
        v[SCALE_A],
        v[GAIN_H],
        v[SHIFT_H],
        g_u,
        g_bup,
        g_d,
        v[B_DOWN],
        v[SCALE_H],
    )


def solution(mesh):
    vector = P(("img", "row"))
    matrix = P(("img", "row"), None)
    image = P("img", "row", None)
    head = P("img", None)
    in_specs = (image, head, head, vector, vector, vector, matrix, vector, vector, matrix, vector, vector, vector, vector)
    in_specs += (matrix, vector, matrix, vector, vector, image, head)
    out_specs = (image, head, image, head, vector, vector, vector, matrix, vector, vector, matrix, vector, vector)
    out_specs += (vector, vector, matrix, vector, matrix, vector, vector)
    return jax.shard_map(on_device, mesh=mesh, in_specs=in_specs, out_specs=out_specs, check_vma=False)
```
